32 devices in a mesh: groups: 2 (over x), rows: 16 (over z, y, core).
Axes of the slice: x: 2, y: 2, z: 4, core: 2. Of those that a mesh axis runs over, the one named last changes fastest.
Arguments:
- ensemble: float32 [131072, 256], P(('groups', 'rows')), parts along dimension 0, may hold values from -60 to 60
- mean_state: float32 [131072], P(('groups', 'rows')), parts along dimension 0, may hold values from -6 to 6
- observed: float32 [4, 128], P('groups'), parts along dimension 0, may hold values from -8 to 8
- error_var: float32 [4, 128], P('groups'), parts along dimension 0, may hold values from 0.5 to 4
- owner: int32 [4], P('groups'), parts along dimension 0, may hold values from 0 to 15
- obs_rows: int32 [4, 128], P('groups'), parts along dimension 0, may hold values from 0 to 4095
Outputs:
- analysis_ensemble: float32 [131072, 256], P(('groups', 'rows')), parts along dimension 0
- analysis_mean: float32 [131072], P(('groups', 'rows')), parts along dimension 0
The draws below stay inside these ranges and needn't reach their ends.
There are 2 independent parts, one for each index of `groups`. The reference program is written for one: setup_inputs(seed, part) draws one part's arguments, and reference() takes and returns one part's arrays. A program takes and returns all parts, laid end to end along the dimension named above; each array names one. Nothing has to cross between parts.
Inputs may be any that keep to these rules, and one draw needn't show every extreme that they name: `obs_rows`: rows may repeat.
All inputs are finite; a program needn't handle non-finite values.
Results may differ from the reference program's by a relative error of at most 0.0003.
Values sent between devices are 32-bit elements; how exact they have to be, the bound alone decides.
No kernel may reach another device: no remote copies, remote signals or barrier semaphores. Data moves between devices by JAX's collectives and lax.ppermute only.
A program may use at most 64 MiB of HBM per device.

```python
import math
import jax
import jax.numpy as jnp
from jax import lax

M = 256
P_SIZE = 128
BATCHES = 2
ROWS_DEV = 4096
NROWS = 65536
N_ROWS = 16


def draw_ensemble(key, part):
    key = jax.random.fold_in(key, 11)
    key_values, key_columns, key_rough = jax.random.split(key, 3)
    position = jnp.arange(NROWS, dtype=jnp.float32) / (NROWS - 1.0)
    device_of_row = jnp.arange(NROWS, dtype=jnp.int32) // ROWS_DEV
    column_scales = jnp.exp(jax.random.uniform(key_columns, (N_ROWS, M), jnp.float32, -1.1, 1.1))
    rough = jnp.exp(jax.random.uniform(key_rough, (NROWS,), jnp.float32, -0.8, 0.8))
    values = jax.random.truncated_normal(key_values, -4.0, 4.0, (NROWS, M), jnp.float32)
    row_scales = 0.6 * jnp.power(3.0, position) * rough
    return values * row_scales[:, None] * column_scales[device_of_row]


def set_ends(result, stream_key, least, largest):
    index_at = [jax.random.randint(jax.random.fold_in(stream_key, axis), (), 0, length) for axis, length in enumerate(result.shape)]
    main_axis = result.shape.index(max(result.shape))
    neighbour = index_at[:main_axis] + [(index_at[main_axis] + 1) % result.shape[main_axis]] + index_at[main_axis + 1:]
    return result.at[tuple(index_at)].set(least).at[tuple(neighbour)].set(largest)


def level_of(rng, dims, shards, smallest, top_value):
    def one(dim, parts):
        steps = jax.random.uniform(jax.random.fold_in(jax.random.fold_in(rng, 6), dim), (parts,), jnp.float32, smallest / len(shards), top_value / len(shards))
        return jnp.repeat(jnp.exp(steps), dims[dim] // parts).reshape((-1,) + (1,) * (len(dims) - dim - 1))

    gain = one(*shards[0])
    for cut in shards[1:]:
        gain = gain * one(*cut)
    return gain


def normal_values(own_key, extent, scale, bound, cuts=(), kind=jnp.bfloat16):
    entries = scale * jax.random.normal(own_key, extent, jnp.float32)
    if cuts:
        entries = entries * level_of(own_key, extent, cuts, -0.22, 0.18)
    return jnp.clip(entries, -bound, bound).astype(kind)


def setup_inputs(seed: int = 0, part: int = 0) -> dict:
    arg_keys = jax.random.split(jax.random.key(seed), 7)
    part_keys = jax.random.split(jax.random.fold_in(arg_keys[6], part), 7)
    ensemble = draw_ensemble(jax.random.fold_in(jax.random.fold_in(arg_keys[6], part), 71), part)
    mean_state = normal_values(part_keys[1], (NROWS,), 1.0, 6.0, ((0, 16),), jnp.float32)
    observed = normal_values(part_keys[2], (BATCHES, P_SIZE), 1.5, 8.0, (), jnp.float32)
    error_var = jnp.clip(jnp.exp(jax.random.uniform(part_keys[3], (BATCHES, P_SIZE), jnp.float32, math.log(0.5), math.log(4.0))), 0.5, 4.0)
    owner = jax.random.randint(part_keys[4], (BATCHES,), 0, N_ROWS).astype(jnp.int32)
    obs_rows = set_ends(jax.random.randint(part_keys[5], (BATCHES, P_SIZE), 0, ROWS_DEV), jax.random.fold_in(part_keys[5], 1), 0, ROWS_DEV - 1).astype(jnp.int32)
    return dict(ensemble=ensemble, mean_state=mean_state, observed=observed, error_var=error_var, owner=owner, obs_rows=obs_rows)


RELAX = 0.6

def factors(prior_rows, prior_mean, observed_now, variance_now):
    members = prior_rows.shape[1]
    weight = 1.0 / (members - 1.0)
    inverse = 1.0 / variance_now
    innovation = observed_now - prior_mean
    scaled = prior_rows * jnp.sqrt(inverse * weight)[:, None]
    identity = jnp.eye(members, dtype=prior_rows.dtype)
    system = identity + jnp.dot(scaled.T, scaled, precision=lax.Precision.HIGHEST)
    lower = jnp.linalg.cholesky(system)
    target = jnp.dot(prior_rows.T, inverse * innovation, precision=lax.Precision.HIGHEST) * weight
    increment = jax.scipy.linalg.cho_solve((lower, True), target)
    inverse_lower = jax.scipy.linalg.solve_triangular(lower, identity, lower=True)
    return (inverse_lower.T, increment)

def reference(ensemble, mean_state, observed, error_var, owner, obs_rows):
    for batch in range(BATCHES):
        global_rows = (owner[batch] * ROWS_DEV + obs_rows[batch]).astype(jnp.int32)
        prior_rows = jnp.take(ensemble, global_rows, axis=0)
        prior_mean = jnp.take(mean_state, global_rows, axis=0)
        transform, increment = factors(prior_rows, prior_mean, observed[batch], error_var[batch])
        mean_state = mean_state + jnp.dot(ensemble, increment, precision=lax.Precision.HIGHEST)
        updated = jnp.dot(ensemble, transform, precision=lax.Precision.HIGHEST)
        before = jnp.sum(ensemble * ensemble)
        after = jnp.sum(updated * updated)
        factor = 1.0 + RELAX * (jnp.sqrt(before / after) - 1.0)
        ensemble = factor * updated
    return (ensemble, mean_state)
```

```python
import jax
import jax.numpy as jnp
from jax import lax
from jax.sharding import PartitionSpec as P

RELAX = 0.6
HI = lax.Precision.HIGHEST
AXIS = "rows"


def dot(a, b, dims=((1,), (0,))):
    return lax.dot_general(a, b, (dims, ((), ())), precision=HI, preferred_element_type=jnp.float32)


def stages_of(count):
    bits = count.bit_length() - 1
    stages = []
    low = 0
    while low < bits:
        width = 1 if low < 2 else min(2, bits - low)
        stages.append((low, width))
        low += width
    return stages


def swap(value, count, mask):
    return lax.ppermute(value, AXIS, [(i, i ^ mask) for i in range(count)])


def all_reduce(value, count):
    me = lax.axis_index(AXIS)
    stages = stages_of(count)
    for low, width in stages:
        parts = 1 << width
        digit = (me >> low) & (parts - 1)
        chunks = value.reshape((parts, value.shape[0] // parts) + value.shape[1:])
        total = lax.dynamic_index_in_dim(chunks, digit, 0, keepdims=False)
        for m in range(1, parts):
            piece = lax.dynamic_index_in_dim(chunks, digit ^ m, 0, keepdims=False)
            total = total + swap(piece, count, m << low)
        value = total
    for low, width in reversed(stages):
        parts = 1 << width
        digit = (me >> low) & (parts - 1)
        pieces = [value] + [swap(value, count, m << low) for m in range(1, parts)]
        ordered = []
        for j in range(parts):
            item = pieces[0]
            for m in range(1, parts):
                item = jnp.where((digit ^ j) == m, pieces[m], item)
            ordered.append(item)
        value = jnp.concatenate(ordered, axis=0)
    return value


def on_device(count, ensemble, mean_state, observed, error_var, owner, obs_rows):
    members = ensemble.shape[1]
    batches, obs = obs_rows.shape
    me = lax.axis_index(AXIS)
    rows = [jnp.where(owner[k] == me, jnp.take(ensemble, obs_rows[k], axis=0), 0.0) for k in range(batches)]
    means = [jnp.where(owner[k] == me, jnp.take(mean_state, obs_rows[k], axis=0), 0.0) for k in range(batches)]
    gram = dot(ensemble, ensemble, ((0,), (0,)))
    extra = jnp.concatenate(means).reshape(-1, members)
    pad = -(batches * obs + members + extra.shape[0]) % (8 * count)
    packed = jnp.concatenate(rows + [gram, extra, jnp.zeros((pad, members), jnp.float32)], axis=0)
    packed = all_reduce(packed, count)
    first, second = packed[:obs], packed[obs : 2 * obs]
    gram = packed[2 * obs : 2 * obs + members]
    means = packed[2 * obs + members : 2 * obs + members + extra.shape[0]].reshape(batches, obs)

    weight = 1.0 / (members - 1.0)
    inverse = 1.0 / error_var
    identity = jnp.eye(members, dtype=jnp.float32)
    scaled = first * jnp.sqrt(inverse[0] * weight)[:, None]
    system = identity + dot(scaled, scaled, ((0,), (0,)))
    lower = jnp.linalg.cholesky(system)
    inv_lower = jax.scipy.linalg.solve_triangular(lower, identity, lower=True)
    target = dot(first, (inverse[0] * (observed[0] - means[0]))[:, None], ((0,), (0,))) * weight
    increment = dot(inv_lower, dot(inv_lower, target), ((0,), (0,)))
    before = jnp.trace(gram)
    after = jnp.sum(dot(inv_lower, gram) * inv_lower)
    factor1 = 1.0 + RELAX * (jnp.sqrt(before / after) - 1.0)

    scaled = second * (factor1 * jnp.sqrt(inverse[1] * weight))[:, None]
    system = system + dot(scaled, scaled, ((0,), (0,)))
    lower = jnp.linalg.cholesky(system)
    inv_lower = jax.scipy.linalg.solve_triangular(lower, identity, lower=True)
    innovation = observed[1] - means[1] - dot(second, increment)[:, 0]
    target = dot(second, (inverse[1] * innovation)[:, None], ((0,), (0,))) * (weight * factor1 * factor1)
    increment = increment + dot(inv_lower, dot(inv_lower, target), ((0,), (0,)))
    after2 = jnp.sum(dot(inv_lower, gram) * inv_lower)
    factor2 = 1.0 + RELAX * (jnp.sqrt(after / after2) - 1.0)
    transform = inv_lower * (factor1 * factor2)
    analysis = dot(ensemble, transform, ((1,), (1,)))
    return analysis, mean_state + dot(ensemble, increment)[:, 0]


def solution(mesh):
    count = mesh.shape[AXIS]
    in_specs = (
        P(("groups", "rows"), None),
        P(("groups", "rows")),
        P("groups", None),
        P("groups", None),
        P("groups"),
        P("groups", None),
    )
    out_specs = (P(("groups", "rows"), None), P(("groups", "rows")))

    def body(*args):
        return on_device(count, *args)

    return jax.shard_map(body, mesh=mesh, in_specs=in_specs, out_specs=out_specs, check_vma=False)
```

```python
import functools

import jax
import jax.numpy as jnp
from jax import lax
from jax.experimental import pallas as pl
from jax.experimental.pallas import tpu as pltpu
from jax.sharding import PartitionSpec as P

RELAX = 0.6
HI = lax.Precision.HIGHEST
AXIS = "rows"
F32 = jnp.float32
BF16 = jnp.bfloat16
LANES = 128
SUB = 8
OBS = 128
VMEM_LIMIT = 40 * 1024 * 1024

S1, S2, G0, G1, INNOV, PACKED = 0, 128, 256, 384, 448, 480


def dot(a, b, dims=((1,), (0,)), precision=HI):
    return lax.dot_general(a, b, (dims, ((), ())), precision=precision, preferred_element_type=F32)


def column(row):
    return jnp.broadcast_to(row, (LANES, LANES)).T


def split(x):
    high = x.astype(BF16)
    return high, (x - high.astype(F32)).astype(BF16)


def gather_kernel(
    chunks, owner_s, rows_s, rows_v, observed, error_var, mean_v, x_hbm, packed, x_buf, picked, sem
):
    me = lax.axis_index(AXIS)
    members = x_buf.shape[1]
    size = x_buf.shape[0] // chunks

    def copy(i):
        part = pl.ds(i * size, size)
        return pltpu.make_async_copy(x_hbm.at[part], x_buf.at[part], sem.at[i])

    for i in range(chunks):
        copy(i).start()

    innovations = []
    scales = []
    lane = lax.broadcasted_iota(jnp.int32, (OBS, LANES), 1)
    for k in range(2):
        index = column(rows_v[k : k + 1, :].astype(F32)).astype(jnp.int32)
        prior = jnp.zeros((OBS, LANES), F32)
        for r in range(mean_v.shape[0]):
            prior = prior + jnp.where(index == lane + r * LANES, mean_v[r : r + 1, :], 0.0)
        prior = jnp.sum(prior.T, axis=0, keepdims=True)
        scale = lax.rsqrt(error_var[k : k + 1, :] * (members - 1.0))
        scale = jnp.where(owner_s[k] == me, scale, 0.0)
        innovations.append(scale * (observed[k : k + 1, :] - prior))
        scales.append(column(scale))

    def gram(i, carry):
        copy(i).wait()
        x = x_buf[pl.ds(pl.multiple_of(i * size, size), size), :]
        high = x.astype(BF16)
        rest = x - high.astype(F32)
        mid = rest.astype(BF16)
        low = (rest - mid.astype(F32)).astype(BF16)
        both = dot(high, high, ((0,), (0,)), None) + dot(mid, mid, ((0,), (0,)), None)
        cross = dot(high, mid, ((0,), (0,)), None) + dot(high, low, ((0,), (0,)), None)
        return carry[0] + both, carry[1] + cross

    zero = jnp.zeros((members, members), F32)
    both, cross = lax.fori_loop(0, chunks, gram, (zero, zero))
    total = both + cross + cross.T
    half = members // 2
    packed[G0 : G0 + half, :] = total[:half, :]
    packed[G1 : G1 + half // 2, :half] = total[half : half + half // 2, half:]
    packed[G1 : G1 + half // 2, half:] = total[half + half // 2 :, half:]

    for k, at in ((0, S1), (1, S2)):

        def take(o, _, k=k):
            picked[pl.ds(o, 1), :] = x_buf[pl.ds(rows_s[k, o], 1), :]
            return 0

        lax.fori_loop(0, OBS, take, 0, unroll=8)
        packed[at : at + OBS, :half] = picked[:, :half] * scales[k]
        packed[at : at + OBS, half:] = picked[:, half:] * scales[k]

    packed[INNOV:PACKED, :] = jnp.zeros((PACKED - INNOV, members), F32)
    packed[INNOV : INNOV + 1, :half] = innovations[0]
    packed[INNOV : INNOV + 1, half:] = innovations[1]


def factor(a):
    count = LANES // SUB
    lane = lax.broadcasted_iota(jnp.int32, (SUB, LANES), 1)
    sub = lax.broadcasted_iota(jnp.int32, (SUB, LANES), 0)
    rows = [a[SUB * i : SUB * (i + 1), :] for i in range(count)]
    out = []

    def spread(x, c):
        return jnp.broadcast_to(x[:, c : c + 1], (SUB, LANES))

    def row(x, j):
        return jnp.broadcast_to(x[j : j + 1, :], (SUB, LANES))

    for s in range(count):
        base = SUB * s
        here = (lane >= base) & (lane < base + SUB)
        cols = [spread(rows[s], base + j) for j in range(SUB)]
        work = jnp.where(here, (lane - base == sub).astype(F32), rows[s])
        done = jnp.zeros((SUB, LANES), F32)
        for j in range(0, SUB, 2):
            left, right = cols[j], cols[j + 1]
            pa, pb, pc = row(left, j), row(right, j), row(right, j + 1)
            det = pa * pc - pb * pb
            inv_det = pl.reciprocal(det, approx=True)
            top, low = row(work, j), row(work, j + 1)
            num0 = pc * top - pb * low
            num1 = pa * low - pb * top
            done = jnp.where(sub == j, top * lax.rsqrt(pa), done)
            done = jnp.where(sub == j + 1, num1 * lax.rsqrt(pa * det), done)
            pair = (sub == j) | (sub == j + 1)
            base_of = lambda v: jnp.where(pair, 0.0, v)
            mult0 = jnp.where(sub == j, -1.0, jnp.where(sub == j + 1, 0.0, left))
            mult1 = jnp.where(sub == j + 1, -1.0, jnp.where(sub == j, 0.0, right))
            work = base_of(work) - (mult0 * num0 + mult1 * num1) * inv_det
            for q in range(j + 2, SUB):
                t, l = row(cols[q], j), row(cols[q], j + 1)
                step = mult0 * (pc * t - pb * l) + mult1 * (pa * l - pb * t)
                cols[q] = base_of(cols[q]) - step * inv_det
        out.append(jnp.where(lane <= base + sub, done, 0.0))
        for i in range(s + 1, count):
            total = None
            for j in range(SUB):
                term = spread(rows[i], base + j) * row(work, j)
                total = term if total is None else total + term
            rows[i] = jnp.where(here, 0.0, rows[i]) - total
    return jnp.concatenate(out, axis=0)


def blend(before, after):
    return 1.0 + RELAX * (jnp.sqrt(before / after) - 1.0)


def update_kernel(chunks, half_v, other_v, mean_v, x_hbm, out_hbm, mean_out, full, x_buf, o_buf, in_sem, out_sem):
    members = x_buf.shape[1]
    size = x_buf.shape[0] // chunks

    def load(i):
        part = pl.ds(i * size, size)
        return pltpu.make_async_copy(x_hbm.at[part], x_buf.at[part], in_sem.at[i])

    def store(i):
        part = pl.ds(i * size, size)
        return pltpu.make_async_copy(o_buf.at[part], out_hbm.at[part], out_sem.at[i])

    for i in range(chunks):
        load(i).start()

    mine = lax.axis_index(AXIS) & 1
    span = half_v.shape[0]
    full[pl.ds(pl.multiple_of(mine * span, SUB), span), :] = half_v[...]
    full[pl.ds(pl.multiple_of((1 - mine) * span, SUB), span), :] = other_v[...]

    half = members // 2
    quarter = half // 2
    first = full[S1 : S1 + OBS, :]
    second = full[S2 : S2 + OBS, :]
    g01 = full[G0 : G0 + half, half:]
    g11 = jnp.concatenate([full[G1 : G1 + quarter, :half], full[G1 : G1 + quarter, half:]], axis=0)
    gram = jnp.concatenate(
        [full[G0 : G0 + half, :], jnp.concatenate([g01.T, g11], axis=1)], axis=0
    )
    innov1 = column(full[INNOV : INNOV + 1, :half])
    innov2 = column(full[INNOV : INNOV + 1, half:])
    eye = (
        lax.broadcasted_iota(jnp.int32, (half, half), 0) == lax.broadcasted_iota(jnp.int32, (half, half), 1)
    ).astype(F32)

    inv_m = factor(eye + dot(first, first, ((1,), (1,))))
    v_and_f = dot(inv_m, jnp.concatenate([first, innov1], axis=1))
    v, f = v_and_f[:, :members], v_and_f[:, members:]
    before = jnp.sum(eye * full[G0 : G0 + half, :half]) + jnp.sum(eye * g11)
    after1 = before - jnp.sum(dot(v, gram) * v)
    factor1 = blend(before, after1)
    v_scaled = v * jnp.concatenate([f, f], axis=1)
    increment = jnp.sum(v_scaled, axis=0, keepdims=True)
    innov2 = innov2 - jnp.sum(second * increment, axis=1, keepdims=True)

    a1 = dot(first, first, ((0,), (0,)))
    a2 = dot(second, jnp.concatenate([second, innov2], axis=1), ((0,), (0,))) * (factor1 * factor1)
    k00 = eye + a1[:half, :half] + a2[:half, :half]
    k01 = a1[:half, half:] + a2[:half, half:members]
    k11 = eye + a1[half:, half:] + a2[half:, half:members]
    inv00 = factor(k00)
    u = dot(inv00, k01)
    inv11 = factor(k11 - dot(u, u, ((0,), (0,))))
    inv10 = -dot(inv11, dot(u, inv00, ((0,), (0,))))
    y0 = dot(inv00, a2[:half, members:])
    y1 = dot(inv11, a2[half:, members:] - dot(u, y0, ((0,), (0,))))
    increment0 = jnp.sum(y0 * inv00 + y1 * inv10, axis=0, keepdims=True)
    increment1 = jnp.sum(y1 * inv11, axis=0, keepdims=True)
    increment = increment + jnp.concatenate([increment0, increment1], axis=1)
    inverse = jnp.concatenate(
        [jnp.concatenate([inv00, jnp.zeros_like(inv00)], axis=1), jnp.concatenate([inv10, inv11], axis=1)], axis=0
    )
    after2 = jnp.sum(dot(inverse, gram) * inverse)
    transform = inverse * (factor1 * blend(after1, after2))

    t_high, t_low = split(transform)
    t_all = jnp.concatenate([t_high, t_high, t_low], axis=1)
    w_high, w_low = split(increment)
    row16 = lax.broadcasted_iota(jnp.int32, (16, members), 0)
    w = jnp.where(row16 == 0, w_high.astype(F32), jnp.where(row16 == 1, w_low.astype(F32), 0.0)).astype(BF16)

    def apply(i, _):
        load(i).wait()
        part = pl.ds(pl.multiple_of(i * size, size), size)
        high, low = split(x_buf[part, :])
        o_buf[part, :] = dot(jnp.concatenate([high, low, high], axis=1), t_all, ((1,), (1,)), None)
        store(i).start()
        step = dot(w, high, ((1,), (1,)), None) + dot(w, low, ((1,), (1,)), None)
        where = pl.ds(pl.multiple_of(i * size, size), size)
        mean_out[:, where] = mean_v[:, where] + step[0:1, :] + step[1:2, :]
        return 0

    lax.fori_loop(0, chunks, apply, 0)
    for i in range(chunks):
        store(i).wait()


def spec(space):
    return pl.BlockSpec(memory_space=space)


def gather(ensemble, mean_state, observed, error_var, owner, obs_rows):
    rows, members = ensemble.shape
    chunks = 8
    return pl.pallas_call(
        functools.partial(gather_kernel, chunks),
        out_shape=jax.ShapeDtypeStruct((PACKED, members), F32),
        in_specs=[spec(pltpu.SMEM), spec(pltpu.SMEM)] + [spec(pltpu.VMEM)] * 4 + [spec(pl.ANY)],
        out_specs=spec(pltpu.VMEM),
        scratch_shapes=[
            pltpu.VMEM((rows, members), F32),
            pltpu.VMEM((OBS, members), F32),
            pltpu.SemaphoreType.DMA((chunks,)),
        ],
        compiler_params=pltpu.CompilerParams(vmem_limit_bytes=VMEM_LIMIT),
    )(owner, obs_rows, obs_rows, observed, error_var, mean_state.reshape(-1, LANES), ensemble)


def update(half, other, ensemble, mean_state):
    rows, members = ensemble.shape
    chunks = 8
    out, mean = pl.pallas_call(
        functools.partial(update_kernel, chunks),
        out_shape=(jax.ShapeDtypeStruct((rows, members), F32), jax.ShapeDtypeStruct((1, rows), F32)),
        in_specs=[spec(pltpu.VMEM)] * 3 + [spec(pl.ANY)],
        out_specs=(spec(pl.ANY), spec(pltpu.VMEM)),
        scratch_shapes=[
            pltpu.VMEM((PACKED, members), F32),
            pltpu.VMEM((rows, members), F32),
            pltpu.VMEM((rows, members), F32),
            pltpu.SemaphoreType.DMA((chunks,)),
            pltpu.SemaphoreType.DMA((chunks,)),
        ],
        compiler_params=pltpu.CompilerParams(vmem_limit_bytes=VMEM_LIMIT),
    )(half, other, mean_state.reshape(1, rows), ensemble)
    return out, mean.reshape(rows)


def swap(value, count, mask):
    return lax.ppermute(value, AXIS, [(i, i ^ mask) for i in range(count)])


def total(value, count):
    me = lax.axis_index(AXIS)
    for bit in (0, 1):
        odd = ((me >> bit) & 1) == 1
        low, high = jnp.split(value, 2, axis=0)
        value = jnp.where(odd, high, low) + swap(jnp.where(odd, low, high), count, 1 << bit)
    mask = 4
    while mask < count:
        value = value + swap(value, count, mask)
        mask *= 2
    got = swap(value, count, 2)
    odd = ((me >> 1) & 1) == 1
    value = jnp.concatenate([jnp.where(odd, got, value), jnp.where(odd, value, got)], axis=0)
    return value, swap(value, count, 1)


def on_device(count, ensemble, mean_state, observed, error_var, owner, obs_rows):
    packed = gather(ensemble, mean_state, observed, error_var, owner, obs_rows)
    half, other = total(packed, count)
    return update(half, other, ensemble, mean_state)


def solution(mesh):
    count = mesh.shape[AXIS]
    in_specs = (
        P(("groups", "rows"), None),
        P(("groups", "rows")),
        P("groups", None),
        P("groups", None),
        P("groups"),
        P("groups", None),
    )
    out_specs = (P(("groups", "rows"), None), P(("groups", "rows")))

    def body(*args):
        return on_device(count, *args)

    return jax.shard_map(body, mesh=mesh, in_specs=in_specs, out_specs=out_specs, check_vma=False)
```

```python
import functools

import jax
import jax.numpy as jnp
from jax import lax
from jax.experimental import pallas as pl
from jax.experimental.pallas import tpu as pltpu
from jax.sharding import PartitionSpec as P

RELAX = 0.6
HI = lax.Precision.HIGHEST
AXIS = "rows"
F32 = jnp.float32
BF16 = jnp.bfloat16
LANES = 128
SUB = 8
OBS = 128
VMEM_LIMIT = 64 * 1024 * 1024
UPDATE_LIMIT = 51 * 1024 * 1024

S1, S2, G0, G1, INNOV, PACKED = 0, 128, 256, 384, 448, 480


def dot(a, b, dims=((1,), (0,)), precision=HI):
    return lax.dot_general(a, b, (dims, ((), ())), precision=precision, preferred_element_type=F32)


def column(row):
    return jnp.broadcast_to(row, (LANES, LANES)).T


def split(x):
    high = x.astype(BF16)
    return high, (x - high.astype(F32)).astype(BF16)


def gather_kernel(
    chunks, owner_h, rows_h, observed_h, error_h, mean_h, x_hbm, packed,
    owner_s, rows_s, rows_v, observed, error_var, mean_v, x_buf, picked, sem, small_sem,
):
    me = lax.axis_index(AXIS)
    members = x_buf.shape[1]
    size = x_buf.shape[0] // chunks
    pairs = (
        (rows_h, rows_v), (observed_h, observed), (error_h, error_var), (mean_h, mean_v), (owner_h, owner_s), (rows_h, rows_s)
    )
    small = [pltpu.make_async_copy(a, b, small_sem.at[i]) for i, (a, b) in enumerate(pairs)]
    for item in small:
        item.start()

    def copy(i):
        part = pl.ds(i * size, size)
        return pltpu.make_async_copy(x_hbm.at[part], x_buf.at[part], sem.at[i])

    for i in range(chunks):
        copy(i).start()

    for item in small:
        item.wait()

    innovations = []
    scales = []
    lane = lax.broadcasted_iota(jnp.int32, (OBS, LANES), 1)
    for k in range(2):
        index = column(rows_v[k : k + 1, :].astype(F32)).astype(jnp.int32)
        prior = jnp.zeros((OBS, LANES), F32)
        for r in range(mean_v.shape[0]):
            prior = prior + jnp.where(index == lane + r * LANES, mean_v[r : r + 1, :], 0.0)
        prior = jnp.sum(prior.T, axis=0, keepdims=True)
        scale = lax.rsqrt(error_var[k : k + 1, :] * (members - 1.0))
        scale = jnp.where(owner_s[k] == me, scale, 0.0)
        innovations.append(scale * (observed[k : k + 1, :] - prior))
        scales.append(column(scale))

    def gram(i, carry):
        copy(i).wait()
        x = x_buf[pl.ds(pl.multiple_of(i * size, size), size), :]
        high = x.astype(BF16)
        mid = (x - high.astype(F32)).astype(BF16)
        first = dot(high, jnp.concatenate([high, mid], axis=1), ((0,), (0,)), None)
        both = first[:, :members] + dot(mid, mid, ((0,), (0,)), None)
        return carry[0] + both, carry[1] + first[:, members:]

    zero = jnp.zeros((members, members), F32)
    both, cross = lax.fori_loop(0, chunks, gram, (zero, zero))
    total = both + cross + cross.T
    half = members // 2
    packed[G0 : G0 + half, :] = total[:half, :]
    packed[G1 : G1 + half // 2, :half] = total[half : half + half // 2, half:]
    packed[G1 : G1 + half // 2, half:] = total[half + half // 2 :, half:]

    for k, at in ((0, S1), (1, S2)):

        def take(o, _, k=k):
            picked[pl.ds(o, 1), :] = x_buf[pl.ds(rows_s[k, o], 1), :]
            return 0

        lax.fori_loop(0, OBS, take, 0, unroll=8)
        packed[at : at + OBS, :half] = picked[:, :half] * scales[k]
        packed[at : at + OBS, half:] = picked[:, half:] * scales[k]

    packed[INNOV:PACKED, :] = jnp.zeros((PACKED - INNOV, members), F32)
    packed[INNOV : INNOV + 1, :half] = innovations[0]
    packed[INNOV : INNOV + 1, half:] = innovations[1]


def factor(a):
    count = LANES // SUB
    lane = lax.broadcasted_iota(jnp.int32, (SUB, LANES), 1)
    sub = lax.broadcasted_iota(jnp.int32, (SUB, LANES), 0)
    rows = [a[SUB * i : SUB * (i + 1), :] for i in range(count)]
    out = []

    def spread(x, c):
        return jnp.broadcast_to(x[:, c : c + 1], (SUB, LANES))

    def row(x, j):
        return jnp.broadcast_to(x[j : j + 1, :], (SUB, LANES))

    for s in range(count):
        base = SUB * s
        here = (lane >= base) & (lane < base + SUB)
        cols = [spread(rows[s], base + j) for j in range(SUB)]
        work = jnp.where(here, (lane - base == sub).astype(F32), rows[s])
        done = jnp.zeros((SUB, LANES), F32)
        for j in range(0, SUB, 2):
            left, right = cols[j], cols[j + 1]
            pa, pb, pc = row(left, j), row(right, j), row(right, j + 1)
            det = pa * pc - pb * pb
            inv_det = pl.reciprocal(det, approx=True)
            top, low = row(work, j), row(work, j + 1)
            num0 = pc * top - pb * low
            num1 = pa * low - pb * top
            done = jnp.where(sub == j, top * lax.rsqrt(pa), done)
            done = jnp.where(sub == j + 1, num1 * lax.rsqrt(pa * det), done)
            pair = (sub == j) | (sub == j + 1)
            base_of = lambda v: jnp.where(pair, 0.0, v)
            mult0 = jnp.where(sub == j, -1.0, jnp.where(sub == j + 1, 0.0, left))
            mult1 = jnp.where(sub == j + 1, -1.0, jnp.where(sub == j, 0.0, right))
            work = base_of(work) - (mult0 * num0 + mult1 * num1) * inv_det
            for q in range(j + 2, SUB):
                t, l = row(cols[q], j), row(cols[q], j + 1)
                step = mult0 * (pc * t - pb * l) + mult1 * (pa * l - pb * t)
                cols[q] = base_of(cols[q]) - step * inv_det
        out.append(jnp.where(lane <= base + sub, done, 0.0))
        for i in range(s + 1, count):
            total = None
            for j in range(SUB):
                term = spread(rows[i], base + j) * row(work, j)
                total = term if total is None else total + term
            rows[i] = jnp.where(here, 0.0, rows[i]) - total
    return jnp.concatenate(out, axis=0)


def blend(before, after):
    return 1.0 + RELAX * (jnp.sqrt(before / after) - 1.0)


def update_kernel(chunks, half_v, other_v, mean_v, x_hbm, out_hbm, mean_out, full, x_buf, o_buf, in_sem, out_sem):
    members = x_buf.shape[1]
    size = x_buf.shape[0] // chunks

    def load(i):
        part = pl.ds(i * size, size)
        return pltpu.make_async_copy(x_hbm.at[part], x_buf.at[part], in_sem.at[i])

    def store(i):
        part = pl.ds(i * size, size)
        return pltpu.make_async_copy(o_buf.at[part], out_hbm.at[part], out_sem.at[i])

    for i in range(chunks):
        load(i).start()

    mine = lax.axis_index(AXIS) & 1
    span = half_v.shape[0]
    full[pl.ds(pl.multiple_of(mine * span, SUB), span), :] = half_v[...]
    full[pl.ds(pl.multiple_of((1 - mine) * span, SUB), span), :] = other_v[...]

    half = members // 2
    quarter = half // 2
    first = full[S1 : S1 + OBS, :]
    second = full[S2 : S2 + OBS, :]
    g01 = full[G0 : G0 + half, half:]
    g11 = jnp.concatenate([full[G1 : G1 + quarter, :half], full[G1 : G1 + quarter, half:]], axis=0)
    gram = jnp.concatenate(
        [full[G0 : G0 + half, :], jnp.concatenate([g01.T, g11], axis=1)], axis=0
    )
    innov1 = column(full[INNOV : INNOV + 1, :half])
    innov2 = column(full[INNOV : INNOV + 1, half:])
    eye = (
        lax.broadcasted_iota(jnp.int32, (half, half), 0) == lax.broadcasted_iota(jnp.int32, (half, half), 1)
    ).astype(F32)

    inv_m = factor(eye + dot(first, first, ((1,), (1,))))
    v_and_f = dot(inv_m, jnp.concatenate([first, innov1], axis=1))
    v, f = v_and_f[:, :members], v_and_f[:, members:]
    before = jnp.sum(eye * full[G0 : G0 + half, :half]) + jnp.sum(eye * g11)
    after1 = before - jnp.sum(dot(v, gram) * v)
    factor1 = blend(before, after1)
    v_scaled = v * jnp.concatenate([f, f], axis=1)
    increment = jnp.sum(v_scaled, axis=0, keepdims=True)
    innov2 = innov2 - jnp.sum(second * increment, axis=1, keepdims=True)

    a1 = dot(first, first, ((0,), (0,)))
    a2 = dot(second, jnp.concatenate([second, innov2], axis=1), ((0,), (0,))) * (factor1 * factor1)
    k00 = eye + a1[:half, :half] + a2[:half, :half]
    k01 = a1[:half, half:] + a2[:half, half:members]
    k11 = eye + a1[half:, half:] + a2[half:, half:members]
    inv00 = factor(k00)
    u = dot(inv00, k01)
    inv11 = factor(k11 - dot(u, u, ((0,), (0,))))
    inv10 = -dot(inv11, dot(u, inv00, ((0,), (0,))))
    y0 = dot(inv00, a2[:half, members:])
    y1 = dot(inv11, a2[half:, members:] - dot(u, y0, ((0,), (0,))))
    increment0 = jnp.sum(y0 * inv00 + y1 * inv10, axis=0, keepdims=True)
    increment1 = jnp.sum(y1 * inv11, axis=0, keepdims=True)
    increment = increment + jnp.concatenate([increment0, increment1], axis=1)
    inverse = jnp.concatenate(
        [jnp.concatenate([inv00, jnp.zeros_like(inv00)], axis=1), jnp.concatenate([inv10, inv11], axis=1)], axis=0
    )
    after2 = jnp.sum(dot(inverse, gram) * inverse)
    transform = inverse * (factor1 * blend(after1, after2))

    t_high, t_low = split(transform)
    t_all = jnp.concatenate([t_high, t_high, t_low], axis=1)
    w_high, w_low = split(increment)
    row16 = lax.broadcasted_iota(jnp.int32, (16, members), 0)
    w = jnp.where(row16 == 0, w_high.astype(F32), jnp.where(row16 == 1, w_low.astype(F32), 0.0)).astype(BF16)

    def apply(i, _):
        load(i).wait()
        part = pl.ds(pl.multiple_of(i * size, size), size)
        high, low = split(x_buf[part, :])
        o_buf[part, :] = dot(jnp.concatenate([high, low, high], axis=1), t_all, ((1,), (1,)), None)
        store(i).start()
        step = dot(w, high, ((1,), (1,)), None) + dot(w, low, ((1,), (1,)), None)
        where = pl.ds(pl.multiple_of(i * size, size), size)
        mean_out[:, where] = mean_v[:, where] + step[0:1, :] + step[1:2, :]
        return 0

    lax.fori_loop(0, chunks, apply, 0)
    for i in range(chunks):
        store(i).wait()


def spec(space):
    return pl.BlockSpec(memory_space=space)


def gather(ensemble, mean_state, observed, error_var, owner, obs_rows):
    rows, members = ensemble.shape
    chunks = 8
    return pl.pallas_call(
        functools.partial(gather_kernel, chunks),
        out_shape=jax.ShapeDtypeStruct((PACKED, members), F32),
        in_specs=[spec(pltpu.HBM)] * 6,
        out_specs=spec(pltpu.VMEM),
        scratch_shapes=[
            pltpu.SMEM(owner.shape, jnp.int32),
            pltpu.SMEM(obs_rows.shape, jnp.int32),
            pltpu.VMEM(obs_rows.shape, jnp.int32),
            pltpu.VMEM(observed.shape, F32),
            pltpu.VMEM(error_var.shape, F32),
            pltpu.VMEM((rows // LANES, LANES), F32),
            pltpu.VMEM((rows, members), F32),
            pltpu.VMEM((OBS, members), F32),
            pltpu.SemaphoreType.DMA((chunks,)),
            pltpu.SemaphoreType.DMA((6,)),
        ],
        compiler_params=pltpu.CompilerParams(vmem_limit_bytes=VMEM_LIMIT),
    )(owner, obs_rows, observed, error_var, mean_state.reshape(-1, LANES), ensemble)


def update(half, other, ensemble, mean_state):
    rows, members = ensemble.shape
    chunks = 8
    out, mean = pl.pallas_call(
        functools.partial(update_kernel, chunks),
        out_shape=(jax.ShapeDtypeStruct((rows, members), F32), jax.ShapeDtypeStruct((1, rows), F32)),
        in_specs=[spec(pltpu.VMEM)] * 3 + [spec(pltpu.HBM)],
        out_specs=(spec(pltpu.HBM), spec(pltpu.VMEM)),
        scratch_shapes=[
            pltpu.VMEM((PACKED, members), F32),
            pltpu.VMEM((rows, members), F32),
            pltpu.VMEM((rows, members), F32),
            pltpu.SemaphoreType.DMA((chunks,)),
            pltpu.SemaphoreType.DMA((chunks,)),
        ],
        compiler_params=pltpu.CompilerParams(vmem_limit_bytes=UPDATE_LIMIT),
    )(half, other, mean_state.reshape(1, rows), ensemble)
    return out, mean.reshape(rows)


def swap(value, count, mask):
    return lax.ppermute(value, AXIS, [(i, i ^ mask) for i in range(count)])


def total(value, count):
    me = lax.axis_index(AXIS)
    for bit in (0, 1):
        odd = ((me >> bit) & 1) == 1
        low, high = jnp.split(value, 2, axis=0)
        value = jnp.where(odd, high, low) + swap(jnp.where(odd, low, high), count, 1 << bit)
    mask = 4
    while mask < count:
        value = value + swap(value, count, mask)
        mask *= 2
    got = swap(value, count, 2)
    odd = ((me >> 1) & 1) == 1
    value = jnp.concatenate([jnp.where(odd, got, value), jnp.where(odd, value, got)], axis=0)
    return value, swap(value, count, 1)


def on_device(count, ensemble, mean_state, observed, error_var, owner, obs_rows):
    packed = gather(ensemble, mean_state, observed, error_var, owner, obs_rows)
    half, other = total(packed, count)
    return update(half, other, ensemble, mean_state)


def solution(mesh):
    count = mesh.shape[AXIS]
    in_specs = (
        P(("groups", "rows"), None),
        P(("groups", "rows")),
        P("groups", None),
        P("groups", None),
        P("groups"),
        P("groups", None),
    )
    out_specs = (P(("groups", "rows"), None), P(("groups", "rows")))

    def body(*args):
        return on_device(count, *args)

    return jax.shard_map(body, mesh=mesh, in_specs=in_specs, out_specs=out_specs, check_vma=False)
```

```python
import functools

import jax
import jax.numpy as jnp
from jax import lax
from jax.experimental import pallas as pl
from jax.experimental.pallas import tpu as pltpu
from jax.sharding import PartitionSpec as P

RELAX = 0.6
HI = lax.Precision.HIGHEST
AXIS = "rows"
F32 = jnp.float32
BF16 = jnp.bfloat16
LANES = 128
SUB = 8
OBS = 128
VMEM_LIMIT = 51 * 1024 * 1024
STEP = 16

G0, G1, GRAM_ROWS = 0, 128, 192
S1, S2, INNOV, OBS_ROWS = 0, 128, 256, 288


def dot(a, b, dims=((1,), (0,)), precision=HI):
    return lax.dot_general(a, b, (dims, ((), ())), precision=precision, preferred_element_type=F32)


def column(row):
    return jnp.broadcast_to(row, (LANES, LANES)).T


def split(x):
    high = x.astype(BF16)
    return high, (x - high.astype(F32)).astype(BF16)


def deal(full, keep, send):
    mine = lax.axis_index(AXIS) & 1
    span = keep.shape[0]
    keep[...] = full[pl.ds(pl.multiple_of(mine * span, SUB), span), :]
    send[...] = full[pl.ds(pl.multiple_of((1 - mine) * span, SUB), span), :]


def chunk_copy(source, target, sem, chunks):
    size = source.shape[0] // chunks

    def copy(i):
        part = pl.ds(i * size, size)
        return pltpu.make_async_copy(source.at[part], target.at[part], sem.at[i])

    return copy


def gram_kernel(chunks, x_hbm, keep, send, full, x_buf, sem):
    members = x_buf.shape[1]
    size = x_buf.shape[0] // chunks
    half = members // 2
    copy = chunk_copy(x_hbm, x_buf, sem, chunks)
    for i in range(chunks):
        copy(i).start()
    total = None
    for i in range(chunks):
        copy(i).wait()
        high, low = split(x_buf[i * size : (i + 1) * size, :])
        part = dot(high, jnp.concatenate([high, low], axis=1), ((0,), (0,)), None)
        total = part if total is None else total + part
    cross = total[:, members:]
    total = total[:, :members] + cross + cross.T
    full[G0 : G0 + half, :] = total[:half, :]
    full[G1 : G1 + half // 2, :half] = total[half : half + half // 2, half:]
    full[G1 : G1 + half // 2, half:] = total[half + half // 2 :, half:]
    deal(full, keep, send)


def gather_kernel(
    chunks, owner_s, rows_s, rows_v, observed, error_var, mean_v, x_hbm, keep, send, full, x_buf, picked, sem
):
    me = lax.axis_index(AXIS)
    members = x_buf.shape[1]
    half = members // 2
    copy = chunk_copy(x_hbm, x_buf, sem, chunks)
    for i in range(chunks):
        copy(i).start()

    full[INNOV:OBS_ROWS, :] = jnp.zeros((OBS_ROWS - INNOV, members), F32)
    scales = []
    lane = lax.broadcasted_iota(jnp.int32, (OBS, LANES), 1)
    for k in range(2):
        index = column(rows_v[k : k + 1, :].astype(F32)).astype(jnp.int32)
        prior = jnp.zeros((OBS, LANES), F32)
        for r in range(mean_v.shape[0]):
            prior = prior + jnp.where(index == lane + r * LANES, mean_v[r : r + 1, :], 0.0)
        prior = jnp.sum(prior.T, axis=0, keepdims=True)
        scale = lax.rsqrt(error_var[k : k + 1, :] * (members - 1.0))
        scale = jnp.where(owner_s[k] == me, scale, 0.0)
        full[INNOV : INNOV + 1, k * half : (k + 1) * half] = scale * (observed[k : k + 1, :] - prior)
        scales.append(column(scale))

    for i in range(chunks):
        copy(i).wait()
    for k, at in ((0, S1), (1, S2)):

        def take(o, _, k=k):
            picked[pl.ds(o, 1), :] = x_buf[pl.ds(rows_s[k, o], 1), :]
            return 0

        lax.fori_loop(0, OBS, take, 0, unroll=8)
        full[at : at + OBS, :half] = picked[:, :half] * scales[k]
        full[at : at + OBS, half:] = picked[:, half:] * scales[k]
    deal(full, keep, send)


def tree(terms):
    while len(terms) > 1:
        terms = [terms[i] + terms[i + 1] if i + 1 < len(terms) else terms[i] for i in range(0, len(terms), 2)]
    return terms[0]


def factor(a):
    count = LANES // SUB
    lane = lax.broadcasted_iota(jnp.int32, (SUB, LANES), 1)
    sub = lax.broadcasted_iota(jnp.int32, (SUB, LANES), 0)
    rows = [a[SUB * i : SUB * (i + 1), :] for i in range(count)]
    out = []

    def spread(x, c):
        return jnp.broadcast_to(x[:, c : c + 1], (SUB, LANES))

    def row(x, j):
        return jnp.broadcast_to(x[j : j + 1, :], (SUB, LANES))

    groups = STEP // SUB
    for s in range(0, count, groups):
        base = SUB * s
        here = (lane >= base) & (lane < base + STEP)
        cols = [[spread(rows[s + g], base + q) for g in range(groups)] for q in range(STEP)]
        work = [
            jnp.where(here, (lane - base == sub + SUB * g).astype(F32), rows[s + g]) for g in range(groups)
        ]
        done = [jnp.zeros((SUB, LANES), F32) for _ in range(groups)]
        for p in range(0, STEP, 2):
            at, j = divmod(p, SUB)
            first, second = sub == j, sub == j + 1
            pair = first | second
            pa, pb, pc = row(cols[p][at], j), row(cols[p][at], j + 1), row(cols[p + 1][at], j + 1)
            det = pa * pc - pb * pb
            inv = pl.reciprocal(det, approx=True)
            top, low = row(work[at], j), row(work[at], j + 1)
            done[at] = jnp.where(first, top * lax.rsqrt(pa), done[at])
            done[at] = jnp.where(second, (pa * low - pb * top) * lax.rsqrt(pa * det), done[at])
            raw, scaled = [], []
            for g in range(groups):
                m0, m1 = cols[p][g], cols[p + 1][g]
                if g == at:
                    m0 = jnp.where(first, -1.0, jnp.where(second, 0.0, m0))
                    m1 = jnp.where(second, -1.0, jnp.where(first, 0.0, m1))
                u0, u1 = m0 * pc - m1 * pb, m1 * pa - m0 * pb
                raw.append((u0, u1))
                scaled.append((u0 * inv, u1 * inv))
            for q in range(p + 2, STEP + 1):
                kept = cols[q] if q < STEP else work
                t, l = row(kept[at], j), row(kept[at], j + 1)
                moved = []
                for g in range(groups):
                    old = jnp.where(pair, 0.0, kept[g]) if g == at else kept[g]
                    if q < p + 4:
                        moved.append(old - (raw[g][0] * t + raw[g][1] * l) * inv)
                    else:
                        moved.append(old - (scaled[g][0] * t + scaled[g][1] * l))
                if q < STEP:
                    cols[q] = moved
                else:
                    work = moved
        for g in range(groups):
            out.append(jnp.where(lane <= base + SUB * g + sub, done[g], 0.0))
        lines = [row(work[p // SUB], p % SUB) for p in range(STEP)]
        for i in range(s + groups, count):
            change = tree([spread(rows[i], base + p) * lines[p] for p in range(STEP)])
            rows[i] = jnp.where(here, 0.0, rows[i]) - change
    return jnp.concatenate(out, axis=0)


def blend(before, after):
    return 1.0 + RELAX * (jnp.sqrt(before / after) - 1.0)


def join(mine, other, full):
    bit = lax.axis_index(AXIS) & 1
    span = mine.shape[0]
    full[pl.ds(pl.multiple_of(bit * span, SUB), span), :] = mine[...]
    full[pl.ds(pl.multiple_of((1 - bit) * span, SUB), span), :] = other[...]


def update_kernel(
    chunks, gram_mine, gram_other, obs_mine, obs_other, mean_v, x_hbm, out_hbm, mean_out,
    gram_full, full, x_buf, o_buf, in_sem, out_sem,
):
    members = x_buf.shape[1]
    size = x_buf.shape[0] // chunks
    load = chunk_copy(x_hbm, x_buf, in_sem, chunks)
    store = chunk_copy(o_buf, out_hbm, out_sem, chunks)
    for i in range(chunks):
        load(i).start()

    join(gram_mine, gram_other, gram_full)
    join(obs_mine, obs_other, full)

    half = members // 2
    quarter = half // 2
    first = full[S1 : S1 + OBS, :]
    second = full[S2 : S2 + OBS, :]
    g00 = gram_full[G0 : G0 + half, :half]
    g01 = gram_full[G0 : G0 + half, half:]
    g11 = jnp.concatenate([gram_full[G1 : G1 + quarter, :half], gram_full[G1 : G1 + quarter, half:]], axis=0)
    gram = jnp.concatenate(
        [jnp.concatenate([g00, g01], axis=1), jnp.concatenate([g01.T, g11], axis=1)], axis=0
    )
    innov1 = column(full[INNOV : INNOV + 1, :half])
    innov2 = column(full[INNOV : INNOV + 1, half:])
    eye = (
        lax.broadcasted_iota(jnp.int32, (half, half), 0) == lax.broadcasted_iota(jnp.int32, (half, half), 1)
    ).astype(F32)

    inv_m = factor(eye + dot(first, first, ((1,), (1,))))
    v_and_f = dot(inv_m, jnp.concatenate([first, innov1], axis=1))
    v, f = v_and_f[:, :members], v_and_f[:, members:]
    before = jnp.sum(eye * (g00 + g11))
    after1 = before - jnp.sum(dot(v, gram) * v)
    factor1 = blend(before, after1)
    v_scaled = v * jnp.concatenate([f, f], axis=1)
    increment = jnp.sum(v_scaled, axis=0, keepdims=True)
    innov2 = innov2 - jnp.sum(second * increment, axis=1, keepdims=True)

    a1 = dot(first, first, ((0,), (0,)))
    a2 = dot(second, jnp.concatenate([second, innov2], axis=1), ((0,), (0,))) * (factor1 * factor1)
    k00 = eye + a1[:half, :half] + a2[:half, :half]
    k01 = a1[:half, half:] + a2[:half, half:members]
    k11 = eye + a1[half:, half:] + a2[half:, half:members]
    inv00 = factor(k00)
    u = dot(inv00, k01)
    inv11 = factor(k11 - dot(u, u, ((0,), (0,))))
    inv10 = -dot(inv11, dot(u, inv00, ((0,), (0,))))
    y0 = dot(inv00, a2[:half, members:])
    y1 = dot(inv11, a2[half:, members:] - dot(u, y0, ((0,), (0,))))
    increment0 = jnp.sum(y0 * inv00 + y1 * inv10, axis=0, keepdims=True)
    increment1 = jnp.sum(y1 * inv11, axis=0, keepdims=True)
    increment = increment + jnp.concatenate([increment0, increment1], axis=1)
    inverse = jnp.concatenate(
        [jnp.concatenate([inv00, jnp.zeros_like(inv00)], axis=1), jnp.concatenate([inv10, inv11], axis=1)], axis=0
    )
    after2 = jnp.sum(dot(inverse, gram) * inverse)
    transform = inverse * (factor1 * blend(after1, after2))

    t_high, t_low = split(transform)
    t_all = jnp.concatenate([t_high, t_high, t_low], axis=1)
    w_high, w_low = split(increment)
    row16 = lax.broadcasted_iota(jnp.int32, (16, members), 0)
    w = jnp.where(row16 == 0, w_high.astype(F32), jnp.where(row16 == 1, w_low.astype(F32), 0.0)).astype(BF16)

    def apply(i, _):
        load(i).wait()
        part = pl.ds(pl.multiple_of(i * size, size), size)
        high, low = split(x_buf[part, :])
        o_buf[part, :] = dot(jnp.concatenate([high, low, high], axis=1), t_all, ((1,), (1,)), None)
        store(i).start()
        step = dot(w, high, ((1,), (1,)), None) + dot(w, low, ((1,), (1,)), None)
        where = pl.ds(pl.multiple_of(i * size, size), size)
        mean_out[:, where] = mean_v[:, where] + step[0:1, :] + step[1:2, :]
        return 0

    lax.fori_loop(0, chunks, apply, 0)
    for i in range(chunks):
        store(i).wait()


def spec(space):
    return pl.BlockSpec(memory_space=space)


def params():
    return pltpu.CompilerParams(vmem_limit_bytes=VMEM_LIMIT)


def gram_halves(ensemble):
    rows, members = ensemble.shape
    chunks = 4
    half = jax.ShapeDtypeStruct((GRAM_ROWS // 2, members), F32)
    return pl.pallas_call(
        functools.partial(gram_kernel, chunks),
        out_shape=(half, half),
        in_specs=[spec(pltpu.HBM)],
        out_specs=(spec(pltpu.VMEM), spec(pltpu.VMEM)),
        scratch_shapes=[
            pltpu.VMEM((GRAM_ROWS, members), F32),
            pltpu.VMEM((rows, members), F32),
            pltpu.SemaphoreType.DMA((chunks,)),
        ],
        cost_estimate=pl.CostEstimate(
            flops=4 * rows * members * members, bytes_accessed=4 * rows * members, transcendentals=0
        ),
        compiler_params=params(),
    )(ensemble)


def gather(ensemble, mean_state, observed, error_var, owner, obs_rows):
    rows, members = ensemble.shape
    chunks = 4
    half = jax.ShapeDtypeStruct((OBS_ROWS // 2, members), F32)
    return pl.pallas_call(
        functools.partial(gather_kernel, chunks),
        out_shape=(half, half),
        in_specs=[spec(pltpu.SMEM), spec(pltpu.SMEM)] + [spec(pltpu.VMEM)] * 4 + [spec(pltpu.HBM)],
        out_specs=(spec(pltpu.VMEM), spec(pltpu.VMEM)),
        scratch_shapes=[
            pltpu.VMEM((OBS_ROWS, members), F32),
            pltpu.VMEM((rows, members), F32),
            pltpu.VMEM((OBS, members), F32),
            pltpu.SemaphoreType.DMA((chunks,)),
        ],
        cost_estimate=pl.CostEstimate(
            flops=2 * rows * members * members, bytes_accessed=4 * rows * members, transcendentals=0
        ),
        compiler_params=params(),
    )(owner, obs_rows, obs_rows, observed, error_var, mean_state.reshape(-1, LANES), ensemble)


def update(gram, obs, ensemble, mean_state):
    rows, members = ensemble.shape
    chunks = 8
    out, mean = pl.pallas_call(
        functools.partial(update_kernel, chunks),
        out_shape=(jax.ShapeDtypeStruct((rows, members), F32), jax.ShapeDtypeStruct((1, rows), F32)),
        in_specs=[spec(pltpu.VMEM)] * 5 + [spec(pltpu.HBM)],
        out_specs=(spec(pltpu.HBM), spec(pltpu.VMEM)),
        scratch_shapes=[
            pltpu.VMEM((GRAM_ROWS, members), F32),
            pltpu.VMEM((OBS_ROWS, members), F32),
            pltpu.VMEM((rows, members), F32),
            pltpu.VMEM((rows, members), F32),
            pltpu.SemaphoreType.DMA((chunks,)),
            pltpu.SemaphoreType.DMA((chunks,)),
        ],
        compiler_params=params(),
    )(*gram, *obs, mean_state.reshape(1, rows), ensemble)
    return out, mean.reshape(rows)


def swap(value, count, mask):
    return lax.ppermute(value, AXIS, [(i, i ^ mask) for i in range(count)])


def total(halves, count):
    me = lax.axis_index(AXIS)
    keep, send = halves
    value = keep + swap(send, count, 1)
    odd = ((me >> 1) & 1) == 1
    low, high = jnp.split(value, 2, axis=0)
    value = jnp.where(odd, high, low) + swap(jnp.where(odd, low, high), count, 2)
    mask = 4
    while mask < count:
        value = value + swap(value, count, mask)
        mask *= 2
    got = swap(value, count, 2)
    value = jnp.concatenate([jnp.where(odd, got, value), jnp.where(odd, value, got)], axis=0)
    return value, swap(value, count, 1)


def on_device(count, ensemble, mean_state, observed, error_var, owner, obs_rows):
    gram = total(gram_halves(ensemble), count)
    obs = total(gather(ensemble, mean_state, observed, error_var, owner, obs_rows), count)
    return update(gram, obs, ensemble, mean_state)


def solution(mesh):
    count = mesh.shape[AXIS]
    in_specs = (
        P(("groups", "rows"), None),
        P(("groups", "rows")),
        P("groups", None),
        P("groups", None),
        P("groups"),
        P("groups", None),
    )
    out_specs = (P(("groups", "rows"), None), P(("groups", "rows")))

    def body(*args):
        return on_device(count, *args)

    return jax.shard_map(body, mesh=mesh, in_specs=in_specs, out_specs=out_specs, check_vma=False)
```

```python
import functools

import jax
import jax.numpy as jnp
from jax import lax
from jax.experimental import pallas as pl
from jax.experimental.pallas import tpu as pltpu
from jax.sharding import PartitionSpec as P

RELAX = 0.6
HI = lax.Precision.HIGHEST
AXIS = "rows"
F32 = jnp.float32
BF16 = jnp.bfloat16
LANES = 128
SUB = 8
OBS = 128
VMEM_LIMIT = 51 * 1024 * 1024
STEP = 16

FIRST_ROWS, FIRST_HALF = 64, 80
GRAM_ROWS, SECOND_ROWS, SECOND_HALF = 96, 64, 160


def dot(a, b, dims=((1,), (0,)), precision=HI):
    return lax.dot_general(a, b, (dims, ((), ())), precision=precision, preferred_element_type=F32)


def column(row):
    return jnp.broadcast_to(row, (LANES, LANES)).T


def split(x):
    high = x.astype(BF16)
    return high, (x - high.astype(F32)).astype(BF16)


def halves(full, span):
    mine = lax.axis_index(AXIS) & 1
    return [full[pl.ds(pl.multiple_of(bit * span, SUB), span), :] for bit in (mine, 1 - mine)]


def chunk_copy(source, target, sem, chunks):
    size = source.shape[0] // chunks

    def copy(i):
        part = pl.ds(i * size, size)
        return pltpu.make_async_copy(source.at[part], target.at[part], sem.at[i])

    return copy


def gram_kernel(chunks, x_hbm, keep, send, full, x_buf, sem):
    members = x_buf.shape[1]
    size = x_buf.shape[0] // chunks
    half = members // 2
    copy = chunk_copy(x_hbm, x_buf, sem, chunks)
    for i in range(chunks):
        copy(i).start()
    total = None
    for i in range(chunks):
        copy(i).wait()
        high, low = split(x_buf[i * size : (i + 1) * size, :])
        part = dot(high, jnp.concatenate([high, low], axis=1), ((0,), (0,)), None)
        total = part if total is None else total + part
    cross = total[:, members:]
    total = total[:, :members] + cross + cross.T
    full[:half, :] = total[:half, :]
    full[half:, :half] = total[half : half + half // 2, half:]
    full[half:, half:] = total[half + half // 2 :, half:]
    keep[...], send[...] = halves(full, GRAM_ROWS)


def gather_kernel(
    chunks, owner_s, rows_s, rows_v, observed, error_var, mean_v, gram_keep, gram_send, x_hbm,
    first_keep, first_send, second_keep, second_send, picked, x_buf, sem,
):
    me = lax.axis_index(AXIS)
    members = x_buf.shape[1]
    half = members // 2
    copy = chunk_copy(x_hbm, x_buf, sem, chunks)
    for i in range(chunks):
        copy(i).start()

    second_keep[:GRAM_ROWS, :] = gram_keep[...]
    second_send[:GRAM_ROWS, :] = gram_send[...]
    innovations = []
    scales = []
    lane = lax.broadcasted_iota(jnp.int32, (OBS, LANES), 1)
    for k in range(2):
        index = column(rows_v[k : k + 1, :].astype(F32)).astype(jnp.int32)
        prior = jnp.zeros((OBS, LANES), F32)
        for r in range(mean_v.shape[0]):
            prior = prior + jnp.where(index == lane + r * LANES, mean_v[r : r + 1, :], 0.0)
        prior = jnp.sum(prior.T, axis=0, keepdims=True)
        scale = lax.rsqrt(error_var[k : k + 1, :] * (members - 1.0))
        scale = jnp.where(owner_s[k] == me, scale, 0.0)
        innovations.append(scale * (observed[k : k + 1, :] - prior))
        scales.append(column(scale))
    line = lax.broadcasted_iota(jnp.int32, (FIRST_HALF - FIRST_ROWS, members), 0)
    tail = jnp.where(line == 0, jnp.concatenate(innovations, axis=1), 0.0)
    first_keep[FIRST_ROWS:, :] = tail
    first_send[FIRST_ROWS:, :] = tail

    for i in range(chunks):
        copy(i).wait()
    for k, keep, send, at in ((0, first_keep, first_send, 0), (1, second_keep, second_send, GRAM_ROWS)):

        def take(o, _, k=k):
            picked[pl.ds(o, 1), :] = x_buf[pl.ds(rows_s[k, o], 1), :]
            return 0

        lax.fori_loop(0, OBS, take, 0, unroll=16)
        picked[:, :half] = picked[:, :half] * scales[k]
        picked[:, half:] = picked[:, half:] * scales[k]
        keep[at : at + OBS // 2, :], send[at : at + OBS // 2, :] = halves(picked, OBS // 2)


def tree(terms):
    while len(terms) > 1:
        terms = [terms[i] + terms[i + 1] if i + 1 < len(terms) else terms[i] for i in range(0, len(terms), 2)]
    return terms[0]


def factor(a):
    count = LANES // SUB
    lane = lax.broadcasted_iota(jnp.int32, (SUB, LANES), 1)
    sub = lax.broadcasted_iota(jnp.int32, (SUB, LANES), 0)
    rows = [a[SUB * i : SUB * (i + 1), :] for i in range(count)]
    out = []

    def spread(x, c):
        return jnp.broadcast_to(x[:, c : c + 1], (SUB, LANES))

    def row(x, j):
        return jnp.broadcast_to(x[j : j + 1, :], (SUB, LANES))

    groups = STEP // SUB
    for s in range(0, count, groups):
        base = SUB * s
        here = (lane >= base) & (lane < base + STEP)
        cols = [[spread(rows[s + g], base + q) for g in range(groups)] for q in range(STEP)]
        work = [
            jnp.where(here, (lane - base == sub + SUB * g).astype(F32), rows[s + g]) for g in range(groups)
        ]
        done = [jnp.zeros((SUB, LANES), F32) for _ in range(groups)]
        for p in range(0, STEP, 2):
            at, j = divmod(p, SUB)
            first, second = sub == j, sub == j + 1
            pair = first | second
            pa, pb, pc = row(cols[p][at], j), row(cols[p][at], j + 1), row(cols[p + 1][at], j + 1)
            det = pa * pc - pb * pb
            inv = pl.reciprocal(det, approx=True)
            top, low = row(work[at], j), row(work[at], j + 1)
            done[at] = jnp.where(first, top * lax.rsqrt(pa), done[at])
            done[at] = jnp.where(second, (pa * low - pb * top) * lax.rsqrt(pa * det), done[at])
            raw, scaled = [], []
            for g in range(groups):
                m0, m1 = cols[p][g], cols[p + 1][g]
                if g == at:
                    m0 = jnp.where(first, -1.0, jnp.where(second, 0.0, m0))
                    m1 = jnp.where(second, -1.0, jnp.where(first, 0.0, m1))
                u0, u1 = m0 * pc - m1 * pb, m1 * pa - m0 * pb
                raw.append((u0, u1))
                scaled.append((u0 * inv, u1 * inv))
            for q in range(p + 2, STEP + 1):
                kept = cols[q] if q < STEP else work
                t, l = row(kept[at], j), row(kept[at], j + 1)
                moved = []
                for g in range(groups):
                    old = jnp.where(pair, 0.0, kept[g]) if g == at else kept[g]
                    if q < p + 4:
                        moved.append(old - (raw[g][0] * t + raw[g][1] * l) * inv)
                    else:
                        moved.append(old - (scaled[g][0] * t + scaled[g][1] * l))
                if q < STEP:
                    cols[q] = moved
                else:
                    work = moved
        for g in range(groups):
            out.append(jnp.where(lane <= base + SUB * g + sub, done[g], 0.0))
        lines = [row(work[p // SUB], p % SUB) for p in range(STEP)]
        for i in range(s + groups, count):
            change = tree([spread(rows[i], base + p) * lines[p] for p in range(STEP)])
            rows[i] = jnp.where(here, 0.0, rows[i]) - change
    return jnp.concatenate(out, axis=0)


def blend(before, after):
    return 1.0 + RELAX * (jnp.sqrt(before / after) - 1.0)


def join(mine, other, full, at, span):
    bit = lax.axis_index(AXIS) & 1
    full[pl.ds(pl.multiple_of(bit * span, SUB), span), :] = mine[at : at + span, :]
    full[pl.ds(pl.multiple_of((1 - bit) * span, SUB), span), :] = other[at : at + span, :]


def identity(size):
    return (
        lax.broadcasted_iota(jnp.int32, (size, size), 0) == lax.broadcasted_iota(jnp.int32, (size, size), 1)
    ).astype(F32)


def first_kernel(mine, other, v_out, system_out, extra_out, full):
    join(mine, other, full, 0, FIRST_ROWS)
    rows = full[...]
    members = rows.shape[1]
    half = members // 2
    innovations = mine[FIRST_ROWS : FIRST_ROWS + 1, :]
    inv_m = factor(identity(OBS) + dot(rows, rows, ((1,), (1,))))
    v_and_f = dot(inv_m, jnp.concatenate([rows, column(innovations[:, :half])], axis=1))
    v, f = v_and_f[:, :members], v_and_f[:, members:]
    v_out[...] = v
    system_out[...] = identity(members) + dot(rows, rows, ((0,), (0,)))
    increment = jnp.sum(v * jnp.concatenate([f, f], axis=1), axis=0, keepdims=True)
    line = lax.broadcasted_iota(jnp.int32, (SUB, members), 0)
    extra_out[...] = jnp.where(line == 0, increment, jnp.where(line == 1, innovations, 0.0))


def update_kernel(
    chunks, mine, other, v_in, system, extra, mean_v, x_hbm, out_hbm, mean_out,
    gram_full, obs_full, x_buf, o_buf, in_sem, out_sem,
):
    members = x_buf.shape[1]
    size = x_buf.shape[0] // chunks
    load = chunk_copy(x_hbm, x_buf, in_sem, chunks)
    store = chunk_copy(o_buf, out_hbm, out_sem, chunks)
    for i in range(chunks):
        load(i).start()

    join(mine, other, gram_full, 0, GRAM_ROWS)
    join(mine, other, obs_full, GRAM_ROWS, SECOND_ROWS)
    half = members // 2
    quarter = half // 2
    second = obs_full[...]
    g00 = gram_full[:half, :half]
    g01 = gram_full[:half, half:]
    g11 = jnp.concatenate([gram_full[half:, :half], gram_full[half:, half:]], axis=0)
    gram = jnp.concatenate(
        [jnp.concatenate([g00, g01], axis=1), jnp.concatenate([g01.T, g11], axis=1)], axis=0
    )
    v = v_in[...]
    increment = extra[0:1, :]
    innov2 = column(extra[1:2, half:]) - jnp.sum(second * increment, axis=1, keepdims=True)
    before = jnp.sum(identity(half) * (g00 + g11))
    after1 = before - jnp.sum(dot(v, gram) * v)
    factor1 = blend(before, after1)

    a2 = dot(second, jnp.concatenate([second, innov2], axis=1), ((0,), (0,))) * (factor1 * factor1)
    k00 = system[:half, :half] + a2[:half, :half]
    k01 = system[:half, half:] + a2[:half, half:members]
    k11 = system[half:, half:] + a2[half:, half:members]
    inv00 = factor(k00)
    u = dot(inv00, k01)
    inv11 = factor(k11 - dot(u, u, ((0,), (0,))))
    inv10 = -dot(inv11, dot(u, inv00, ((0,), (0,))))
    y0 = dot(inv00, a2[:half, members:])
    y1 = dot(inv11, a2[half:, members:] - dot(u, y0, ((0,), (0,))))
    increment0 = jnp.sum(y0 * inv00 + y1 * inv10, axis=0, keepdims=True)
    increment1 = jnp.sum(y1 * inv11, axis=0, keepdims=True)
    increment = increment + jnp.concatenate([increment0, increment1], axis=1)
    inverse = jnp.concatenate(
        [jnp.concatenate([inv00, jnp.zeros_like(inv00)], axis=1), jnp.concatenate([inv10, inv11], axis=1)], axis=0
    )
    after2 = jnp.sum(dot(inverse, gram) * inverse)
    transform = inverse * (factor1 * blend(after1, after2))

    t_high, t_low = split(transform)
    t_all = jnp.concatenate([t_high, t_high, t_low], axis=1)
    w_high, w_low = split(increment)
    row16 = lax.broadcasted_iota(jnp.int32, (16, members), 0)
    w = jnp.where(row16 == 0, w_high.astype(F32), jnp.where(row16 == 1, w_low.astype(F32), 0.0)).astype(BF16)

    def apply(i, _):
        load(i).wait()
        part = pl.ds(pl.multiple_of(i * size, size), size)
        high, low = split(x_buf[part, :])
        o_buf[part, :] = dot(jnp.concatenate([high, low, high], axis=1), t_all, ((1,), (1,)), None)
        store(i).start()
        step = dot(w, high, ((1,), (1,)), None) + dot(w, low, ((1,), (1,)), None)
        where = pl.ds(pl.multiple_of(i * size, size), size)
        mean_out[:, where] = mean_v[:, where] + step[0:1, :] + step[1:2, :]
        return 0

    lax.fori_loop(0, chunks, apply, 0)
    for i in range(chunks):
        store(i).wait()


def spec(space):
    return pl.BlockSpec(memory_space=space)


def params():
    return pltpu.CompilerParams(vmem_limit_bytes=VMEM_LIMIT)


def cost(flops, bytes_accessed):
    return pl.CostEstimate(flops=flops, bytes_accessed=bytes_accessed, transcendentals=0)


def gram_halves(ensemble):
    rows, members = ensemble.shape
    chunks = 4
    half = jax.ShapeDtypeStruct((GRAM_ROWS, members), F32)
    return pl.pallas_call(
        functools.partial(gram_kernel, chunks),
        out_shape=(half, half),
        in_specs=[spec(pltpu.HBM)],
        out_specs=(spec(pltpu.VMEM), spec(pltpu.VMEM)),
        scratch_shapes=[
            pltpu.VMEM((2 * GRAM_ROWS, members), F32),
            pltpu.VMEM((rows, members), F32),
            pltpu.SemaphoreType.DMA((chunks,)),
        ],
        cost_estimate=cost(4 * rows * members * members, 4 * rows * members),
        compiler_params=params(),
    )(ensemble)


def gather(ensemble, mean_state, observed, error_var, owner, obs_rows, gram):
    rows, members = ensemble.shape
    chunks = 4
    first = jax.ShapeDtypeStruct((FIRST_HALF, members), F32)
    second = jax.ShapeDtypeStruct((SECOND_HALF, members), F32)
    out = pl.pallas_call(
        functools.partial(gather_kernel, chunks),
        out_shape=(first, first, second, second),
        in_specs=[spec(pltpu.SMEM), spec(pltpu.SMEM)] + [spec(pltpu.VMEM)] * 6 + [spec(pltpu.HBM)],
        out_specs=[spec(pltpu.VMEM)] * 4,
        scratch_shapes=[
            pltpu.VMEM((OBS, members), F32),
            pltpu.VMEM((rows, members), F32),
            pltpu.SemaphoreType.DMA((chunks,)),
        ],
        cost_estimate=cost(2 * rows * members * members, 4 * rows * members),
        compiler_params=params(),
    )(owner, obs_rows, obs_rows, observed, error_var, mean_state.reshape(-1, LANES), *gram, ensemble)
    return out[:2], out[2:]


def first_batch(first):
    members = first[0].shape[1]
    return pl.pallas_call(
        first_kernel,
        out_shape=(
            jax.ShapeDtypeStruct((OBS, members), F32),
            jax.ShapeDtypeStruct((members, members), F32),
            jax.ShapeDtypeStruct((SUB, members), F32),
        ),
        in_specs=[spec(pltpu.VMEM)] * 2,
        out_specs=[spec(pltpu.VMEM)] * 3,
        scratch_shapes=[pltpu.VMEM((OBS, members), F32)],
        cost_estimate=cost(5 * 10**9, 2 * OBS * members * 4),
        compiler_params=params(),
    )(*first)


def update(second, batch, ensemble, mean_state):
    rows, members = ensemble.shape
    chunks = 8
    out, mean = pl.pallas_call(
        functools.partial(update_kernel, chunks),
        out_shape=(jax.ShapeDtypeStruct((rows, members), F32), jax.ShapeDtypeStruct((1, rows), F32)),
        in_specs=[spec(pltpu.VMEM)] * 6 + [spec(pltpu.HBM)],
        out_specs=(spec(pltpu.HBM), spec(pltpu.VMEM)),
        scratch_shapes=[
            pltpu.VMEM((2 * GRAM_ROWS, members), F32),
            pltpu.VMEM((OBS, members), F32),
            pltpu.VMEM((rows, members), F32),
            pltpu.VMEM((rows, members), F32),
            pltpu.SemaphoreType.DMA((chunks,)),
            pltpu.SemaphoreType.DMA((chunks,)),
        ],
        compiler_params=params(),
    )(*second, *batch, mean_state.reshape(1, rows), ensemble)
    return out, mean.reshape(rows)


def swap(value, count, mask):
    return lax.ppermute(value, AXIS, [(i, i ^ mask) for i in range(count)])


def total(halves, count, beside=None):
    me = lax.axis_index(AXIS)
    keep, send = halves
    value = keep + swap(send, count, 1)
    odd = ((me >> 1) & 1) == 1
    low, high = jnp.split(value, 2, axis=0)
    value = jnp.where(odd, high, low) + swap(jnp.where(odd, low, high), count, 2)
    mask = 4
    while mask < count:
        value = value + swap(value, count, mask)
        mask *= 2
    got = swap(value, count, 2)
    if beside is not None:
        got, beside = lax.optimization_barrier((got, beside))
    value = jnp.concatenate([jnp.where(odd, got, value), jnp.where(odd, value, got)], axis=0)
    return (value, swap(value, count, 1)), beside


def on_device(count, ensemble, mean_state, observed, error_var, owner, obs_rows):
    gram = gram_halves(ensemble)
    first, second = gather(ensemble, mean_state, observed, error_var, owner, obs_rows, gram)
    batch = first_batch(total(first, count)[0])
    second, batch = total(second, count, batch)
    return update(second, batch, ensemble, mean_state)


def solution(mesh):
    count = mesh.shape[AXIS]
    in_specs = (
        P(("groups", "rows"), None),
        P(("groups", "rows")),
        P("groups", None),
        P("groups", None),
        P("groups"),
        P("groups", None),
    )
    out_specs = (P(("groups", "rows"), None), P(("groups", "rows")))

    def body(*args):
        return on_device(count, *args)

    return jax.shard_map(body, mesh=mesh, in_specs=in_specs, out_specs=out_specs, check_vma=False)
```

```python
import functools

import jax
import jax.numpy as jnp
from jax import lax
from jax.experimental import pallas as pl
from jax.experimental.pallas import tpu as pltpu
from jax.sharding import PartitionSpec as P

RELAX = 0.6
HI = lax.Precision.HIGHEST
AXIS = "rows"
F32 = jnp.float32
BF16 = jnp.bfloat16
LANES = 128
SUB = 8
OBS = 128
VMEM_LIMIT = 51 * 1024 * 1024
STEP = 16

A0, A1, B0, B1, G00, G01, G11 = range(0, 7 * 128, 128)
PACKED = 7 * 128
INNOV = G00 + 64


def dot(a, b, dims=((1,), (0,)), precision=HI):
    return lax.dot_general(a, b, (dims, ((), ())), precision=precision, preferred_element_type=F32)


def column(row):
    return jnp.broadcast_to(row, (LANES, LANES)).T


def split(x):
    high = x.astype(BF16)
    return high, (x - high.astype(F32)).astype(BF16)


def chunk_copy(source, target, sem, chunks):
    size = source.shape[0] // chunks

    def copy(i):
        part = pl.ds(i * size, size)
        return pltpu.make_async_copy(source.at[part], target.at[part], sem.at[i])

    return copy


def gram_kernel(chunks, x_hbm, out, x_buf, sem):
    members = x_buf.shape[1]
    size = x_buf.shape[0] // chunks
    half = members // 2
    copy = chunk_copy(x_hbm, x_buf, sem, chunks)
    for i in range(chunks):
        copy(i).start()
    total = None
    for i in range(chunks):
        copy(i).wait()
        high, low = split(x_buf[i * size : (i + 1) * size, :])
        part = dot(high, jnp.concatenate([high, low], axis=1), ((0,), (0,)), None)
        total = part if total is None else total + part
    cross = total[:, members:]
    total = total[:, :members] + cross + cross.T
    out[:half, :] = total[:half, :half]
    out[half : 2 * half, :] = total[:half, half:]
    out[2 * half :, :] = total[half:, half:]


def gather_kernel(
    owner_s, rows_s, rows_v, observed, error_var, mean_v, gram, x_hbm, keep, send, full, picked, sem
):
    me = lax.axis_index(AXIS)
    members = picked.shape[2]
    half = members // 2

    for k in range(2):

        @pl.when(owner_s[k] == me)
        def _(k=k):
            def fetch(o, _):
                pltpu.make_async_copy(
                    x_hbm.at[pl.ds(rows_s[k, o], 1)], picked.at[k, pl.ds(o, 1)], sem.at[k]
                ).start()
                return 0

            lax.fori_loop(0, OBS, fetch, 0, unroll=8)

    innovations = []
    scales = []
    lane = lax.broadcasted_iota(jnp.int32, (OBS, LANES), 1)
    for k in range(2):
        index = column(rows_v[k : k + 1, :].astype(F32)).astype(jnp.int32)
        prior = jnp.zeros((OBS, LANES), F32)
        for r in range(mean_v.shape[0]):
            prior = prior + jnp.where(index == lane + r * LANES, mean_v[r : r + 1, :], 0.0)
        prior = jnp.sum(prior.T, axis=0, keepdims=True)
        scale = lax.rsqrt(error_var[k : k + 1, :] * (members - 1.0))
        scales.append(column(scale))
        innov = jnp.where(owner_s[k] == me, scale * (observed[k : k + 1, :] - prior), 0.0)
        innovations += [innov[:, : half // 2], innov[:, half // 2 :]]

    full[G00:, :] = gram[...]
    for i, innov in enumerate(innovations):
        full[INNOV + i : INNOV + i + 1, : half // 2] = innov
    full[:G00, :] = jnp.zeros((G00, LANES), F32)
    for k, left, right in ((0, A0, A1), (1, B0, B1)):

        @pl.when(owner_s[k] == me)
        def _(k=k, left=left, right=right):
            pltpu.make_async_copy(x_hbm.at[pl.ds(0, OBS)], picked.at[k], sem.at[k]).wait()
            full[left : left + OBS, :] = picked[k, :, :half] * scales[k]
            full[right : right + OBS, :] = picked[k, :, half:] * scales[k]

    mine = me & 1
    span = PACKED // 2
    keep[...] = full[pl.ds(pl.multiple_of(mine * span, SUB), span), :]
    send[...] = full[pl.ds(pl.multiple_of((1 - mine) * span, SUB), span), :]


def tree(terms):
    while len(terms) > 1:
        terms = [terms[i] + terms[i + 1] if i + 1 < len(terms) else terms[i] for i in range(0, len(terms), 2)]
    return terms[0]


def factor(a):
    count = LANES // SUB
    lane = lax.broadcasted_iota(jnp.int32, (SUB, LANES), 1)
    sub = lax.broadcasted_iota(jnp.int32, (SUB, LANES), 0)
    rows = [a[SUB * i : SUB * (i + 1), :] for i in range(count)]
    out = []

    def spread(x, c):
        return jnp.broadcast_to(x[:, c : c + 1], (SUB, LANES))

    def row(x, j):
        return jnp.broadcast_to(x[j : j + 1, :], (SUB, LANES))

    groups = STEP // SUB
    for s in range(0, count, groups):
        base = SUB * s
        here = (lane >= base) & (lane < base + STEP)
        cols = [[spread(rows[s + g], base + q) for g in range(groups)] for q in range(STEP)]
        work = [
            jnp.where(here, (lane - base == sub + SUB * g).astype(F32), rows[s + g]) for g in range(groups)
        ]
        done = [jnp.zeros((SUB, LANES), F32) for _ in range(groups)]
        for p in range(0, STEP, 2):
            at, j = divmod(p, SUB)
            first, second = sub == j, sub == j + 1
            pair = first | second
            pa, pb, pc = row(cols[p][at], j), row(cols[p][at], j + 1), row(cols[p + 1][at], j + 1)
            det = pa * pc - pb * pb
            inv = pl.reciprocal(det, approx=True)
            top, low = row(work[at], j), row(work[at], j + 1)
            done[at] = jnp.where(first, top * lax.rsqrt(pa), done[at])
            done[at] = jnp.where(second, (pa * low - pb * top) * lax.rsqrt(pa * det), done[at])
            raw, scaled = [], []
            for g in range(groups):
                m0, m1 = cols[p][g], cols[p + 1][g]
                if g == at:
                    m0 = jnp.where(first, -1.0, jnp.where(second, 0.0, m0))
                    m1 = jnp.where(second, -1.0, jnp.where(first, 0.0, m1))
                u0, u1 = m0 * pc - m1 * pb, m1 * pa - m0 * pb
                raw.append((u0, u1))
                scaled.append((u0 * inv, u1 * inv))
            for q in range(p + 2, STEP + 1):
                kept = cols[q] if q < STEP else work
                t, l = row(kept[at], j), row(kept[at], j + 1)
                moved = []
                for g in range(groups):
                    old = jnp.where(pair, 0.0, kept[g]) if g == at else kept[g]
                    if q < p + 4:
                        moved.append(old - (raw[g][0] * t + raw[g][1] * l) * inv)
                    else:
                        moved.append(old - (scaled[g][0] * t + scaled[g][1] * l))
                if q < STEP:
                    cols[q] = moved
                else:
                    work = moved
        for g in range(groups):
            out.append(jnp.where(lane <= base + SUB * g + sub, done[g], 0.0))
        lines = [row(work[p // SUB], p % SUB) for p in range(STEP)]
        for i in range(s + groups, count):
            change = tree([spread(rows[i], base + p) * lines[p] for p in range(STEP)])
            rows[i] = jnp.where(here, 0.0, rows[i]) - change
    return jnp.concatenate(out, axis=0)


def blend(before, after):
    return 1.0 + RELAX * (jnp.sqrt(before / after) - 1.0)


def add_up(x):
    return jnp.sum(jnp.sum(x, axis=0, keepdims=True), axis=1, keepdims=True)


def dot3(a, b):
    a_high, a_low = split(a)
    b_high, b_low = split(b)
    return dot(
        jnp.concatenate([a_high, a_low, a_high], axis=1), jnp.concatenate([b_high, b_high, b_low], axis=0), precision=None
    )


def identity(size):
    return (
        lax.broadcasted_iota(jnp.int32, (size, size), 0) == lax.broadcasted_iota(jnp.int32, (size, size), 1)
    ).astype(F32)


def update_kernel(
    chunks, mine_v, other_v, mean_v, x_hbm, out_hbm, mean_out, full, x_buf, o_buf, in_sem, out_sem
):
    members = x_buf.shape[1]
    size = x_buf.shape[0] // chunks
    load = chunk_copy(x_hbm, x_buf, in_sem, chunks)
    store = chunk_copy(o_buf, out_hbm, out_sem, chunks)
    for i in range(chunks):
        load(i).start()

    mine = lax.axis_index(AXIS) & 1
    span = PACKED // 2
    full[pl.ds(pl.multiple_of(mine * span, SUB), span), :] = mine_v[...]
    full[pl.ds(pl.multiple_of((1 - mine) * span, SUB), span), :] = other_v[...]

    half = members // 2
    quarter = half // 2

    def block(at):
        return full[at : at + half, :]

    def innovation(k):
        at = INNOV + 2 * k
        return column(jnp.concatenate([full[at : at + 1, :quarter], full[at + 1 : at + 2, :quarter]], axis=1))

    first = jnp.concatenate([block(A0), block(A1)], axis=1)
    second = jnp.concatenate([block(B0), block(B1)], axis=1)
    g00, g01, g11 = block(G00), block(G01), block(G11)
    line = lax.broadcasted_iota(jnp.int32, (half, half), 0)
    lane = lax.broadcasted_iota(jnp.int32, (half, half), 1)
    g00 = jnp.where((line >= quarter) & (lane < quarter), g00.T, g00)
    gram = jnp.concatenate(
        [jnp.concatenate([g00, g01], axis=1), jnp.concatenate([g01.T, g11], axis=1)], axis=0
    )
    eye = identity(half)

    inv_m = factor(eye + dot(first, first, ((1,), (1,))))
    v_and_f = dot(inv_m, jnp.concatenate([first, innovation(0)], axis=1))
    v, f = v_and_f[:, :members], v_and_f[:, members:]
    before = add_up(eye * (g00 + g11))
    after1 = before - add_up(dot3(v, gram) * v)
    factor1 = blend(before, after1)
    increment = jnp.sum(v * jnp.concatenate([f, f], axis=1), axis=0, keepdims=True)
    innov2 = innovation(1) - jnp.sum(second * increment, axis=1, keepdims=True)

    a1 = dot(first, first, ((0,), (0,)))
    a2 = dot(second, jnp.concatenate([second, innov2], axis=1), ((0,), (0,)))
    square = factor1 * factor1
    k00 = eye + a1[:half, :half] + a2[:half, :half] * square
    k01 = a1[:half, half:] + a2[:half, half:members] * square
    k11 = eye + a1[half:, half:] + a2[half:, half:members] * square
    inv00 = factor(k00)
    u = dot(inv00, k01)
    inv11 = factor(k11 - dot(u, u, ((0,), (0,))))
    inv10 = -dot(inv11, dot(u, inv00, ((0,), (0,))))
    y0 = dot(inv00, a2[:half, members:] * square)
    y1 = dot(inv11, a2[half:, members:] * square - dot(u, y0, ((0,), (0,))))
    bottom = jnp.concatenate([inv10, inv11], axis=1)
    top_trace = add_up(dot3(inv00, g00) * inv00)
    after2 = top_trace + add_up(dot3(bottom, gram) * bottom)
    factor2 = factor1 * blend(after1, after2)
    increment0 = jnp.sum(y0 * inv00 + y1 * inv10, axis=0, keepdims=True)
    increment1 = jnp.sum(y1 * inv11, axis=0, keepdims=True)
    increment = increment + jnp.concatenate([increment0, increment1], axis=1)

    inverse = jnp.concatenate([jnp.concatenate([inv00, jnp.zeros_like(inv00)], axis=1), bottom], axis=0)
    high, low = split(inverse)
    transform = jnp.concatenate([high, high, low], axis=1)
    step_line = lax.broadcasted_iota(jnp.int32, (LANES, LANES), 0)
    diagonal = step_line == lax.broadcasted_iota(jnp.int32, (LANES, LANES), 1)

    def apply(i, at):
        load(i).wait()
        x = x_buf[pl.ds(at, size), :]
        high, low = split(x)
        moved = dot(jnp.concatenate([high, low, high], axis=1), transform, ((1,), (1,)), None)
        o_buf[pl.ds(at, size), :] = moved * factor2
        store(i).start()
        steps = jnp.sum(x * increment, axis=1, keepdims=True)
        for j in range(0, size, LANES):
            step = jnp.sum(jnp.where(diagonal, steps[j : j + LANES, :], 0.0), axis=0, keepdims=True)
            part = pl.ds(at + j, LANES)
            mean_out[:, part] = mean_v[:, part] + step

    apply(0, 0)

    def body(i, _):
        apply(i, pl.multiple_of(i * size, size))
        return 0

    lax.fori_loop(1, chunks, body, 0)
    for i in range(chunks):
        store(i).wait()


def spec(space):
    return pl.BlockSpec(memory_space=space)


def params():
    return pltpu.CompilerParams(vmem_limit_bytes=VMEM_LIMIT)


def cost(flops, bytes_accessed):
    return pl.CostEstimate(flops=flops, bytes_accessed=bytes_accessed, transcendentals=0)


def cost(flops, bytes_accessed):
    return pl.CostEstimate(flops=flops, bytes_accessed=bytes_accessed, transcendentals=0)


def gram_of(ensemble):
    rows, members = ensemble.shape
    chunks = 4
    return pl.pallas_call(
        functools.partial(gram_kernel, chunks),
        out_shape=jax.ShapeDtypeStruct((PACKED - G00, LANES), F32),
        in_specs=[spec(pltpu.HBM)],
        out_specs=spec(pltpu.VMEM),
        scratch_shapes=[pltpu.VMEM((rows, members), F32), pltpu.SemaphoreType.DMA((chunks,))],
        cost_estimate=cost(4 * rows * members * members, 4 * rows * members),
        compiler_params=params(),
    )(ensemble)


def gather(ensemble, mean_state, observed, error_var, owner, obs_rows, gram):
    members = ensemble.shape[1]
    half = jax.ShapeDtypeStruct((PACKED // 2, LANES), F32)
    return pl.pallas_call(
        gather_kernel,
        out_shape=(half, half),
        in_specs=[spec(pltpu.SMEM), spec(pltpu.SMEM)] + [spec(pltpu.VMEM)] * 5 + [spec(pltpu.HBM)],
        out_specs=[spec(pltpu.VMEM)] * 2,
        scratch_shapes=[
            pltpu.VMEM((PACKED, LANES), F32),
            pltpu.VMEM((2, OBS, members), F32),
            pltpu.SemaphoreType.DMA((2,)),
        ],
        compiler_params=params(),
    )(owner, obs_rows, obs_rows, observed, error_var, mean_state.reshape(-1, LANES), gram, ensemble)


def update(packed, ensemble, mean_state):
    rows, members = ensemble.shape
    chunks = 8
    out, mean = pl.pallas_call(
        functools.partial(update_kernel, chunks),
        out_shape=(jax.ShapeDtypeStruct((rows, members), F32), jax.ShapeDtypeStruct((1, rows), F32)),
        in_specs=[spec(pltpu.VMEM)] * 3 + [spec(pltpu.HBM)],
        out_specs=(spec(pltpu.HBM), spec(pltpu.VMEM)),
        scratch_shapes=[
            pltpu.VMEM((PACKED, LANES), F32),
            pltpu.VMEM((rows, members), F32),
            pltpu.VMEM((rows, members), F32),
            pltpu.SemaphoreType.DMA((chunks,)),
            pltpu.SemaphoreType.DMA((chunks,)),
        ],
        compiler_params=params(),
    )(*packed, mean_state.reshape(1, rows), ensemble)
    return out, mean.reshape(rows)


def swap(value, count, mask):
    return lax.ppermute(value, AXIS, [(i, i ^ mask) for i in range(count)])


def total(keep, send, count):
    odd = ((lax.axis_index(AXIS) >> 1) & 1) == 1
    value = keep + swap(send, count, 1)
    low, high = jnp.split(value, 2, axis=0)
    value = jnp.where(odd, high, low) + swap(jnp.where(odd, low, high), count, 2)
    mask = 4
    while mask < count:
        value = value + swap(value, count, mask)
        mask *= 2
    got = swap(value, count, 2)
    value = jnp.concatenate([jnp.where(odd, got, value), jnp.where(odd, value, got)], axis=0)
    return value, swap(value, count, 1)


def on_device(count, ensemble, mean_state, observed, error_var, owner, obs_rows):
    gram = gram_of(ensemble)
    keep, send = gather(ensemble, mean_state, observed, error_var, owner, obs_rows, gram)
    return update(total(keep, send, count), ensemble, mean_state)


def solution(mesh):
    count = mesh.shape[AXIS]
    in_specs = (
        P(("groups", "rows"), None),
        P(("groups", "rows")),
        P("groups", None),
        P("groups", None),
        P("groups"),
        P("groups", None),
    )
    out_specs = (P(("groups", "rows"), None), P(("groups", "rows")))

    def body(*args):
        return on_device(count, *args)

    return jax.shard_map(body, mesh=mesh, in_specs=in_specs, out_specs=out_specs, check_vma=False)
```

```python
import functools

import jax
import jax.numpy as jnp
from jax import lax
from jax.experimental import pallas as pl
from jax.experimental.pallas import tpu as pltpu
from jax.sharding import PartitionSpec as P

RELAX = 0.6
HI = lax.Precision.HIGHEST
AXIS = "rows"
F32 = jnp.float32
BF16 = jnp.bfloat16
LANES = 128
SUB = 8
OBS = 128
VMEM_LIMIT = 51 * 1024 * 1024
STEP = 16

A0, A1, B0, B1, G00, G01, G11 = range(0, 7 * 128, 128)
PACKED = 7 * 128
INNOV = G00 + 64


def dot(a, b, dims=((1,), (0,)), precision=HI):
    return lax.dot_general(a, b, (dims, ((), ())), precision=precision, preferred_element_type=F32)


def column(row):
    return jnp.broadcast_to(row, (LANES, LANES)).T


def split(x):
    high = x.astype(BF16)
    return high, (x - high.astype(F32)).astype(BF16)


def chunk_copy(source, target, sem, chunks):
    size = source.shape[0] // chunks

    def copy(i):
        part = pl.ds(i * size, size)
        return pltpu.make_async_copy(source.at[part], target.at[part], sem.at[i])

    return copy


def gram_kernel(chunks, x_hbm, out, x_buf, sem):
    members = x_buf.shape[1]
    size = x_buf.shape[0] // chunks
    half = members // 2
    copy = chunk_copy(x_hbm, x_buf, sem, chunks)
    for i in range(chunks):
        copy(i).start()
    total = None
    for i in range(chunks):
        copy(i).wait()
        high, low = split(x_buf[i * size : (i + 1) * size, :])
        part = dot(high, jnp.concatenate([high, low], axis=1), ((0,), (0,)), None)
        total = part if total is None else total + part
    cross = total[:, members:]
    total = total[:, :members] + cross + cross.T
    out[:half, :] = total[:half, :half]
    out[half : 2 * half, :] = total[:half, half:]
    out[2 * half :, :] = total[half:, half:]


def gather_kernel(
    owner_s, rows_s, rows_v, observed, error_var, mean_v, gram, x_hbm, keep, send, full, picked, sem
):
    me = lax.axis_index(AXIS)
    members = picked.shape[2]
    half = members // 2

    for k in range(2):

        @pl.when(owner_s[k] == me)
        def _(k=k):
            def fetch(o, _):
                pltpu.make_async_copy(
                    x_hbm.at[pl.ds(rows_s[k, o], 1)], picked.at[k, pl.ds(o, 1)], sem.at[k]
                ).start()
                return 0

            lax.fori_loop(0, OBS, fetch, 0, unroll=8)

    innovations = []
    scales = []
    lane = lax.broadcasted_iota(jnp.int32, (OBS, LANES), 1)
    for k in range(2):
        index = column(rows_v[k : k + 1, :].astype(F32)).astype(jnp.int32)
        prior = jnp.zeros((OBS, LANES), F32)
        for r in range(mean_v.shape[0]):
            prior = prior + jnp.where(index == lane + r * LANES, mean_v[r : r + 1, :], 0.0)
        prior = jnp.sum(prior.T, axis=0, keepdims=True)
        scale = lax.rsqrt(error_var[k : k + 1, :] * (members - 1.0))
        scales.append(column(scale))
        innov = jnp.where(owner_s[k] == me, scale * (observed[k : k + 1, :] - prior), 0.0)
        innovations += [innov[:, : half // 2], innov[:, half // 2 :]]

    full[G00:, :] = gram[...]
    for i, innov in enumerate(innovations):
        full[INNOV + i : INNOV + i + 1, : half // 2] = innov
    full[:G00, :] = jnp.zeros((G00, LANES), F32)
    for k, left, right in ((0, A0, A1), (1, B0, B1)):

        @pl.when(owner_s[k] == me)
        def _(k=k, left=left, right=right):
            pltpu.make_async_copy(x_hbm.at[pl.ds(0, OBS)], picked.at[k], sem.at[k]).wait()
            full[left : left + OBS, :] = picked[k, :, :half] * scales[k]
            full[right : right + OBS, :] = picked[k, :, half:] * scales[k]

    mine = me & 1
    span = PACKED // 2
    keep[...] = full[pl.ds(pl.multiple_of(mine * span, SUB), span), :]
    send[...] = full[pl.ds(pl.multiple_of((1 - mine) * span, SUB), span), :]


def tree(terms):
    while len(terms) > 1:
        terms = [terms[i] + terms[i + 1] if i + 1 < len(terms) else terms[i] for i in range(0, len(terms), 2)]
    return terms[0]


def factor(a):
    count = LANES // SUB
    lane = lax.broadcasted_iota(jnp.int32, (SUB, LANES), 1)
    sub = lax.broadcasted_iota(jnp.int32, (SUB, LANES), 0)
    rows = [a[SUB * i : SUB * (i + 1), :] for i in range(count)]
    out = []

    def spread(x, c):
        return jnp.broadcast_to(x[:, c : c + 1], (SUB, LANES))

    def row(x, j):
        return jnp.broadcast_to(x[j : j + 1, :], (SUB, LANES))

    groups = STEP // SUB
    for s in range(0, count, groups):
        base = SUB * s
        here = (lane >= base) & (lane < base + STEP)
        cols = [[spread(rows[s + g], base + q) for g in range(groups)] for q in range(STEP)]
        work = [
            jnp.where(here, (lane - base == sub + SUB * g).astype(F32), rows[s + g]) for g in range(groups)
        ]
        done = [jnp.zeros((SUB, LANES), F32) for _ in range(groups)]
        for p in range(0, STEP, 2):
            at, j = divmod(p, SUB)
            first, second = sub == j, sub == j + 1
            pair = first | second
            pa, pb, pc = row(cols[p][at], j), row(cols[p][at], j + 1), row(cols[p + 1][at], j + 1)
            det = pa * pc - pb * pb
            inv = pl.reciprocal(det, approx=True)
            top, low = row(work[at], j), row(work[at], j + 1)
            done[at] = jnp.where(first, top * lax.rsqrt(pa), done[at])
            done[at] = jnp.where(second, (pa * low - pb * top) * lax.rsqrt(pa * det), done[at])
            raw, scaled = [], []
            for g in range(groups):
                m0, m1 = cols[p][g], cols[p + 1][g]
                if g == at:
                    m0 = jnp.where(first, -1.0, jnp.where(second, 0.0, m0))
                    m1 = jnp.where(second, -1.0, jnp.where(first, 0.0, m1))
                u0, u1 = m0 * pc - m1 * pb, m1 * pa - m0 * pb
                raw.append((u0, u1))
                scaled.append((u0 * inv, u1 * inv))
            for q in range(p + 2, STEP + 1):
                kept = cols[q] if q < STEP else work
                t, l = row(kept[at], j), row(kept[at], j + 1)
                moved = []
                for g in range(groups):
                    old = jnp.where(pair, 0.0, kept[g]) if g == at else kept[g]
                    if q < p + 4:
                        moved.append(old - (raw[g][0] * t + raw[g][1] * l) * inv)
                    else:
                        moved.append(old - (scaled[g][0] * t + scaled[g][1] * l))
                if q < STEP:
                    cols[q] = moved
                else:
                    work = moved
        for g in range(groups):
            out.append(jnp.where(lane <= base + SUB * g + sub, done[g], 0.0))
        lines = [row(work[p // SUB], p % SUB) for p in range(STEP)]
        later = s + 2 * groups
        for i in range(s + groups, min(later, count)):
            change = tree([spread(rows[i], base + p) * lines[p] for p in range(STEP)])
            rows[i] = jnp.where(here, 0.0, rows[i]) - change
        if later < count:
            rest = jnp.concatenate(rows[later:], axis=0)
            inside = jnp.concatenate([here] * (count - later), axis=0)
            pieces = [jnp.zeros((base, LANES), F32)] if base else []
            pieces += work + [jnp.zeros((LANES - base - STEP, LANES), F32)]
            change = dot(jnp.where(inside, rest, 0.0), jnp.concatenate(pieces, axis=0))
            rest = jnp.where(inside, 0.0, rest) - change
            rows[later:] = [rest[SUB * i : SUB * (i + 1), :] for i in range(count - later)]
    return jnp.concatenate(out, axis=0)


def blend(before, after):
    return 1.0 + RELAX * (jnp.sqrt(before / after) - 1.0)


def add_up(x):
    return jnp.sum(jnp.sum(x, axis=0, keepdims=True), axis=1, keepdims=True)


def dot3(a, b):
    a_high, a_low = split(a)
    b_high, b_low = split(b)
    return dot(
        jnp.concatenate([a_high, a_low, a_high], axis=1), jnp.concatenate([b_high, b_high, b_low], axis=0), precision=None
    )


def identity(size):
    return (
        lax.broadcasted_iota(jnp.int32, (size, size), 0) == lax.broadcasted_iota(jnp.int32, (size, size), 1)
    ).astype(F32)


def update_kernel(
    chunks, mine_v, other_v, mean_v, x_hbm, out_hbm, mean_out, full, x_buf, o_buf, in_sem, out_sem
):
    members = x_buf.shape[1]
    size = x_buf.shape[0] // chunks
    load = chunk_copy(x_hbm, x_buf, in_sem, chunks)
    store = chunk_copy(o_buf, out_hbm, out_sem, chunks)
    for i in range(chunks):
        load(i).start()

    mine = lax.axis_index(AXIS) & 1
    span = PACKED // 2
    full[pl.ds(pl.multiple_of(mine * span, SUB), span), :] = mine_v[...]
    full[pl.ds(pl.multiple_of((1 - mine) * span, SUB), span), :] = other_v[...]

    half = members // 2
    quarter = half // 2

    def block(at):
        return full[at : at + half, :]

    def innovation(k):
        at = INNOV + 2 * k
        return column(jnp.concatenate([full[at : at + 1, :quarter], full[at + 1 : at + 2, :quarter]], axis=1))

    first = jnp.concatenate([block(A0), block(A1)], axis=1)
    second = jnp.concatenate([block(B0), block(B1)], axis=1)
    g00, g01, g11 = block(G00), block(G01), block(G11)
    line = lax.broadcasted_iota(jnp.int32, (half, half), 0)
    lane = lax.broadcasted_iota(jnp.int32, (half, half), 1)
    g00 = jnp.where((line >= quarter) & (lane < quarter), g00.T, g00)
    gram = jnp.concatenate(
        [jnp.concatenate([g00, g01], axis=1), jnp.concatenate([g01.T, g11], axis=1)], axis=0
    )
    eye = identity(half)

    inv_m = factor(eye + dot(first, first, ((1,), (1,))))
    v_and_f = dot(inv_m, jnp.concatenate([first, innovation(0)], axis=1))
    v, f = v_and_f[:, :members], v_and_f[:, members:]
    before = add_up(eye * (g00 + g11))
    after1 = before - add_up(dot3(v, gram) * v)
    factor1 = blend(before, after1)
    increment = jnp.sum(v * jnp.concatenate([f, f], axis=1), axis=0, keepdims=True)
    innov2 = innovation(1) - jnp.sum(second * increment, axis=1, keepdims=True)

    a1 = dot(first, first, ((0,), (0,)))
    a2 = dot(second, jnp.concatenate([second, innov2], axis=1), ((0,), (0,)))
    square = factor1 * factor1
    k00 = eye + a1[:half, :half] + a2[:half, :half] * square
    k01 = a1[:half, half:] + a2[:half, half:members] * square
    k11 = eye + a1[half:, half:] + a2[half:, half:members] * square
    inv00 = factor(k00)
    u = dot(inv00, k01)
    inv11 = factor(k11 - dot(u, u, ((0,), (0,))))
    inv10 = -dot(inv11, dot(u, inv00, ((0,), (0,))))
    y0 = dot(inv00, a2[:half, members:] * square)
    y1 = dot(inv11, a2[half:, members:] * square - dot(u, y0, ((0,), (0,))))
    bottom = jnp.concatenate([inv10, inv11], axis=1)
    top_trace = add_up(dot3(inv00, g00) * inv00)
    after2 = top_trace + add_up(dot3(bottom, gram) * bottom)
    factor2 = factor1 * blend(after1, after2)
    increment0 = jnp.sum(y0 * inv00 + y1 * inv10, axis=0, keepdims=True)
    increment1 = jnp.sum(y1 * inv11, axis=0, keepdims=True)
    increment = increment + jnp.concatenate([increment0, increment1], axis=1)

    inverse = jnp.concatenate([jnp.concatenate([inv00, jnp.zeros_like(inv00)], axis=1), bottom], axis=0)
    high, low = split(inverse)
    transform = jnp.concatenate([high, high, low], axis=1)
    step_line = lax.broadcasted_iota(jnp.int32, (LANES, LANES), 0)
    diagonal = step_line == lax.broadcasted_iota(jnp.int32, (LANES, LANES), 1)

    def apply(i, at):
        load(i).wait()
        x = x_buf[pl.ds(at, size), :]
        high, low = split(x)
        moved = dot(jnp.concatenate([high, low, high], axis=1), transform, ((1,), (1,)), None)
        o_buf[pl.ds(at, size), :] = moved * factor2
        store(i).start()
        steps = jnp.sum(x * increment, axis=1, keepdims=True)
        for j in range(0, size, LANES):
            step = jnp.sum(jnp.where(diagonal, steps[j : j + LANES, :], 0.0), axis=0, keepdims=True)
            part = pl.ds(at + j, LANES)
            mean_out[:, part] = mean_v[:, part] + step

    apply(0, 0)

    def body(i, _):
        apply(i, pl.multiple_of(i * size, size))
        return 0

    lax.fori_loop(1, chunks, body, 0)
    for i in range(chunks):
        store(i).wait()


def spec(space):
    return pl.BlockSpec(memory_space=space)


def params():
    return pltpu.CompilerParams(vmem_limit_bytes=VMEM_LIMIT)


def cost(flops, bytes_accessed):
    return pl.CostEstimate(flops=flops, bytes_accessed=bytes_accessed, transcendentals=0)


def cost(flops, bytes_accessed):
    return pl.CostEstimate(flops=flops, bytes_accessed=bytes_accessed, transcendentals=0)


def gram_of(ensemble):
    rows, members = ensemble.shape
    chunks = 4
    return pl.pallas_call(
        functools.partial(gram_kernel, chunks),
        out_shape=jax.ShapeDtypeStruct((PACKED - G00, LANES), F32),
        in_specs=[spec(pltpu.HBM)],
        out_specs=spec(pltpu.VMEM),
        scratch_shapes=[pltpu.VMEM((rows, members), F32), pltpu.SemaphoreType.DMA((chunks,))],
        cost_estimate=cost(4 * rows * members * members, 4 * rows * members),
        compiler_params=params(),
    )(ensemble)


def gather(ensemble, mean_state, observed, error_var, owner, obs_rows, gram):
    members = ensemble.shape[1]
    half = jax.ShapeDtypeStruct((PACKED // 2, LANES), F32)
    return pl.pallas_call(
        gather_kernel,
        out_shape=(half, half),
        in_specs=[spec(pltpu.SMEM), spec(pltpu.SMEM)] + [spec(pltpu.VMEM)] * 5 + [spec(pltpu.HBM)],
        out_specs=[spec(pltpu.VMEM)] * 2,
        scratch_shapes=[
            pltpu.VMEM((PACKED, LANES), F32),
            pltpu.VMEM((2, OBS, members), F32),
            pltpu.SemaphoreType.DMA((2,)),
        ],
        compiler_params=params(),
    )(owner, obs_rows, obs_rows, observed, error_var, mean_state.reshape(-1, LANES), gram, ensemble)


def update(packed, ensemble, mean_state):
    rows, members = ensemble.shape
    chunks = 8
    out, mean = pl.pallas_call(
        functools.partial(update_kernel, chunks),
        out_shape=(jax.ShapeDtypeStruct((rows, members), F32), jax.ShapeDtypeStruct((1, rows), F32)),
        in_specs=[spec(pltpu.VMEM)] * 3 + [spec(pltpu.HBM)],
        out_specs=(spec(pltpu.HBM), spec(pltpu.VMEM)),
        scratch_shapes=[
            pltpu.VMEM((PACKED, LANES), F32),
            pltpu.VMEM((rows, members), F32),
            pltpu.VMEM((rows, members), F32),
            pltpu.SemaphoreType.DMA((chunks,)),
            pltpu.SemaphoreType.DMA((chunks,)),
        ],
        compiler_params=params(),
    )(*packed, mean_state.reshape(1, rows), ensemble)
    return out, mean.reshape(rows)


def swap(value, count, mask):
    return lax.ppermute(value, AXIS, [(i, i ^ mask) for i in range(count)])


def total(keep, send, count):
    value = keep + swap(send, count, 1)
    parts = count // 2
    groups = [list(range(start, count, 2)) for start in (0, 1)]

    def trade(x):
        return lax.all_to_all(x, AXIS, split_axis=0, concat_axis=0, axis_index_groups=groups)

    shares = value.reshape(parts, value.shape[0] // parts, LANES)
    share = jnp.sum(trade(shares), axis=0)
    value = trade(jnp.broadcast_to(share, (parts,) + share.shape)).reshape(value.shape)
    return value, swap(value, count, 1)


def on_device(count, ensemble, mean_state, observed, error_var, owner, obs_rows):
    gram = gram_of(ensemble)
    keep, send = gather(ensemble, mean_state, observed, error_var, owner, obs_rows, gram)
    return update(total(keep, send, count), ensemble, mean_state)


def solution(mesh):
    count = mesh.shape[AXIS]
    in_specs = (
        P(("groups", "rows"), None),
        P(("groups", "rows")),
        P("groups", None),
        P("groups", None),
        P("groups"),
        P("groups", None),
    )
    out_specs = (P(("groups", "rows"), None), P(("groups", "rows")))

    def body(*args):
        return on_device(count, *args)

    return jax.shard_map(body, mesh=mesh, in_specs=in_specs, out_specs=out_specs, check_vma=False)
```

```python
import functools

import jax
import jax.numpy as jnp
from jax import lax
from jax.experimental import pallas as pl
from jax.experimental.pallas import tpu as pltpu
from jax.sharding import PartitionSpec as P

RELAX = 0.6
HI = lax.Precision.HIGHEST
AXIS = "rows"
F32 = jnp.float32
BF16 = jnp.bfloat16
LANES = 128
SUB = 8
OBS = 128
VMEM_LIMIT = 51 * 1024 * 1024
STEP = 16

A0, A1, B0, B1, G00, G01, G11 = range(0, 7 * 128, 128)
PACKED = 7 * 128
INNOV = G00 + 64


def dot(a, b, dims=((1,), (0,)), precision=HI):
    return lax.dot_general(a, b, (dims, ((), ())), precision=precision, preferred_element_type=F32)


def column(row):
    return jnp.broadcast_to(row, (LANES, LANES)).T


def split(x):
    high = x.astype(BF16)
    return high, (x - high.astype(F32)).astype(BF16)


def chunk_copy(source, target, sem, chunks):
    size = source.shape[0] // chunks

    def copy(i):
        part = pl.ds(i * size, size)
        return pltpu.make_async_copy(source.at[part], target.at[part], sem.at[i])

    return copy


def gram_kernel(chunks, x_hbm, out, x_buf, sem):
    members = x_buf.shape[1]
    size = x_buf.shape[0] // chunks
    half = members // 2
    copy = chunk_copy(x_hbm, x_buf, sem, chunks)
    for i in range(chunks):
        copy(i).start()
    total = None
    for i in range(chunks):
        copy(i).wait()
        high, low = split(x_buf[i * size : (i + 1) * size, :])
        part = dot(high, jnp.concatenate([high, low], axis=1), ((0,), (0,)), None)
        total = part if total is None else total + part
    cross = total[:, members:]
    total = total[:, :members] + cross + cross.T
    out[:half, :] = total[:half, :half]
    out[half : 2 * half, :] = total[:half, half:]
    out[2 * half :, :] = total[half:, half:]


def gather_kernel(
    owner_s, rows_s, rows_v, observed, error_var, mean_v, gram, x_hbm, keep, send, full, picked, sem
):
    me = lax.axis_index(AXIS)
    members = picked.shape[2]
    half = members // 2

    for k in range(2):

        @pl.when(owner_s[k] == me)
        def _(k=k):
            def fetch(o, _):
                pltpu.make_async_copy(
                    x_hbm.at[pl.ds(rows_s[k, o], 1)], picked.at[k, pl.ds(o, 1)], sem.at[k]
                ).start()
                return 0

            lax.fori_loop(0, OBS, fetch, 0, unroll=8)

    innovations = []
    scales = []
    lane = lax.broadcasted_iota(jnp.int32, (OBS, LANES), 1)
    for k in range(2):
        index = column(rows_v[k : k + 1, :].astype(F32)).astype(jnp.int32)
        prior = jnp.zeros((OBS, LANES), F32)
        for r in range(mean_v.shape[0]):
            prior = prior + jnp.where(index == lane + r * LANES, mean_v[r : r + 1, :], 0.0)
        prior = jnp.sum(prior.T, axis=0, keepdims=True)
        scale = lax.rsqrt(error_var[k : k + 1, :] * (members - 1.0))
        scales.append(column(scale))
        innov = jnp.where(owner_s[k] == me, scale * (observed[k : k + 1, :] - prior), 0.0)
        innovations += [innov[:, : half // 2], innov[:, half // 2 :]]

    full[G00:, :] = gram[...]
    for i, innov in enumerate(innovations):
        full[INNOV + i : INNOV + i + 1, : half // 2] = innov
    full[:G00, :] = jnp.zeros((G00, LANES), F32)
    for k, left, right in ((0, A0, A1), (1, B0, B1)):

        @pl.when(owner_s[k] == me)
        def _(k=k, left=left, right=right):
            pltpu.make_async_copy(x_hbm.at[pl.ds(0, OBS)], picked.at[k], sem.at[k]).wait()
            full[left : left + OBS, :] = picked[k, :, :half] * scales[k]
            full[right : right + OBS, :] = picked[k, :, half:] * scales[k]

    mine = me & 1
    span = PACKED // 2
    keep[...] = full[pl.ds(pl.multiple_of(mine * span, SUB), span), :]
    send[...] = full[pl.ds(pl.multiple_of((1 - mine) * span, SUB), span), :]


def tree(terms):
    while len(terms) > 1:
        terms = [terms[i] + terms[i + 1] if i + 1 < len(terms) else terms[i] for i in range(0, len(terms), 2)]
    return terms[0]


def factor(a):
    count = LANES // SUB
    lane = lax.broadcasted_iota(jnp.int32, (SUB, LANES), 1)
    sub = lax.broadcasted_iota(jnp.int32, (SUB, LANES), 0)
    rows = [a[SUB * i : SUB * (i + 1), :] for i in range(count)]
    out = []

    def spread(x, c):
        return jnp.broadcast_to(x[:, c : c + 1], (SUB, LANES))

    def row(x, j):
        return jnp.broadcast_to(x[j : j + 1, :], (SUB, LANES))

    groups = STEP // SUB
    for s in range(0, count, groups):
        base = SUB * s
        here = (lane >= base) & (lane < base + STEP)
        cols = [[spread(rows[s + g], base + q) for g in range(groups)] for q in range(STEP)]
        work = [
            jnp.where(here, (lane - base == sub + SUB * g).astype(F32), rows[s + g]) for g in range(groups)
        ]
        done = [jnp.zeros((SUB, LANES), F32) for _ in range(groups)]
        for p in range(0, STEP, 2):
            at, j = divmod(p, SUB)
            first, second = sub == j, sub == j + 1
            pair = first | second
            pa, pb, pc = row(cols[p][at], j), row(cols[p][at], j + 1), row(cols[p + 1][at], j + 1)
            det = pa * pc - pb * pb
            inv = pl.reciprocal(det, approx=True)
            top, low = row(work[at], j), row(work[at], j + 1)
            done[at] = jnp.where(first, top * lax.rsqrt(pa), done[at])
            done[at] = jnp.where(second, (pa * low - pb * top) * lax.rsqrt(pa * det), done[at])
            raw, scaled = [], []
            for g in range(groups):
                m0, m1 = cols[p][g], cols[p + 1][g]
                if g == at:
                    m0 = jnp.where(first, -1.0, jnp.where(second, 0.0, m0))
                    m1 = jnp.where(second, -1.0, jnp.where(first, 0.0, m1))
                u0, u1 = m0 * pc - m1 * pb, m1 * pa - m0 * pb
                raw.append((u0, u1))
                scaled.append((u0 * inv, u1 * inv))
            for q in range(p + 2, STEP + 1):
                kept = cols[q] if q < STEP else work
                t, l = row(kept[at], j), row(kept[at], j + 1)
                moved = []
                for g in range(groups):
                    old = jnp.where(pair, 0.0, kept[g]) if g == at else kept[g]
                    if q < p + 4:
                        moved.append(old - (raw[g][0] * t + raw[g][1] * l) * inv)
                    else:
                        moved.append(old - (scaled[g][0] * t + scaled[g][1] * l))
                if q < STEP:
                    cols[q] = moved
                else:
                    work = moved
        for g in range(groups):
            out.append(jnp.where(lane <= base + SUB * g + sub, done[g], 0.0))
        lines = [row(work[p // SUB], p % SUB) for p in range(STEP)]
        later = s + 2 * groups
        for i in range(s + groups, min(later, count)):
            change = tree([spread(rows[i], base + p) * lines[p] for p in range(STEP)])
            rows[i] = jnp.where(here, 0.0, rows[i]) - change
        if later < count:
            rest = jnp.concatenate(rows[later:], axis=0)
            inside = jnp.concatenate([here] * (count - later), axis=0)
            pieces = [jnp.zeros((base, LANES), F32)] if base else []
            pieces += work + [jnp.zeros((LANES - base - STEP, LANES), F32)]
            change = dot(jnp.where(inside, rest, 0.0), jnp.concatenate(pieces, axis=0))
            rest = jnp.where(inside, 0.0, rest) - change
            rows[later:] = [rest[SUB * i : SUB * (i + 1), :] for i in range(count - later)]
    return jnp.concatenate(out, axis=0)


def blend(before, after):
    return 1.0 + RELAX * (jnp.sqrt(before / after) - 1.0)


def add_up(x):
    return jnp.sum(jnp.sum(x, axis=0, keepdims=True), axis=1, keepdims=True)


def identity(size):
    return (
        lax.broadcasted_iota(jnp.int32, (size, size), 0) == lax.broadcasted_iota(jnp.int32, (size, size), 1)
    ).astype(F32)


def update_kernel(
    chunks, mine_v, other_v, mean_v, x_hbm, out_hbm, mean_out, full, x_buf, o_buf, in_sem, out_sem
):
    members = x_buf.shape[1]
    size = x_buf.shape[0] // chunks
    load = chunk_copy(x_hbm, x_buf, in_sem, chunks)
    store = chunk_copy(o_buf, out_hbm, out_sem, chunks)
    for i in range(chunks):
        load(i).start()

    mine = lax.axis_index(AXIS) & 1
    span = PACKED // 2
    full[pl.ds(pl.multiple_of(mine * span, SUB), span), :] = mine_v[...]
    full[pl.ds(pl.multiple_of((1 - mine) * span, SUB), span), :] = other_v[...]

    half = members // 2
    quarter = half // 2

    def block(at):
        return full[at : at + half, :]

    def innovation(k):
        at = INNOV + 2 * k
        return column(jnp.concatenate([full[at : at + 1, :quarter], full[at + 1 : at + 2, :quarter]], axis=1))

    first = jnp.concatenate([block(A0), block(A1)], axis=1)
    second = jnp.concatenate([block(B0), block(B1)], axis=1)
    g00, g01, g11 = block(G00), block(G01), block(G11)
    line = lax.broadcasted_iota(jnp.int32, (half, half), 0)
    lane = lax.broadcasted_iota(jnp.int32, (half, half), 1)
    g00 = jnp.where((line >= quarter) & (lane < quarter), g00.T, g00)
    gram = jnp.concatenate(
        [jnp.concatenate([g00, g01], axis=1), jnp.concatenate([g01.T, g11], axis=1)], axis=0
    )
    eye = identity(half)

    inv_m = factor(eye + dot(first, first, ((1,), (1,))))
    seen = dot(dot(first, gram), first, ((1,), (1,)))
    before = add_up(eye * (g00 + g11))
    after1 = before - add_up(dot(inv_m, seen) * inv_m)
    factor1 = blend(before, after1)

    a1 = dot(first, first, ((0,), (0,)))
    a2 = dot(second, second, ((0,), (0,)))
    square = factor1 * factor1
    k00 = eye + a1[:half, :half] + a2[:half, :half] * square
    k01 = a1[:half, half:] + a2[:half, half:] * square
    k11 = eye + a1[half:, half:] + a2[half:, half:] * square
    inv00 = factor(k00)
    u = dot(inv00, k01)
    inv11 = factor(k11 - dot(u, u, ((0,), (0,))))

    v_and_f = dot(inv_m, jnp.concatenate([first, innovation(0)], axis=1))
    v, f = v_and_f[:, :members], v_and_f[:, members:]
    increment = jnp.sum(v * jnp.concatenate([f, f], axis=1), axis=0, keepdims=True)
    innov2 = innovation(1) - jnp.sum(second * increment, axis=1, keepdims=True)
    target = dot(second, innov2, ((0,), (0,))) * square
    y0 = dot(inv00, target[:half, :])
    below = target[half:, :] - dot(u, y0, ((0,), (0,)))

    q = dot(u, inv00, ((0,), (0,)))
    inv10 = -dot(inv11, q)
    y1 = dot(inv11, below)
    left = g01.T - dot(q, g00)
    rest = g11 - dot(q, g01) - dot(left, q, ((1,), (1,)))
    after2 = add_up(dot(inv00, g00) * inv00) + add_up(dot(inv11, rest) * inv11)
    factor2 = factor1 * blend(after1, after2)
    increment0 = jnp.sum(y0 * inv00 + y1 * inv10, axis=0, keepdims=True)
    increment1 = jnp.sum(y1 * inv11, axis=0, keepdims=True)
    increment = increment + jnp.concatenate([increment0, increment1], axis=1)
    bottom = jnp.concatenate([inv10, inv11], axis=1)

    inverse = jnp.concatenate([jnp.concatenate([inv00, jnp.zeros_like(inv00)], axis=1), bottom], axis=0)
    high, low = split(inverse)
    transform = jnp.concatenate([high, high, low], axis=1)
    step_line = lax.broadcasted_iota(jnp.int32, (LANES, LANES), 0)
    diagonal = step_line == lax.broadcasted_iota(jnp.int32, (LANES, LANES), 1)

    def apply(i, at):
        load(i).wait()
        x = x_buf[pl.ds(at, size), :]
        high, low = split(x)
        moved = dot(jnp.concatenate([high, low, high], axis=1), transform, ((1,), (1,)), None)
        o_buf[pl.ds(at, size), :] = moved * factor2
        store(i).start()
        steps = jnp.sum(x * increment, axis=1, keepdims=True)
        for j in range(0, size, LANES):
            step = jnp.sum(jnp.where(diagonal, steps[j : j + LANES, :], 0.0), axis=0, keepdims=True)
            part = pl.ds(at + j, LANES)
            mean_out[:, part] = mean_v[:, part] + step

    apply(0, 0)

    def body(i, _):
        apply(i, pl.multiple_of(i * size, size))
        return 0

    lax.fori_loop(1, chunks, body, 0)
    for i in range(chunks):
        store(i).wait()


def spec(space):
    return pl.BlockSpec(memory_space=space)


def params():
    return pltpu.CompilerParams(vmem_limit_bytes=VMEM_LIMIT)


def cost(flops, bytes_accessed):
    return pl.CostEstimate(flops=flops, bytes_accessed=bytes_accessed, transcendentals=0)


def cost(flops, bytes_accessed):
    return pl.CostEstimate(flops=flops, bytes_accessed=bytes_accessed, transcendentals=0)


def gram_of(ensemble):
    rows, members = ensemble.shape
    chunks = 4
    return pl.pallas_call(
        functools.partial(gram_kernel, chunks),
        out_shape=jax.ShapeDtypeStruct((PACKED - G00, LANES), F32),
        in_specs=[spec(pltpu.HBM)],
        out_specs=spec(pltpu.VMEM),
        scratch_shapes=[pltpu.VMEM((rows, members), F32), pltpu.SemaphoreType.DMA((chunks,))],
        cost_estimate=cost(4 * rows * members * members, 4 * rows * members),
        compiler_params=params(),
    )(ensemble)


def gather(ensemble, mean_state, observed, error_var, owner, obs_rows, gram):
    members = ensemble.shape[1]
    half = jax.ShapeDtypeStruct((PACKED // 2, LANES), F32)
    return pl.pallas_call(
        gather_kernel,
        out_shape=(half, half),
        in_specs=[spec(pltpu.SMEM), spec(pltpu.SMEM)] + [spec(pltpu.VMEM)] * 5 + [spec(pltpu.HBM)],
        out_specs=[spec(pltpu.VMEM)] * 2,
        scratch_shapes=[
            pltpu.VMEM((PACKED, LANES), F32),
            pltpu.VMEM((2, OBS, members), F32),
            pltpu.SemaphoreType.DMA((2,)),
        ],
        compiler_params=params(),
    )(owner, obs_rows, obs_rows, observed, error_var, mean_state.reshape(-1, LANES), gram, ensemble)


def update(packed, ensemble, mean_state):
    rows, members = ensemble.shape
    chunks = 8
    out, mean = pl.pallas_call(
        functools.partial(update_kernel, chunks),
        out_shape=(jax.ShapeDtypeStruct((rows, members), F32), jax.ShapeDtypeStruct((1, rows), F32)),
        in_specs=[spec(pltpu.VMEM)] * 3 + [spec(pltpu.HBM)],
        out_specs=(spec(pltpu.HBM), spec(pltpu.VMEM)),
        scratch_shapes=[
            pltpu.VMEM((PACKED, LANES), F32),
            pltpu.VMEM((rows, members), F32),
            pltpu.VMEM((rows, members), F32),
            pltpu.SemaphoreType.DMA((chunks,)),
            pltpu.SemaphoreType.DMA((chunks,)),
        ],
        compiler_params=params(),
    )(*packed, mean_state.reshape(1, rows), ensemble)
    return out, mean.reshape(rows)


def swap(value, count, mask):
    return lax.ppermute(value, AXIS, [(i, i ^ mask) for i in range(count)])


def total(keep, send, count):
    odd = ((lax.axis_index(AXIS) >> 1) & 1) == 1
    value = keep + swap(send, count, 1)
    low, high = jnp.split(value, 2, axis=0)
    value = jnp.where(odd, high, low) + swap(jnp.where(odd, low, high), count, 2)
    mask = 4
    while mask < count:
        value = value + swap(value, count, mask)
        mask *= 2
    got = swap(value, count, 2)
    value = jnp.concatenate([jnp.where(odd, got, value), jnp.where(odd, value, got)], axis=0)
    return value, swap(value, count, 1)


def on_device(count, ensemble, mean_state, observed, error_var, owner, obs_rows):
    gram = gram_of(ensemble)
    keep, send = gather(ensemble, mean_state, observed, error_var, owner, obs_rows, gram)
    return update(total(keep, send, count), ensemble, mean_state)


def solution(mesh):
    count = mesh.shape[AXIS]
    in_specs = (
        P(("groups", "rows"), None),
        P(("groups", "rows")),
        P("groups", None),
        P("groups", None),
        P("groups"),
        P("groups", None),
    )
    out_specs = (P(("groups", "rows"), None), P(("groups", "rows")))

    def body(*args):
        return on_device(count, *args)

    return jax.shard_map(body, mesh=mesh, in_specs=in_specs, out_specs=out_specs, check_vma=False)
```

```python
import functools

import jax
import jax.numpy as jnp
from jax import lax
from jax.experimental import pallas as pl
from jax.experimental.pallas import tpu as pltpu
from jax.sharding import PartitionSpec as P

RELAX = 0.6
HI = lax.Precision.HIGHEST
AXIS = "rows"
F32 = jnp.float32
BF16 = jnp.bfloat16
LANES = 128
SUB = 8
OBS = 128
VMEM_LIMIT = 51 * 1024 * 1024
STEP = 8

A0, A1, B0, B1, G00, G01, G11 = range(0, 7 * 128, 128)
PACKED = 7 * 128
INNOV = G00 + 64


def dot(a, b, dims=((1,), (0,)), precision=HI):
    return lax.dot_general(a, b, (dims, ((), ())), precision=precision, preferred_element_type=F32)


def column(row):
    return jnp.broadcast_to(row, (LANES, LANES)).T


def split(x):
    high = x.astype(BF16)
    return high, (x - high.astype(F32)).astype(BF16)


def chunk_copy(source, target, sem, chunks):
    size = source.shape[0] // chunks

    def copy(i):
        part = pl.ds(i * size, size)
        return pltpu.make_async_copy(source.at[part], target.at[part], sem.at[i])

    return copy


def gram_kernel(chunks, x_hbm, out, x_buf, sem):
    members = x_buf.shape[1]
    size = x_buf.shape[0] // chunks
    half = members // 2
    copy = chunk_copy(x_hbm, x_buf, sem, chunks)
    for i in range(chunks):
        copy(i).start()
    total = None
    for i in range(chunks):
        copy(i).wait()
        high, low = split(x_buf[i * size : (i + 1) * size, :])
        part = dot(high, jnp.concatenate([high, low], axis=1), ((0,), (0,)), None)
        total = part if total is None else total + part
    cross = total[:, members:]
    total = total[:, :members] + cross + cross.T
    out[:half, :] = total[:half, :half]
    out[half : 2 * half, :] = total[:half, half:]
    out[2 * half :, :] = total[half:, half:]


def gather_kernel(
    owner_s, rows_s, rows_v, observed, error_var, mean_v, gram, x_hbm, keep, send, full, picked, sem
):
    me = lax.axis_index(AXIS)
    members = picked.shape[2]
    half = members // 2

    for k in range(2):

        @pl.when(owner_s[k] == me)
        def _(k=k):
            def fetch(o, _):
                pltpu.make_async_copy(
                    x_hbm.at[pl.ds(rows_s[k, o], 1)], picked.at[k, pl.ds(o, 1)], sem.at[k]
                ).start()
                return 0

            lax.fori_loop(0, OBS, fetch, 0, unroll=8)

    innovations = []
    scales = []
    lane = lax.broadcasted_iota(jnp.int32, (OBS, LANES), 1)
    for k in range(2):
        index = column(rows_v[k : k + 1, :].astype(F32)).astype(jnp.int32)
        prior = jnp.zeros((OBS, LANES), F32)
        for r in range(mean_v.shape[0]):
            prior = prior + jnp.where(index == lane + r * LANES, mean_v[r : r + 1, :], 0.0)
        prior = jnp.sum(prior.T, axis=0, keepdims=True)
        scale = lax.rsqrt(error_var[k : k + 1, :] * (members - 1.0))
        scales.append(column(scale))
        innov = jnp.where(owner_s[k] == me, scale * (observed[k : k + 1, :] - prior), 0.0)
        innovations += [innov[:, : half // 2], innov[:, half // 2 :]]

    full[G00:, :] = gram[...]
    for i, innov in enumerate(innovations):
        full[INNOV + i : INNOV + i + 1, : half // 2] = innov
    full[:G00, :] = jnp.zeros((G00, LANES), F32)
    for k, left, right in ((0, A0, A1), (1, B0, B1)):

        @pl.when(owner_s[k] == me)
        def _(k=k, left=left, right=right):
            pltpu.make_async_copy(x_hbm.at[pl.ds(0, OBS)], picked.at[k], sem.at[k]).wait()
            full[left : left + OBS, :] = picked[k, :, :half] * scales[k]
            full[right : right + OBS, :] = picked[k, :, half:] * scales[k]

    mine = me & 1
    span = PACKED // 2
    keep[...] = full[pl.ds(pl.multiple_of(mine * span, SUB), span), :]
    send[...] = full[pl.ds(pl.multiple_of((1 - mine) * span, SUB), span), :]


def tree(terms):
    while len(terms) > 1:
        terms = [terms[i] + terms[i + 1] if i + 1 < len(terms) else terms[i] for i in range(0, len(terms), 2)]
    return terms[0]


def factor(a):
    count = LANES // SUB
    lane = lax.broadcasted_iota(jnp.int32, (SUB, LANES), 1)
    sub = lax.broadcasted_iota(jnp.int32, (SUB, LANES), 0)
    rows = [a[SUB * i : SUB * (i + 1), :] for i in range(count)]
    out = []

    def spread(x, c):
        return jnp.broadcast_to(x[:, c : c + 1], (SUB, LANES))

    def row(x, j):
        return jnp.broadcast_to(x[j : j + 1, :], (SUB, LANES))

    groups = STEP // SUB
    for s in range(0, count, groups):
        base = SUB * s
        here = (lane >= base) & (lane < base + STEP)
        cols = [[spread(rows[s + g], base + q) for g in range(groups)] for q in range(STEP)]
        work = [
            jnp.where(here, (lane - base == sub + SUB * g).astype(F32), rows[s + g]) for g in range(groups)
        ]
        done = [jnp.zeros((SUB, LANES), F32) for _ in range(groups)]
        for p in range(0, STEP, 2):
            at, j = divmod(p, SUB)
            first, second = sub == j, sub == j + 1
            pair = first | second
            pa, pb, pc = row(cols[p][at], j), row(cols[p][at], j + 1), row(cols[p + 1][at], j + 1)
            det = pa * pc - pb * pb
            inv = pl.reciprocal(det, approx=True)
            top, low = row(work[at], j), row(work[at], j + 1)
            done[at] = jnp.where(first, top * lax.rsqrt(pa), done[at])
            done[at] = jnp.where(second, (pa * low - pb * top) * lax.rsqrt(pa * det), done[at])
            raw, scaled = [], []
            for g in range(groups):
                m0, m1 = cols[p][g], cols[p + 1][g]
                if g == at:
                    m0 = jnp.where(first, -1.0, jnp.where(second, 0.0, m0))
                    m1 = jnp.where(second, -1.0, jnp.where(first, 0.0, m1))
                u0, u1 = m0 * pc - m1 * pb, m1 * pa - m0 * pb
                raw.append((u0, u1))
                scaled.append((u0 * inv, u1 * inv))
            for q in range(p + 2, STEP + 1):
                kept = cols[q] if q < STEP else work
                t, l = row(kept[at], j), row(kept[at], j + 1)
                moved = []
                for g in range(groups):
                    old = jnp.where(pair, 0.0, kept[g]) if g == at else kept[g]
                    if q < p + 4:
                        moved.append(old - (raw[g][0] * t + raw[g][1] * l) * inv)
                    else:
                        moved.append(old - (scaled[g][0] * t + scaled[g][1] * l))
                if q < STEP:
                    cols[q] = moved
                else:
                    work = moved
        for g in range(groups):
            out.append(jnp.where(lane <= base + SUB * g + sub, done[g], 0.0))
        lines = [row(work[p // SUB], p % SUB) for p in range(STEP)]
        later = s + 2 * groups
        for i in range(s + groups, min(later, count)):
            change = tree([spread(rows[i], base + p) * lines[p] for p in range(STEP)])
            rows[i] = jnp.where(here, 0.0, rows[i]) - change
        if later < count:
            rest = jnp.concatenate(rows[later:], axis=0)
            inside = jnp.concatenate([here] * (count - later), axis=0)
            pieces = [jnp.zeros((base, LANES), F32)] if base else []
            pieces += work + [jnp.zeros((LANES - base - STEP, LANES), F32)]
            change = dot(jnp.where(inside, rest, 0.0), jnp.concatenate(pieces, axis=0))
            rest = jnp.where(inside, 0.0, rest) - change
            rows[later:] = [rest[SUB * i : SUB * (i + 1), :] for i in range(count - later)]
    return jnp.concatenate(out, axis=0)


def blend(before, after):
    return 1.0 + RELAX * (jnp.sqrt(before / after) - 1.0)


def add_up(x):
    return jnp.sum(jnp.sum(x, axis=0, keepdims=True), axis=1, keepdims=True)


def dot3(a, b):
    a_high, a_low = split(a)
    b_high, b_low = split(b)
    left = jnp.concatenate([a_high, a_low, a_high], axis=1)
    return dot(left, jnp.concatenate([b_high, b_high, b_low], axis=0), precision=None)


def identity(size):
    return (
        lax.broadcasted_iota(jnp.int32, (size, size), 0) == lax.broadcasted_iota(jnp.int32, (size, size), 1)
    ).astype(F32)


def update_kernel(
    chunks, mine_v, other_v, mean_v, x_hbm, out_hbm, mean_out, full, x_buf, o_buf, in_sem, out_sem
):
    members = x_buf.shape[1]
    size = x_buf.shape[0] // chunks
    load = chunk_copy(x_hbm, x_buf, in_sem, chunks)
    store = chunk_copy(o_buf, out_hbm, out_sem, chunks)
    for i in range(chunks):
        load(i).start()

    mine = lax.axis_index(AXIS) & 1
    span = PACKED // 2
    full[pl.ds(pl.multiple_of(mine * span, SUB), span), :] = mine_v[...]
    full[pl.ds(pl.multiple_of((1 - mine) * span, SUB), span), :] = other_v[...]

    half = members // 2
    quarter = half // 2

    def block(at):
        return full[at : at + half, :]

    def innovation(k):
        at = INNOV + 2 * k
        return jnp.concatenate([full[at : at + 1, :quarter], full[at + 1 : at + 2, :quarter]], axis=1)

    first = jnp.concatenate([block(A0), block(A1)], axis=1)
    second = jnp.concatenate([block(B0), block(B1)], axis=1)
    g00, g01, g11 = block(G00), block(G01), block(G11)
    line = lax.broadcasted_iota(jnp.int32, (half, half), 0)
    lane = lax.broadcasted_iota(jnp.int32, (half, half), 1)
    g00 = jnp.where((line >= quarter) & (lane < quarter), g00.T, g00)
    gram = jnp.concatenate(
        [jnp.concatenate([g00, g01], axis=1), jnp.concatenate([g01.T, g11], axis=1)], axis=0
    )
    eye = identity(half)

    inv_m = factor(eye + dot(first, first, ((1,), (1,))))
    v = dot(inv_m, first)
    before = add_up(eye * (g00 + g11))
    after1 = before - add_up(dot3(v, gram) * v)
    factor1 = blend(before, after1)
    f = jnp.sum(inv_m * innovation(0), axis=1, keepdims=True)
    increment = jnp.sum(v * f, axis=0, keepdims=True)
    innov2 = column(innovation(1))[:, :1] - jnp.sum(second * increment, axis=1, keepdims=True)
    target = jnp.sum(second * innov2, axis=0, keepdims=True) * (factor1 * factor1)

    z = jnp.concatenate([first.T, second.T * factor1], axis=1)
    system = dot(z, z, ((1,), (1,)))
    inv00 = factor(eye + system[:half, :half])
    l10 = dot(system[half:, :half], inv00, ((1,), (1,)))
    inv11 = factor(eye + system[half:, half:] - dot(l10, l10, ((1,), (1,))))
    inv10 = -dot(inv11, dot(l10, inv00))
    y0 = jnp.sum(inv00 * target[:, :half], axis=1, keepdims=True)
    y1 = jnp.sum(inv10 * target[:, :half] + inv11 * target[:, half:], axis=1, keepdims=True)
    increment0 = jnp.sum(y0 * inv00 + y1 * inv10, axis=0, keepdims=True)
    increment1 = jnp.sum(y1 * inv11, axis=0, keepdims=True)
    increment = increment + jnp.concatenate([increment0, increment1], axis=1)
    bottom = jnp.concatenate([inv10, inv11], axis=1)
    after2 = add_up(dot3(inv00, g00) * inv00) + add_up(dot3(bottom, gram) * bottom)
    factor2 = factor1 * blend(after1, after2)

    turned = jnp.concatenate(
        [jnp.concatenate([inv00.T, inv10.T], axis=1), jnp.concatenate([jnp.zeros_like(inv00), inv11.T], axis=1)], axis=0
    )
    high, low = split(turned)
    transform = jnp.concatenate([high, high, low], axis=0)
    step_line = lax.broadcasted_iota(jnp.int32, (LANES, LANES), 0)
    diagonal = step_line == lax.broadcasted_iota(jnp.int32, (LANES, LANES), 1)

    def apply(i, at):
        load(i).wait()
        x = x_buf[pl.ds(at, size), :]
        high, low = split(x)
        moved = dot(jnp.concatenate([high, low, high], axis=1), transform, precision=None)
        o_buf[pl.ds(at, size), :] = moved * factor2
        store(i).start()
        steps = jnp.sum(x * increment, axis=1, keepdims=True)
        for j in range(0, size, LANES):
            step = jnp.sum(jnp.where(diagonal, steps[j : j + LANES, :], 0.0), axis=0, keepdims=True)
            part = pl.ds(at + j, LANES)
            mean_out[:, part] = mean_v[:, part] + step

    apply(0, 0)

    def body(i, _):
        apply(i, pl.multiple_of(i * size, size))
        return 0

    lax.fori_loop(1, chunks, body, 0)
    for i in range(chunks):
        store(i).wait()


def spec(space):
    return pl.BlockSpec(memory_space=space)


def params():
    return pltpu.CompilerParams(vmem_limit_bytes=VMEM_LIMIT)


def cost(flops, bytes_accessed):
    return pl.CostEstimate(flops=flops, bytes_accessed=bytes_accessed, transcendentals=0)


def cost(flops, bytes_accessed):
    return pl.CostEstimate(flops=flops, bytes_accessed=bytes_accessed, transcendentals=0)


def gram_of(ensemble):
    rows, members = ensemble.shape
    chunks = 4
    return pl.pallas_call(
        functools.partial(gram_kernel, chunks),
        out_shape=jax.ShapeDtypeStruct((PACKED - G00, LANES), F32),
        in_specs=[spec(pltpu.HBM)],
        out_specs=spec(pltpu.VMEM),
        scratch_shapes=[pltpu.VMEM((rows, members), F32), pltpu.SemaphoreType.DMA((chunks,))],
        cost_estimate=cost(4 * rows * members * members, 4 * rows * members),
        compiler_params=params(),
    )(ensemble)


def gather(ensemble, mean_state, observed, error_var, owner, obs_rows, gram):
    members = ensemble.shape[1]
    half = jax.ShapeDtypeStruct((PACKED // 2, LANES), F32)
    return pl.pallas_call(
        gather_kernel,
        out_shape=(half, half),
        in_specs=[spec(pltpu.SMEM), spec(pltpu.SMEM)] + [spec(pltpu.VMEM)] * 5 + [spec(pltpu.HBM)],
        out_specs=[spec(pltpu.VMEM)] * 2,
        scratch_shapes=[
            pltpu.VMEM((PACKED, LANES), F32),
            pltpu.VMEM((2, OBS, members), F32),
            pltpu.SemaphoreType.DMA((2,)),
        ],
        compiler_params=params(),
    )(owner, obs_rows, obs_rows, observed, error_var, mean_state.reshape(-1, LANES), gram, ensemble)


def update(packed, ensemble, mean_state):
    rows, members = ensemble.shape
    chunks = 8
    out, mean = pl.pallas_call(
        functools.partial(update_kernel, chunks),
        out_shape=(jax.ShapeDtypeStruct((rows, members), F32), jax.ShapeDtypeStruct((1, rows), F32)),
        in_specs=[spec(pltpu.VMEM)] * 3 + [spec(pltpu.HBM)],
        out_specs=(spec(pltpu.HBM), spec(pltpu.VMEM)),
        scratch_shapes=[
            pltpu.VMEM((PACKED, LANES), F32),
            pltpu.VMEM((rows, members), F32),
            pltpu.VMEM((rows, members), F32),
            pltpu.SemaphoreType.DMA((chunks,)),
            pltpu.SemaphoreType.DMA((chunks,)),
        ],
        compiler_params=params(),
    )(*packed, mean_state.reshape(1, rows), ensemble)
    return out, mean.reshape(rows)


def swap(value, count, mask):
    return lax.ppermute(value, AXIS, [(i, i ^ mask) for i in range(count)])


def total(keep, send, count):
    odd = ((lax.axis_index(AXIS) >> 1) & 1) == 1
    value = keep + swap(send, count, 1)
    low, high = jnp.split(value, 2, axis=0)
    value = jnp.where(odd, high, low) + swap(jnp.where(odd, low, high), count, 2)
    mask = 4
    while mask < count:
        value = value + swap(value, count, mask)
        mask *= 2
    got = swap(value, count, 2)
    value = jnp.concatenate([jnp.where(odd, got, value), jnp.where(odd, value, got)], axis=0)
    return value, swap(value, count, 1)


def on_device(count, ensemble, mean_state, observed, error_var, owner, obs_rows):
    gram = gram_of(ensemble)
    keep, send = gather(ensemble, mean_state, observed, error_var, owner, obs_rows, gram)
    return update(total(keep, send, count), ensemble, mean_state)


def solution(mesh):
    count = mesh.shape[AXIS]
    in_specs = (
        P(("groups", "rows"), None),
        P(("groups", "rows")),
        P("groups", None),
        P("groups", None),
        P("groups"),
        P("groups", None),
    )
    out_specs = (P(("groups", "rows"), None), P(("groups", "rows")))

    def body(*args):
        return on_device(count, *args)

    return jax.shard_map(body, mesh=mesh, in_specs=in_specs, out_specs=out_specs, check_vma=False)
```

```python
import functools

import jax
import jax.numpy as jnp
from jax import lax
from jax.experimental import pallas as pl
from jax.experimental.pallas import tpu as pltpu
from jax.sharding import PartitionSpec as P

RELAX = 0.6
HI = lax.Precision.HIGHEST
AXIS = "rows"
F32 = jnp.float32
BF16 = jnp.bfloat16
LANES = 128
SUB = 8
OBS = 128
VMEM_LIMIT = 51 * 1024 * 1024
STEP = 16

A0, A1, B0, B1, G00, G01, G11 = range(0, 7 * 128, 128)
PACKED = G11 + 64
INNOV = G00 + 96
INNOV_LANES = 32


def dot(a, b, dims=((1,), (0,)), precision=HI):
    return lax.dot_general(a, b, (dims, ((), ())), precision=precision, preferred_element_type=F32)


def column(row):
    return jnp.broadcast_to(row, (LANES, LANES)).T


def split(x):
    high = x.astype(BF16)
    return high, (x - high.astype(F32)).astype(BF16)


def chunk_copy(source, target, sem, chunks):
    size = source.shape[0] // chunks

    def copy(i):
        part = pl.ds(i * size, size)
        return pltpu.make_async_copy(source.at[part], target.at[part], sem.at[i])

    return copy


def gram_kernel(chunks, x_hbm, out, x_buf, sem):
    members = x_buf.shape[1]
    size = x_buf.shape[0] // chunks
    half = members // 2
    copy = chunk_copy(x_hbm, x_buf, sem, chunks)
    for i in range(chunks):
        copy(i).start()
    total = None
    for i in range(chunks):
        copy(i).wait()
        high, low = split(x_buf[i * size : (i + 1) * size, :])
        part = dot(high, jnp.concatenate([high, low], axis=1), ((0,), (0,)), None)
        total = part if total is None else total + part
    cross = total[:, members:]
    total = total[:, :members] + cross + cross.T
    quarter = half // 2
    out[:quarter, :] = total[:quarter, :half]
    out[quarter:half, :] = jnp.concatenate(
        [total[half + quarter :, half + quarter :], total[quarter:half, quarter:half]], axis=1
    )
    out[half : 2 * half, :] = total[:half, half:]
    out[2 * half :, :] = total[half : half + quarter, half:]


def gather_kernel(
    owner_s, rows_s, rows_v, observed, error_var, mean_v, gram, x_hbm, keep, send, full, picked, sem
):
    me = lax.axis_index(AXIS)
    members = picked.shape[2]
    half = members // 2

    for k in range(2):

        @pl.when(owner_s[k] == me)
        def _(k=k):
            def fetch(o, _):
                pltpu.make_async_copy(
                    x_hbm.at[pl.ds(rows_s[k, o], 1)], picked.at[k, pl.ds(o, 1)], sem.at[k]
                ).start()
                return 0

            lax.fori_loop(0, OBS, fetch, 0, unroll=8)

    innovations = []
    scales = []
    lane = lax.broadcasted_iota(jnp.int32, (OBS, LANES), 1)
    for k in range(2):
        index = column(rows_v[k : k + 1, :].astype(F32)).astype(jnp.int32)
        prior = jnp.zeros((OBS, LANES), F32)
        for r in range(mean_v.shape[0]):
            prior = prior + jnp.where(index == lane + r * LANES, mean_v[r : r + 1, :], 0.0)
        prior = jnp.sum(prior.T, axis=0, keepdims=True)
        scale = lax.rsqrt(error_var[k : k + 1, :] * (members - 1.0))
        scales.append(column(scale))
        innov = jnp.where(owner_s[k] == me, scale * (observed[k : k + 1, :] - prior), 0.0)
        innovations += [innov[:, j : j + INNOV_LANES] for j in range(0, OBS, INNOV_LANES)]

    full[G00:, :] = gram[...]
    for i, innov in enumerate(innovations):
        full[INNOV + i : INNOV + i + 1, :INNOV_LANES] = innov
    full[:G00, :] = jnp.zeros((G00, LANES), F32)
    for k, left, right in ((0, A0, A1), (1, B0, B1)):

        @pl.when(owner_s[k] == me)
        def _(k=k, left=left, right=right):
            pltpu.make_async_copy(x_hbm.at[pl.ds(0, OBS)], picked.at[k], sem.at[k]).wait()
            full[left : left + OBS, :] = picked[k, :, :half] * scales[k]
            full[right : right + OBS, :] = picked[k, :, half:] * scales[k]

    mine = me & 1
    span = PACKED // 2
    keep[...] = full[pl.ds(pl.multiple_of(mine * span, SUB), span), :]
    send[...] = full[pl.ds(pl.multiple_of((1 - mine) * span, SUB), span), :]


def tree(terms):
    while len(terms) > 1:
        terms = [terms[i] + terms[i + 1] if i + 1 < len(terms) else terms[i] for i in range(0, len(terms), 2)]
    return terms[0]


def factor(a):
    count = LANES // SUB
    lane = lax.broadcasted_iota(jnp.int32, (SUB, LANES), 1)
    sub = lax.broadcasted_iota(jnp.int32, (SUB, LANES), 0)
    rows = [a[SUB * i : SUB * (i + 1), :] for i in range(count)]
    out = []

    def spread(x, c):
        return jnp.broadcast_to(x[:, c : c + 1], (SUB, LANES))

    def row(x, j):
        return jnp.broadcast_to(x[j : j + 1, :], (SUB, LANES))

    groups = STEP // SUB
    for s in range(0, count, groups):
        base = SUB * s
        here = (lane >= base) & (lane < base + STEP)
        cols = [[spread(rows[s + g], base + q) for g in range(groups)] for q in range(STEP)]
        work = [
            jnp.where(here, (lane - base == sub + SUB * g).astype(F32), rows[s + g]) for g in range(groups)
        ]
        done = [jnp.zeros((SUB, LANES), F32) for _ in range(groups)]
        for p in range(0, STEP, 2):
            at, j = divmod(p, SUB)
            first, second = sub == j, sub == j + 1
            pair = first | second
            pa, pb, pc = row(cols[p][at], j), row(cols[p][at], j + 1), row(cols[p + 1][at], j + 1)
            det = pa * pc - pb * pb
            inv = pl.reciprocal(det, approx=True)
            top, low = row(work[at], j), row(work[at], j + 1)
            done[at] = jnp.where(first, top * lax.rsqrt(pa), done[at])
            done[at] = jnp.where(second, (pa * low - pb * top) * lax.rsqrt(pa * det), done[at])
            raw, scaled = [], []
            for g in range(groups):
                m0, m1 = cols[p][g], cols[p + 1][g]
                if g == at:
                    m0 = jnp.where(first, -1.0, jnp.where(second, 0.0, m0))
                    m1 = jnp.where(second, -1.0, jnp.where(first, 0.0, m1))
                u0, u1 = m0 * pc - m1 * pb, m1 * pa - m0 * pb
                raw.append((u0, u1))
                scaled.append((u0 * inv, u1 * inv))
            for q in range(p + 2, STEP + 1):
                kept = cols[q] if q < STEP else work
                t, l = row(kept[at], j), row(kept[at], j + 1)
                moved = []
                for g in range(groups):
                    old = jnp.where(pair, 0.0, kept[g]) if g == at else kept[g]
                    if q < p + 4:
                        moved.append(old - (raw[g][0] * t + raw[g][1] * l) * inv)
                    else:
                        moved.append(old - (scaled[g][0] * t + scaled[g][1] * l))
                if q < STEP:
                    cols[q] = moved
                else:
                    work = moved
        for g in range(groups):
            out.append(jnp.where(lane <= base + SUB * g + sub, done[g], 0.0))
        lines = [row(work[p // SUB], p % SUB) for p in range(STEP)]
        later = s + 2 * groups
        for i in range(s + groups, min(later, count)):
            change = tree([spread(rows[i], base + p) * lines[p] for p in range(STEP)])
            rows[i] = jnp.where(here, 0.0, rows[i]) - change
        if later < count:
            rest = jnp.concatenate(rows[later:], axis=0)
            inside = jnp.concatenate([here] * (count - later), axis=0)
            pieces = [jnp.zeros((base, LANES), F32)] if base else []
            pieces += work + [jnp.zeros((LANES - base - STEP, LANES), F32)]
            change = dot(jnp.where(inside, rest, 0.0), jnp.concatenate(pieces, axis=0))
            rest = jnp.where(inside, 0.0, rest) - change
            rows[later:] = [rest[SUB * i : SUB * (i + 1), :] for i in range(count - later)]
    return jnp.concatenate(out, axis=0)


def blend(before, after):
    return 1.0 + RELAX * (jnp.sqrt(before / after) - 1.0)


def add_up(x):
    return jnp.sum(jnp.sum(x, axis=0, keepdims=True), axis=1, keepdims=True)


def dot3(a, b):
    a_high, a_low = split(a)
    b_high, b_low = split(b)
    left = jnp.concatenate([a_high, a_low, a_high], axis=1)
    return dot(left, jnp.concatenate([b_high, b_high, b_low], axis=0), precision=None)


def identity(size):
    return (
        lax.broadcasted_iota(jnp.int32, (size, size), 0) == lax.broadcasted_iota(jnp.int32, (size, size), 1)
    ).astype(F32)


def update_kernel(
    chunks, mine_v, other_v, mean_v, x_hbm, out_hbm, mean_out, full, x_buf, o_buf, in_sem, out_sem
):
    members = x_buf.shape[1]
    size = x_buf.shape[0] // chunks
    load = chunk_copy(x_hbm, x_buf, in_sem, chunks)
    store = chunk_copy(o_buf, out_hbm, out_sem, chunks)
    for i in range(chunks):
        load(i).start()

    mine = lax.axis_index(AXIS) & 1
    span = PACKED // 2
    full[pl.ds(pl.multiple_of(mine * span, SUB), span), :] = mine_v[...]
    full[pl.ds(pl.multiple_of((1 - mine) * span, SUB), span), :] = other_v[...]

    half = members // 2
    quarter = half // 2

    def block(at):
        return full[at : at + half, :]

    def innovation(k):
        count = OBS // INNOV_LANES
        at = INNOV + count * k
        return jnp.concatenate([full[at + j : at + j + 1, :INNOV_LANES] for j in range(count)], axis=1)

    first = jnp.concatenate([block(A0), block(A1)], axis=1)
    second = jnp.concatenate([block(B0), block(B1)], axis=1)
    g00, g01, top = block(G00), block(G01), full[G11:, :]
    line = lax.broadcasted_iota(jnp.int32, (half, half), 0)
    lane = lax.broadcasted_iota(jnp.int32, (half, half), 1)
    last = jnp.concatenate([jnp.zeros((quarter, quarter), F32), g00[quarter:, :quarter]], axis=1)
    corner = (line >= quarter) & (lane < quarter)
    g00 = jnp.where(corner, g00.T, g00)
    g11 = jnp.concatenate([top, last], axis=0)
    inner = (line >= INNOV - G00) & (lane >= quarter) & (lane < quarter + INNOV_LANES)
    g11 = jnp.where(corner | inner, g11.T, g11)
    gram = jnp.concatenate(
        [jnp.concatenate([g00, g01], axis=1), jnp.concatenate([g01.T, g11], axis=1)], axis=0
    )
    eye = identity(half)

    inv_m = factor(eye + dot(first, first, ((1,), (1,))))
    v = dot(inv_m, first)
    before = add_up(eye * (g00 + g11))
    after1 = before - add_up(dot3(v, gram) * v)
    factor1 = blend(before, after1)
    f = jnp.sum(inv_m * innovation(0), axis=1, keepdims=True)
    increment = jnp.sum(v * f, axis=0, keepdims=True)
    innov2 = column(innovation(1))[:, :1] - jnp.sum(second * increment, axis=1, keepdims=True)
    target = jnp.sum(second * innov2, axis=0, keepdims=True) * (factor1 * factor1)

    z = jnp.concatenate([first.T, second.T * factor1], axis=1)
    system = dot(z, z, ((1,), (1,)))
    inv00 = factor(eye + system[:half, :half])
    l10 = dot(system[half:, :half], inv00, ((1,), (1,)))
    inv11 = factor(eye + system[half:, half:] - dot(l10, l10, ((1,), (1,))))
    inv10 = -dot(inv11, dot(l10, inv00))
    y0 = jnp.sum(inv00 * target[:, :half], axis=1, keepdims=True)
    y1 = jnp.sum(inv10 * target[:, :half] + inv11 * target[:, half:], axis=1, keepdims=True)
    increment0 = jnp.sum(y0 * inv00 + y1 * inv10, axis=0, keepdims=True)
    increment1 = jnp.sum(y1 * inv11, axis=0, keepdims=True)
    increment = increment + jnp.concatenate([increment0, increment1], axis=1)
    bottom = jnp.concatenate([inv10, inv11], axis=1)
    after2 = add_up(dot3(inv00, g00) * inv00) + add_up(dot3(bottom, gram) * bottom)
    factor2 = factor1 * blend(after1, after2)

    turned = jnp.concatenate(
        [jnp.concatenate([inv00.T, inv10.T], axis=1), jnp.concatenate([jnp.zeros_like(inv00), inv11.T], axis=1)], axis=0
    )
    high, low = split(turned)
    transform = jnp.concatenate([high, high, low], axis=0)
    step_line = lax.broadcasted_iota(jnp.int32, (LANES, LANES), 0)
    diagonal = step_line == lax.broadcasted_iota(jnp.int32, (LANES, LANES), 1)

    def apply(i, at):
        load(i).wait()
        x = x_buf[pl.ds(at, size), :]
        high, low = split(x)
        moved = dot(jnp.concatenate([high, low, high], axis=1), transform, precision=None)
        o_buf[pl.ds(at, size), :] = moved * factor2
        store(i).start()
        steps = jnp.sum(x * increment, axis=1, keepdims=True)
        for j in range(0, size, LANES):
            step = jnp.sum(jnp.where(diagonal, steps[j : j + LANES, :], 0.0), axis=0, keepdims=True)
            part = pl.ds(at + j, LANES)
            mean_out[:, part] = mean_v[:, part] + step

    for i in range(chunks):
        apply(i, i * size)
    for i in range(chunks):
        store(i).wait()


def spec(space):
    return pl.BlockSpec(memory_space=space)


def params():
    return pltpu.CompilerParams(vmem_limit_bytes=VMEM_LIMIT)


def cost(flops, bytes_accessed):
    return pl.CostEstimate(flops=flops, bytes_accessed=bytes_accessed, transcendentals=0)


def cost(flops, bytes_accessed):
    return pl.CostEstimate(flops=flops, bytes_accessed=bytes_accessed, transcendentals=0)


def gram_of(ensemble):
    rows, members = ensemble.shape
    chunks = 8
    return pl.pallas_call(
        functools.partial(gram_kernel, chunks),
        out_shape=jax.ShapeDtypeStruct((PACKED - G00, LANES), F32),
        in_specs=[spec(pltpu.HBM)],
        out_specs=spec(pltpu.VMEM),
        scratch_shapes=[pltpu.VMEM((rows, members), F32), pltpu.SemaphoreType.DMA((chunks,))],
        cost_estimate=cost(4 * rows * members * members, 4 * rows * members),
        compiler_params=params(),
    )(ensemble)


def gather(ensemble, mean_state, observed, error_var, owner, obs_rows, gram):
    members = ensemble.shape[1]
    half = jax.ShapeDtypeStruct((PACKED // 2, LANES), F32)
    return pl.pallas_call(
        gather_kernel,
        out_shape=(half, half),
        in_specs=[spec(pltpu.SMEM), spec(pltpu.SMEM)] + [spec(pltpu.VMEM)] * 5 + [spec(pltpu.HBM)],
        out_specs=[spec(pltpu.VMEM)] * 2,
        scratch_shapes=[
            pltpu.VMEM((PACKED, LANES), F32),
            pltpu.VMEM((2, OBS, members), F32),
            pltpu.SemaphoreType.DMA((2,)),
        ],
        compiler_params=params(),
    )(owner, obs_rows, obs_rows, observed, error_var, mean_state.reshape(-1, LANES), gram, ensemble)


def update(packed, ensemble, mean_state):
    rows, members = ensemble.shape
    chunks = 8
    out, mean = pl.pallas_call(
        functools.partial(update_kernel, chunks),
        out_shape=(jax.ShapeDtypeStruct((rows, members), F32), jax.ShapeDtypeStruct((1, rows), F32)),
        in_specs=[spec(pltpu.VMEM)] * 3 + [spec(pltpu.HBM)],
        out_specs=(spec(pltpu.HBM), spec(pltpu.VMEM)),
        scratch_shapes=[
            pltpu.VMEM((PACKED, LANES), F32),
            pltpu.VMEM((rows, members), F32),
            pltpu.VMEM((rows, members), F32),
            pltpu.SemaphoreType.DMA((chunks,)),
            pltpu.SemaphoreType.DMA((chunks,)),
        ],
        compiler_params=params(),
    )(*packed, mean_state.reshape(1, rows), ensemble)
    return out, mean.reshape(rows)


def swap(value, count, mask):
    return lax.ppermute(value, AXIS, [(i, i ^ mask) for i in range(count)])


def total(keep, send, count):
    odd = ((lax.axis_index(AXIS) >> 1) & 1) == 1
    value = keep + swap(send, count, 1)
    low, high = jnp.split(value, 2, axis=0)
    value = jnp.where(odd, high, low) + swap(jnp.where(odd, low, high), count, 2)
    mask = 4
    while mask < count:
        value = value + swap(value, count, mask)
        mask *= 2
    got = swap(value, count, 2)
    value = jnp.concatenate([jnp.where(odd, got, value), jnp.where(odd, value, got)], axis=0)
    return value, swap(value, count, 1)


def on_device(count, ensemble, mean_state, observed, error_var, owner, obs_rows):
    gram = gram_of(ensemble)
    keep, send = gather(ensemble, mean_state, observed, error_var, owner, obs_rows, gram)
    return update(total(keep, send, count), ensemble, mean_state)


def solution(mesh):
    count = mesh.shape[AXIS]
    in_specs = (
        P(("groups", "rows"), None),
        P(("groups", "rows")),
        P("groups", None),
        P("groups", None),
        P("groups"),
        P("groups", None),
    )
    out_specs = (P(("groups", "rows"), None), P(("groups", "rows")))

    def body(*args):
        return on_device(count, *args)

    return jax.shard_map(body, mesh=mesh, in_specs=in_specs, out_specs=out_specs, check_vma=False)
```

```python
import functools

import jax
import jax.numpy as jnp
from jax import lax
from jax.experimental import pallas as pl
from jax.experimental.pallas import tpu as pltpu
from jax.sharding import PartitionSpec as P

RELAX = 0.6
HI = lax.Precision.HIGHEST
AXIS = "rows"
F32 = jnp.float32
BF16 = jnp.bfloat16
LANES = 128
SUB = 8
OBS = 128
VMEM_LIMIT = 51 * 1024 * 1024
STEP = 16

A0, A1, B0, B1, G00, G01, G11 = range(0, 7 * 128, 128)
PACKED = G11 + 64
INNOV = G00 + 96
INNOV_LANES = 32


def dot(a, b, dims=((1,), (0,)), precision=HI):
    return lax.dot_general(a, b, (dims, ((), ())), precision=precision, preferred_element_type=F32)


def column(row):
    return jnp.broadcast_to(row, (LANES, LANES)).T


def split(x):
    high = x.astype(BF16)
    return high, (x - high.astype(F32)).astype(BF16)


def chunk_copy(source, target, sem, chunks):
    size = source.shape[0] // chunks

    def copy(i):
        part = pl.ds(i * size, size)
        return pltpu.make_async_copy(source.at[part], target.at[part], sem.at[i])

    return copy


def gram_kernel(chunks, x_hbm, out, x_buf, sem):
    members = x_buf.shape[1]
    size = x_buf.shape[0] // chunks
    half = members // 2
    copy = chunk_copy(x_hbm, x_buf, sem, chunks)
    for i in range(chunks):
        copy(i).start()
    total = None
    for i in range(chunks):
        copy(i).wait()
        high, low = split(x_buf[i * size : (i + 1) * size, :])
        part = dot(high, jnp.concatenate([high, low], axis=1), ((0,), (0,)), None)
        total = part if total is None else total + part
    cross = total[:, members:]
    total = total[:, :members] + cross + cross.T
    quarter = half // 2
    out[:quarter, :] = total[:quarter, :half]
    out[quarter:half, :] = jnp.concatenate(
        [total[half + quarter :, half + quarter :], total[quarter:half, quarter:half]], axis=1
    )
    out[half : 2 * half, :] = total[:half, half:]
    out[2 * half :, :] = total[half : half + quarter, half:]


def gather_kernel(
    owner_s, rows_s, rows_v, observed, error_var, mean_v, gram, x_hbm, keep, send, full, picked, sem
):
    me = lax.axis_index(AXIS)
    members = picked.shape[2]
    half = members // 2

    for k in range(2):

        @pl.when(owner_s[k] == me)
        def _(k=k):
            def fetch(o, _):
                pltpu.make_async_copy(
                    x_hbm.at[pl.ds(rows_s[k, o], 1)], picked.at[k, pl.ds(o, 1)], sem.at[k]
                ).start()
                return 0

            lax.fori_loop(0, OBS, fetch, 0, unroll=8)

    innovations = []
    scales = []
    lane = lax.broadcasted_iota(jnp.int32, (OBS, LANES), 1)
    for k in range(2):
        index = column(rows_v[k : k + 1, :].astype(F32)).astype(jnp.int32)
        prior = jnp.zeros((OBS, LANES), F32)
        for r in range(mean_v.shape[0]):
            prior = prior + jnp.where(index == lane + r * LANES, mean_v[r : r + 1, :], 0.0)
        prior = jnp.sum(prior.T, axis=0, keepdims=True)
        scale = lax.rsqrt(error_var[k : k + 1, :] * (members - 1.0))
        scales.append(column(scale))
        innov = jnp.where(owner_s[k] == me, scale * (observed[k : k + 1, :] - prior), 0.0)
        innovations += [innov[:, j : j + INNOV_LANES] for j in range(0, OBS, INNOV_LANES)]

    full[G00:, :] = gram[...]
    for i, innov in enumerate(innovations):
        full[INNOV + i : INNOV + i + 1, :INNOV_LANES] = innov
    full[:G00, :] = jnp.zeros((G00, LANES), F32)
    for k, left, right in ((0, A0, A1), (1, B0, B1)):

        @pl.when(owner_s[k] == me)
        def _(k=k, left=left, right=right):
            pltpu.make_async_copy(x_hbm.at[pl.ds(0, OBS)], picked.at[k], sem.at[k]).wait()
            full[left : left + OBS, :] = picked[k, :, :half] * scales[k]
            full[right : right + OBS, :] = picked[k, :, half:] * scales[k]

    mine = me & 1
    span = PACKED // 2
    keep[...] = full[pl.ds(pl.multiple_of(mine * span, SUB), span), :]
    send[...] = full[pl.ds(pl.multiple_of((1 - mine) * span, SUB), span), :]


def tree(terms):
    while len(terms) > 1:
        terms = [terms[i] + terms[i + 1] if i + 1 < len(terms) else terms[i] for i in range(0, len(terms), 2)]
    return terms[0]


def factor(a):
    count = LANES // SUB
    lane = lax.broadcasted_iota(jnp.int32, (SUB, LANES), 1)
    sub = lax.broadcasted_iota(jnp.int32, (SUB, LANES), 0)
    rows = [a[SUB * i : SUB * (i + 1), :] for i in range(count)]
    out = []

    def spread(x, c):
        return jnp.broadcast_to(x[:, c : c + 1], (SUB, LANES))

    def row(x, j):
        return jnp.broadcast_to(x[j : j + 1, :], (SUB, LANES))

    groups = STEP // SUB
    for s in range(0, count, groups):
        base = SUB * s
        here = (lane >= base) & (lane < base + STEP)
        cols = [[spread(rows[s + g], base + q) for g in range(groups)] for q in range(STEP)]
        work = [
            jnp.where(here, (lane - base == sub + SUB * g).astype(F32), rows[s + g]) for g in range(groups)
        ]
        done = [jnp.zeros((SUB, LANES), F32) for _ in range(groups)]
        for p in range(0, STEP, 2):
            at, j = divmod(p, SUB)
            first, second = sub == j, sub == j + 1
            pair = first | second
            pa, pb, pc = row(cols[p][at], j), row(cols[p][at], j + 1), row(cols[p + 1][at], j + 1)
            det = pa * pc - pb * pb
            inv = pl.reciprocal(det, approx=True)
            top, low = row(work[at], j), row(work[at], j + 1)
            done[at] = jnp.where(first, top * lax.rsqrt(pa), done[at])
            done[at] = jnp.where(second, (pa * low - pb * top) * lax.rsqrt(pa * det), done[at])
            raw, scaled = [], []
            for g in range(groups):
                m0, m1 = cols[p][g], cols[p + 1][g]
                if g == at:
                    m0 = jnp.where(first, -1.0, jnp.where(second, 0.0, m0))
                    m1 = jnp.where(second, -1.0, jnp.where(first, 0.0, m1))
                u0, u1 = m0 * pc - m1 * pb, m1 * pa - m0 * pb
                raw.append((u0, u1))
                scaled.append((u0 * inv, u1 * inv))
            for q in range(p + 2, STEP + 1):
                kept = cols[q] if q < STEP else work
                t, l = row(kept[at], j), row(kept[at], j + 1)
                moved = []
                for g in range(groups):
                    old = jnp.where(pair, 0.0, kept[g]) if g == at else kept[g]
                    if q < p + 4:
                        moved.append(old - (raw[g][0] * t + raw[g][1] * l) * inv)
                    else:
                        moved.append(old - (scaled[g][0] * t + scaled[g][1] * l))
                if q < STEP:
                    cols[q] = moved
                else:
                    work = moved
        for g in range(groups):
            out.append(jnp.where(lane <= base + SUB * g + sub, done[g], 0.0))
        lines = [row(work[p // SUB], p % SUB) for p in range(STEP)]
        later = s + 2 * groups
        for i in range(s + groups, min(later, count)):
            change = tree([spread(rows[i], base + p) * lines[p] for p in range(STEP)])
            rows[i] = jnp.where(here, 0.0, rows[i]) - change
        if later < count:
            rest = jnp.concatenate(rows[later:], axis=0)
            inside = jnp.concatenate([here] * (count - later), axis=0)
            pieces = [jnp.zeros((base, LANES), F32)] if base else []
            pieces += work + [jnp.zeros((LANES - base - STEP, LANES), F32)]
            change = dot(jnp.where(inside, rest, 0.0), jnp.concatenate(pieces, axis=0))
            rest = jnp.where(inside, 0.0, rest) - change
            rows[later:] = [rest[SUB * i : SUB * (i + 1), :] for i in range(count - later)]
    return jnp.concatenate(out, axis=0)


def blend(before, after):
    return 1.0 + RELAX * (jnp.sqrt(before / after) - 1.0)


def add_up(x):
    return jnp.sum(jnp.sum(x, axis=0, keepdims=True), axis=1, keepdims=True)


def dot3(a, b):
    a_high, a_low = split(a)
    b_high, b_low = split(b)
    left = jnp.concatenate([a_high, a_low, a_high], axis=1)
    return dot(left, jnp.concatenate([b_high, b_high, b_low], axis=0), precision=None)


def identity(size):
    return (
        lax.broadcasted_iota(jnp.int32, (size, size), 0) == lax.broadcasted_iota(jnp.int32, (size, size), 1)
    ).astype(F32)


def update_kernel(
    chunks, mine_v, other_v, mean_v, x_hbm, out_hbm, mean_out, full, x_buf, o_buf, in_sem, out_sem
):
    members = x_buf.shape[1]
    size = x_buf.shape[0] // chunks
    load = chunk_copy(x_hbm, x_buf, in_sem, chunks)
    store = chunk_copy(o_buf, out_hbm, out_sem, chunks)
    for i in range(chunks):
        load(i).start()

    mine = lax.axis_index(AXIS) & 1
    span = PACKED // 2
    full[pl.ds(pl.multiple_of(mine * span, SUB), span), :] = mine_v[...]
    full[pl.ds(pl.multiple_of((1 - mine) * span, SUB), span), :] = other_v[...]

    half = members // 2
    quarter = half // 2

    def block(at):
        return full[at : at + half, :]

    def innovation(k):
        count = OBS // INNOV_LANES
        at = INNOV + count * k
        return column(jnp.concatenate([full[at + j : at + j + 1, :INNOV_LANES] for j in range(count)], axis=1))

    first = jnp.concatenate([block(A0), block(A1)], axis=1)
    second = jnp.concatenate([block(B0), block(B1)], axis=1)
    g00, g01, top = block(G00), block(G01), full[G11:, :]
    line = lax.broadcasted_iota(jnp.int32, (half, half), 0)
    lane = lax.broadcasted_iota(jnp.int32, (half, half), 1)
    last = jnp.concatenate([jnp.zeros((quarter, quarter), F32), g00[quarter:, :quarter]], axis=1)
    corner = (line >= quarter) & (lane < quarter)
    g00 = jnp.where(corner, g00.T, g00)
    g11 = jnp.concatenate([top, last], axis=0)
    inner = (line >= INNOV - G00) & (lane >= quarter) & (lane < quarter + INNOV_LANES)
    g11 = jnp.where(corner | inner, g11.T, g11)
    gram = jnp.concatenate(
        [jnp.concatenate([g00, g01], axis=1), jnp.concatenate([g01.T, g11], axis=1)], axis=0
    )
    eye = identity(half)

    inv_m = factor(eye + dot(first, first, ((1,), (1,))))
    v_and_f = dot(inv_m, jnp.concatenate([first, innovation(0)], axis=1))
    v, f = v_and_f[:, :members], v_and_f[:, members:]
    before = add_up(eye * (g00 + g11))
    after1 = before - add_up(dot3(v, gram) * v)
    factor1 = blend(before, after1)
    increment = jnp.sum(v * jnp.concatenate([f, f], axis=1), axis=0, keepdims=True)
    innov2 = innovation(1) - jnp.sum(second * increment, axis=1, keepdims=True)

    a1 = dot(first, first, ((0,), (0,)))
    a2 = dot(second, jnp.concatenate([second, innov2], axis=1), ((0,), (0,)))
    square = factor1 * factor1
    k00 = eye + a1[:half, :half] + a2[:half, :half] * square
    k01 = a1[:half, half:] + a2[:half, half:members] * square
    k11 = eye + a1[half:, half:] + a2[half:, half:members] * square
    inv00 = factor(k00)
    u = dot(inv00, k01)
    inv11 = factor(k11 - dot(u, u, ((0,), (0,))))
    inv10 = -dot(inv11, dot(u, inv00, ((0,), (0,))))
    y0 = dot(inv00, a2[:half, members:] * square)
    y1 = dot(inv11, a2[half:, members:] * square - dot(u, y0, ((0,), (0,))))
    bottom = jnp.concatenate([inv10, inv11], axis=1)
    top_trace = add_up(dot3(inv00, g00) * inv00)
    after2 = top_trace + add_up(dot3(bottom, gram) * bottom)
    factor2 = factor1 * blend(after1, after2)
    increment0 = jnp.sum(y0 * inv00 + y1 * inv10, axis=0, keepdims=True)
    increment1 = jnp.sum(y1 * inv11, axis=0, keepdims=True)
    increment = increment + jnp.concatenate([increment0, increment1], axis=1)

    turned = jnp.concatenate(
        [jnp.concatenate([inv00.T, inv10.T], axis=1), jnp.concatenate([jnp.zeros_like(inv00), inv11.T], axis=1)], axis=0
    )
    high, low = split(turned)
    transform = jnp.concatenate([high, high, low], axis=0)
    step_line = lax.broadcasted_iota(jnp.int32, (LANES, LANES), 0)
    diagonal = step_line == lax.broadcasted_iota(jnp.int32, (LANES, LANES), 1)

    def apply(i, at):
        load(i).wait()
        x = x_buf[pl.ds(at, size), :]
        high, low = split(x)
        moved = dot(jnp.concatenate([high, low, high], axis=1), transform, precision=None)
        o_buf[pl.ds(at, size), :] = moved * factor2
        store(i).start()
        steps = jnp.sum(x * increment, axis=1, keepdims=True)
        for j in range(0, size, LANES):
            step = jnp.sum(jnp.where(diagonal, steps[j : j + LANES, :], 0.0), axis=0, keepdims=True)
            part = pl.ds(at + j, LANES)
            mean_out[:, part] = mean_v[:, part] + step

    apply(0, 0)

    def body(i, _):
        apply(i, pl.multiple_of(i * size, size))
        return 0

    lax.fori_loop(1, chunks, body, 0)
    for i in range(chunks):
        store(i).wait()


def spec(space):
    return pl.BlockSpec(memory_space=space)


def params():
    return pltpu.CompilerParams(vmem_limit_bytes=VMEM_LIMIT)


def cost(flops, bytes_accessed):
    return pl.CostEstimate(flops=flops, bytes_accessed=bytes_accessed, transcendentals=0)


def cost(flops, bytes_accessed):
    return pl.CostEstimate(flops=flops, bytes_accessed=bytes_accessed, transcendentals=0)


def gram_of(ensemble):
    rows, members = ensemble.shape
    chunks = 4
    return pl.pallas_call(
        functools.partial(gram_kernel, chunks),
        out_shape=jax.ShapeDtypeStruct((PACKED - G00, LANES), F32),
        in_specs=[spec(pltpu.HBM)],
        out_specs=spec(pltpu.VMEM),
        scratch_shapes=[pltpu.VMEM((rows, members), F32), pltpu.SemaphoreType.DMA((chunks,))],
        cost_estimate=cost(4 * rows * members * members, 4 * rows * members),
        compiler_params=params(),
    )(ensemble)


def gather(ensemble, mean_state, observed, error_var, owner, obs_rows, gram):
    members = ensemble.shape[1]
    half = jax.ShapeDtypeStruct((PACKED // 2, LANES), F32)
    return pl.pallas_call(
        gather_kernel,
        out_shape=(half, half),
        in_specs=[spec(pltpu.SMEM), spec(pltpu.SMEM)] + [spec(pltpu.VMEM)] * 5 + [spec(pltpu.HBM)],
        out_specs=[spec(pltpu.VMEM)] * 2,
        scratch_shapes=[
            pltpu.VMEM((PACKED, LANES), F32),
            pltpu.VMEM((2, OBS, members), F32),
            pltpu.SemaphoreType.DMA((2,)),
        ],
        compiler_params=params(),
    )(owner, obs_rows, obs_rows, observed, error_var, mean_state.reshape(-1, LANES), gram, ensemble)


def update(packed, ensemble, mean_state):
    rows, members = ensemble.shape
    chunks = 8
    out, mean = pl.pallas_call(
        functools.partial(update_kernel, chunks),
        out_shape=(jax.ShapeDtypeStruct((rows, members), F32), jax.ShapeDtypeStruct((1, rows), F32)),
        in_specs=[spec(pltpu.VMEM)] * 3 + [spec(pltpu.HBM)],
        out_specs=(spec(pltpu.HBM), spec(pltpu.VMEM)),
        scratch_shapes=[
            pltpu.VMEM((PACKED, LANES), F32),
            pltpu.VMEM((rows, members), F32),
            pltpu.VMEM((rows, members), F32),
            pltpu.SemaphoreType.DMA((chunks,)),
            pltpu.SemaphoreType.DMA((chunks,)),
        ],
        compiler_params=params(),
    )(*packed, mean_state.reshape(1, rows), ensemble)
    return out, mean.reshape(rows)


def swap(value, count, mask):
    return lax.ppermute(value, AXIS, [(i, i ^ mask) for i in range(count)])


def total(keep, send, count):
    odd = ((lax.axis_index(AXIS) >> 1) & 1) == 1
    value = keep + swap(send, count, 1)
    low, high = jnp.split(value, 2, axis=0)
    value = jnp.where(odd, high, low) + swap(jnp.where(odd, low, high), count, 2)
    mask = 4
    while mask < count:
        value = value + swap(value, count, mask)
        mask *= 2
    got = swap(value, count, 2)
    value = jnp.concatenate([jnp.where(odd, got, value), jnp.where(odd, value, got)], axis=0)
    return value, swap(value, count, 1)


def on_device(count, ensemble, mean_state, observed, error_var, owner, obs_rows):
    gram = gram_of(ensemble)
    keep, send = gather(ensemble, mean_state, observed, error_var, owner, obs_rows, gram)
    return update(total(keep, send, count), ensemble, mean_state)


def solution(mesh):
    count = mesh.shape[AXIS]
    in_specs = (
        P(("groups", "rows"), None),
        P(("groups", "rows")),
        P("groups", None),
        P("groups", None),
        P("groups"),
        P("groups", None),
    )
    out_specs = (P(("groups", "rows"), None), P(("groups", "rows")))

    def body(*args):
        return on_device(count, *args)

    return jax.shard_map(body, mesh=mesh, in_specs=in_specs, out_specs=out_specs, check_vma=False)
```

```python
import functools

import jax
import jax.numpy as jnp
from jax import lax
from jax.experimental import pallas as pl
from jax.experimental.pallas import tpu as pltpu
from jax.sharding import PartitionSpec as P

RELAX = 0.6
HI = lax.Precision.HIGHEST
AXIS = "rows"
F32 = jnp.float32
BF16 = jnp.bfloat16
LANES = 128
SUB = 8
OBS = 128
VMEM_LIMIT = 51 * 1024 * 1024
STEP = 16

A0, A1, B0, B1, G00, G01, G11 = range(0, 7 * 128, 128)
PACKED = G11 + 64
INNOV = G00 + 96
INNOV_LANES = 32
EVEN_ROWS = 256


def dot(a, b, dims=((1,), (0,)), precision=HI):
    return lax.dot_general(a, b, (dims, ((), ())), precision=precision, preferred_element_type=F32)


def column(row):
    return jnp.broadcast_to(row, (LANES, LANES)).T


def split(x):
    high = x.astype(BF16)
    return high, (x - high.astype(F32)).astype(BF16)


def chunk_copy(source, target, sem, chunks):
    size = source.shape[0] // chunks

    def copy(i):
        part = pl.ds(i * size, size)
        return pltpu.make_async_copy(source.at[part], target.at[part], sem.at[i])

    return copy


def gram_kernel(chunks, x_hbm, out, x_buf, sem):
    members = x_buf.shape[1]
    size = x_buf.shape[0] // chunks
    half = members // 2
    copy = chunk_copy(x_hbm, x_buf, sem, chunks)
    for i in range(chunks):
        copy(i).start()
    total = None
    for i in range(chunks):
        copy(i).wait()
        high, low = split(x_buf[i * size : (i + 1) * size, :])
        part = dot(high, jnp.concatenate([high, low], axis=1), ((0,), (0,)), None)
        total = part if total is None else total + part
    cross = total[:, members:]
    total = total[:, :members] + cross + cross.T
    quarter = half // 2
    out[:quarter, :] = total[:quarter, :half]
    out[quarter:half, :] = jnp.concatenate(
        [total[half + quarter :, half + quarter :], total[quarter:half, quarter:half]], axis=1
    )
    out[half : 2 * half, :] = total[:half, half:]
    out[2 * half :, :] = total[half : half + quarter, half:]


def gather_kernel(
    owner_s, rows_s, rows_v, observed, error_var, mean_v, gram, x_hbm, even, odd, full, picked, sem
):
    me = lax.axis_index(AXIS)
    members = picked.shape[2]
    half = members // 2

    for k in range(2):

        @pl.when(owner_s[k] == me)
        def _(k=k):
            def fetch(o, _):
                pltpu.make_async_copy(
                    x_hbm.at[pl.ds(rows_s[k, o], 1)], picked.at[k, pl.ds(o, 1)], sem.at[k]
                ).start()
                return 0

            lax.fori_loop(0, OBS, fetch, 0, unroll=8)

    innovations = []
    scales = []
    lane = lax.broadcasted_iota(jnp.int32, (OBS, LANES), 1)
    for k in range(2):
        index = column(rows_v[k : k + 1, :].astype(F32)).astype(jnp.int32)
        prior = jnp.zeros((OBS, LANES), F32)
        for r in range(mean_v.shape[0]):
            prior = prior + jnp.where(index == lane + r * LANES, mean_v[r : r + 1, :], 0.0)
        prior = jnp.sum(prior.T, axis=0, keepdims=True)
        scale = lax.rsqrt(error_var[k : k + 1, :] * (members - 1.0))
        scales.append(column(scale))
        innov = jnp.where(owner_s[k] == me, scale * (observed[k : k + 1, :] - prior), 0.0)
        innovations += [innov[:, j : j + INNOV_LANES] for j in range(0, OBS, INNOV_LANES)]

    full[G00:, :] = gram[...]
    for i, innov in enumerate(innovations):
        full[INNOV + i : INNOV + i + 1, :INNOV_LANES] = innov
    full[:G00, :] = jnp.zeros((G00, LANES), F32)
    for k, left, right in ((0, A0, A1), (1, B0, B1)):

        @pl.when(owner_s[k] == me)
        def _(k=k, left=left, right=right):
            pltpu.make_async_copy(x_hbm.at[pl.ds(0, OBS)], picked.at[k], sem.at[k]).wait()
            full[left : left + OBS, :] = picked[k, :, :half] * scales[k]
            full[right : right + OBS, :] = picked[k, :, half:] * scales[k]

    even[...] = full[:EVEN_ROWS, :]
    odd[...] = full[EVEN_ROWS:, :]


def tree(terms):
    while len(terms) > 1:
        terms = [terms[i] + terms[i + 1] if i + 1 < len(terms) else terms[i] for i in range(0, len(terms), 2)]
    return terms[0]


def factor(a):
    count = LANES // SUB
    lane = lax.broadcasted_iota(jnp.int32, (SUB, LANES), 1)
    sub = lax.broadcasted_iota(jnp.int32, (SUB, LANES), 0)
    rows = [a[SUB * i : SUB * (i + 1), :] for i in range(count)]
    out = []

    def spread(x, c):
        return jnp.broadcast_to(x[:, c : c + 1], (SUB, LANES))

    def row(x, j):
        return jnp.broadcast_to(x[j : j + 1, :], (SUB, LANES))

    groups = STEP // SUB
    for s in range(0, count, groups):
        base = SUB * s
        here = (lane >= base) & (lane < base + STEP)
        cols = [[spread(rows[s + g], base + q) for g in range(groups)] for q in range(STEP)]
        work = [
            jnp.where(here, (lane - base == sub + SUB * g).astype(F32), rows[s + g]) for g in range(groups)
        ]
        done = [jnp.zeros((SUB, LANES), F32) for _ in range(groups)]
        for p in range(0, STEP, 2):
            at, j = divmod(p, SUB)
            first, second = sub == j, sub == j + 1
            pair = first | second
            pa, pb, pc = row(cols[p][at], j), row(cols[p][at], j + 1), row(cols[p + 1][at], j + 1)
            det = pa * pc - pb * pb
            inv = pl.reciprocal(det, approx=True)
            top, low = row(work[at], j), row(work[at], j + 1)
            done[at] = jnp.where(first, top * lax.rsqrt(pa), done[at])
            done[at] = jnp.where(second, (pa * low - pb * top) * lax.rsqrt(pa * det), done[at])
            raw, scaled = [], []
            for g in range(groups):
                m0, m1 = cols[p][g], cols[p + 1][g]
                if g == at:
                    m0 = jnp.where(first, -1.0, jnp.where(second, 0.0, m0))
                    m1 = jnp.where(second, -1.0, jnp.where(first, 0.0, m1))
                u0, u1 = m0 * pc - m1 * pb, m1 * pa - m0 * pb
                raw.append((u0, u1))
                scaled.append((u0 * inv, u1 * inv))
            for q in range(p + 2, STEP + 1):
                kept = cols[q] if q < STEP else work
                t, l = row(kept[at], j), row(kept[at], j + 1)
                moved = []
                for g in range(groups):
                    old = jnp.where(pair, 0.0, kept[g]) if g == at else kept[g]
                    if q < p + 4:
                        moved.append(old - (raw[g][0] * t + raw[g][1] * l) * inv)
                    else:
                        moved.append(old - (scaled[g][0] * t + scaled[g][1] * l))
                if q < STEP:
                    cols[q] = moved
                else:
                    work = moved
        for g in range(groups):
            out.append(jnp.where(lane <= base + SUB * g + sub, done[g], 0.0))
        lines = [row(work[p // SUB], p % SUB) for p in range(STEP)]
        later = s + 2 * groups
        for i in range(s + groups, min(later, count)):
            change = tree([spread(rows[i], base + p) * lines[p] for p in range(STEP)])
            rows[i] = jnp.where(here, 0.0, rows[i]) - change
        if later < count:
            rest = jnp.concatenate(rows[later:], axis=0)
            inside = jnp.concatenate([here] * (count - later), axis=0)
            pieces = [jnp.zeros((base, LANES), F32)] if base else []
            pieces += work + [jnp.zeros((LANES - base - STEP, LANES), F32)]
            change = dot(jnp.where(inside, rest, 0.0), jnp.concatenate(pieces, axis=0))
            rest = jnp.where(inside, 0.0, rest) - change
            rows[later:] = [rest[SUB * i : SUB * (i + 1), :] for i in range(count - later)]
    return jnp.concatenate(out, axis=0)


def blend(before, after):
    return 1.0 + RELAX * (jnp.sqrt(before / after) - 1.0)


def add_up(x):
    return jnp.sum(jnp.sum(x, axis=0, keepdims=True), axis=1, keepdims=True)


def dot3(a, b):
    a_high, a_low = split(a)
    b_high, b_low = split(b)
    left = jnp.concatenate([a_high, a_low, a_high], axis=1)
    return dot(left, jnp.concatenate([b_high, b_high, b_low], axis=0), precision=None)


def identity(size):
    return (
        lax.broadcasted_iota(jnp.int32, (size, size), 0) == lax.broadcasted_iota(jnp.int32, (size, size), 1)
    ).astype(F32)


def update_kernel(
    chunks, even_mine, even_got, odd_mine, odd_got, mean_v, x_hbm, out_hbm, mean_out, full, x_buf, o_buf, in_sem, out_sem
):
    members = x_buf.shape[1]
    size = x_buf.shape[0] // chunks
    load = chunk_copy(x_hbm, x_buf, in_sem, chunks)
    store = chunk_copy(o_buf, out_hbm, out_sem, chunks)
    for i in range(chunks):
        load(i).start()

    is_odd = (lax.axis_index(AXIS) & 1) == 1
    full[:EVEN_ROWS, :] = jnp.where(is_odd, even_got[...], even_mine[...])
    full[EVEN_ROWS:, :] = jnp.where(is_odd, odd_mine[...], odd_got[...])

    half = members // 2
    quarter = half // 2

    def block(at):
        return full[at : at + half, :]

    def innovation(k):
        count = OBS // INNOV_LANES
        at = INNOV + count * k
        return column(jnp.concatenate([full[at + j : at + j + 1, :INNOV_LANES] for j in range(count)], axis=1))

    first = jnp.concatenate([block(A0), block(A1)], axis=1)
    second = jnp.concatenate([block(B0), block(B1)], axis=1)
    g00, g01, top = block(G00), block(G01), full[G11:, :]
    line = lax.broadcasted_iota(jnp.int32, (half, half), 0)
    lane = lax.broadcasted_iota(jnp.int32, (half, half), 1)
    last = jnp.concatenate([jnp.zeros((quarter, quarter), F32), g00[quarter:, :quarter]], axis=1)
    corner = (line >= quarter) & (lane < quarter)
    g00 = jnp.where(corner, g00.T, g00)
    g11 = jnp.concatenate([top, last], axis=0)
    inner = (line >= INNOV - G00) & (lane >= quarter) & (lane < quarter + INNOV_LANES)
    g11 = jnp.where(corner | inner, g11.T, g11)
    gram = jnp.concatenate(
        [jnp.concatenate([g00, g01], axis=1), jnp.concatenate([g01.T, g11], axis=1)], axis=0
    )
    eye = identity(half)

    inv_m = factor(eye + dot(first, first, ((1,), (1,))))
    v_and_f = dot(inv_m, jnp.concatenate([first, innovation(0)], axis=1))
    v, f = v_and_f[:, :members], v_and_f[:, members:]
    before = add_up(eye * (g00 + g11))
    after1 = before - add_up(dot3(v, gram) * v)
    factor1 = blend(before, after1)
    increment = jnp.sum(v * jnp.concatenate([f, f], axis=1), axis=0, keepdims=True)
    innov2 = innovation(1) - jnp.sum(second * increment, axis=1, keepdims=True)

    a1 = dot(first, first, ((0,), (0,)))
    a2 = dot(second, jnp.concatenate([second, innov2], axis=1), ((0,), (0,)))
    square = factor1 * factor1
    k00 = eye + a1[:half, :half] + a2[:half, :half] * square
    k01 = a1[:half, half:] + a2[:half, half:members] * square
    k11 = eye + a1[half:, half:] + a2[half:, half:members] * square
    inv00 = factor(k00)
    u = dot(inv00, k01)
    inv11 = factor(k11 - dot(u, u, ((0,), (0,))))
    inv10 = -dot(inv11, dot(u, inv00, ((0,), (0,))))
    y0 = dot(inv00, a2[:half, members:] * square)
    y1 = dot(inv11, a2[half:, members:] * square - dot(u, y0, ((0,), (0,))))
    bottom = jnp.concatenate([inv10, inv11], axis=1)
    top_trace = add_up(dot3(inv00, g00) * inv00)
    after2 = top_trace + add_up(dot3(bottom, gram) * bottom)
    factor2 = factor1 * blend(after1, after2)
    increment0 = jnp.sum(y0 * inv00 + y1 * inv10, axis=0, keepdims=True)
    increment1 = jnp.sum(y1 * inv11, axis=0, keepdims=True)
    increment = increment + jnp.concatenate([increment0, increment1], axis=1)

    turned = jnp.concatenate(
        [jnp.concatenate([inv00.T, inv10.T], axis=1), jnp.concatenate([jnp.zeros_like(inv00), inv11.T], axis=1)], axis=0
    )
    high, low = split(turned)
    transform = jnp.concatenate([high, high, low], axis=0)
    step_line = lax.broadcasted_iota(jnp.int32, (LANES, LANES), 0)
    diagonal = step_line == lax.broadcasted_iota(jnp.int32, (LANES, LANES), 1)

    def apply(i, at):
        load(i).wait()
        x = x_buf[pl.ds(at, size), :]
        high, low = split(x)
        moved = dot(jnp.concatenate([high, low, high], axis=1), transform, precision=None)
        o_buf[pl.ds(at, size), :] = moved * factor2
        store(i).start()
        steps = jnp.sum(x * increment, axis=1, keepdims=True)
        for j in range(0, size, LANES):
            step = jnp.sum(jnp.where(diagonal, steps[j : j + LANES, :], 0.0), axis=0, keepdims=True)
            part = pl.ds(at + j, LANES)
            mean_out[:, part] = mean_v[:, part] + step

    apply(0, 0)

    def body(i, _):
        apply(i, pl.multiple_of(i * size, size))
        return 0

    lax.fori_loop(1, chunks, body, 0)
    for i in range(chunks):
        store(i).wait()


def spec(space):
    return pl.BlockSpec(memory_space=space)


def params():
    return pltpu.CompilerParams(vmem_limit_bytes=VMEM_LIMIT)


def cost(flops, bytes_accessed):
    return pl.CostEstimate(flops=flops, bytes_accessed=bytes_accessed, transcendentals=0)


def cost(flops, bytes_accessed):
    return pl.CostEstimate(flops=flops, bytes_accessed=bytes_accessed, transcendentals=0)


def gram_of(ensemble):
    rows, members = ensemble.shape
    chunks = 4
    return pl.pallas_call(
        functools.partial(gram_kernel, chunks),
        out_shape=jax.ShapeDtypeStruct((PACKED - G00, LANES), F32),
        in_specs=[spec(pltpu.HBM)],
        out_specs=spec(pltpu.VMEM),
        scratch_shapes=[pltpu.VMEM((rows, members), F32), pltpu.SemaphoreType.DMA((chunks,))],
        cost_estimate=cost(4 * rows * members * members, 4 * rows * members),
        compiler_params=params(),
    )(ensemble)


def gather(ensemble, mean_state, observed, error_var, owner, obs_rows, gram):
    members = ensemble.shape[1]
    return pl.pallas_call(
        gather_kernel,
        out_shape=(
            jax.ShapeDtypeStruct((EVEN_ROWS, LANES), F32),
            jax.ShapeDtypeStruct((PACKED - EVEN_ROWS, LANES), F32),
        ),
        in_specs=[spec(pltpu.SMEM), spec(pltpu.SMEM)] + [spec(pltpu.VMEM)] * 5 + [spec(pltpu.HBM)],
        out_specs=[spec(pltpu.VMEM)] * 2,
        scratch_shapes=[
            pltpu.VMEM((PACKED, LANES), F32),
            pltpu.VMEM((2, OBS, members), F32),
            pltpu.SemaphoreType.DMA((2,)),
        ],
        compiler_params=params(),
    )(owner, obs_rows, obs_rows, observed, error_var, mean_state.reshape(-1, LANES), gram, ensemble)


def update(packed, ensemble, mean_state):
    rows, members = ensemble.shape
    chunks = 8
    out, mean = pl.pallas_call(
        functools.partial(update_kernel, chunks),
        out_shape=(jax.ShapeDtypeStruct((rows, members), F32), jax.ShapeDtypeStruct((1, rows), F32)),
        in_specs=[spec(pltpu.VMEM)] * 5 + [spec(pltpu.HBM)],
        out_specs=(spec(pltpu.HBM), spec(pltpu.VMEM)),
        scratch_shapes=[
            pltpu.VMEM((PACKED, LANES), F32),
            pltpu.VMEM((rows, members), F32),
            pltpu.VMEM((rows, members), F32),
            pltpu.SemaphoreType.DMA((chunks,)),
            pltpu.SemaphoreType.DMA((chunks,)),
        ],
        compiler_params=params(),
    )(*packed, mean_state.reshape(1, rows), ensemble)
    return out, mean.reshape(rows)


def swap(value, senders, mask):
    return lax.ppermute(value, AXIS, [(i, i ^ mask) for i in senders])


def total(value, count, core):
    mine = range(core, count, 2)
    upper = ((lax.axis_index(AXIS) >> 1) & 1) == 1
    low, high = jnp.split(value, 2, axis=0)
    value = jnp.where(upper, high, low) + swap(jnp.where(upper, low, high), mine, 2)
    mask = 4
    while mask < count:
        value = value + swap(value, mine, mask)
        mask *= 2
    got = swap(value, mine, 2)
    value = jnp.concatenate([jnp.where(upper, got, value), jnp.where(upper, value, got)], axis=0)
    return value, swap(value, mine, 1)


def on_device(count, ensemble, mean_state, observed, error_var, owner, obs_rows):
    gram = gram_of(ensemble)
    even, odd = gather(ensemble, mean_state, observed, error_var, owner, obs_rows, gram)
    even_got, odd_got = swap(even, range(1, count, 2), 1), swap(odd, range(0, count, 2), 1)
    even_got, odd_got = lax.optimization_barrier((even_got, odd_got))
    return update(total(even + even_got, count, 0) + total(odd + odd_got, count, 1), ensemble, mean_state)


def solution(mesh):
    count = mesh.shape[AXIS]
    in_specs = (
        P(("groups", "rows"), None),
        P(("groups", "rows")),
        P("groups", None),
        P("groups", None),
        P("groups"),
        P("groups", None),
    )
    out_specs = (P(("groups", "rows"), None), P(("groups", "rows")))

    def body(*args):
        return on_device(count, *args)

    return jax.shard_map(body, mesh=mesh, in_specs=in_specs, out_specs=out_specs, check_vma=False)
```

```python
import functools

import jax
import jax.numpy as jnp
from jax import lax
from jax.experimental import pallas as pl
from jax.experimental.pallas import tpu as pltpu
from jax.sharding import PartitionSpec as P

RELAX = 0.6
HI = lax.Precision.HIGHEST
AXIS = "rows"
F32 = jnp.float32
BF16 = jnp.bfloat16
LANES = 128
SUB = 8
OBS = 128
VMEM_LIMIT = 51 * 1024 * 1024
STEP = 16
SCALE = 2.0**-16

A0, A1, B0, B1, G00, G01, G11 = range(0, 7 * 128, 128)
PACKED = G11 + 64
INNOV = G00 + 96
INNOV_LANES = 32


def dot(a, b, dims=((1,), (0,)), precision=HI):
    return lax.dot_general(a, b, (dims, ((), ())), precision=precision, preferred_element_type=F32)


def column(row):
    return jnp.broadcast_to(row, (LANES, LANES)).T


def split(x):
    high = x.astype(BF16)
    return high, (x - high.astype(F32)).astype(BF16)


def chunk_copy(source, target, sem, chunks):
    size = source.shape[0] // chunks

    def copy(i):
        part = pl.ds(i * size, size)
        return pltpu.make_async_copy(source.at[part], target.at[part], sem.at[i])

    return copy


def gram_kernel(chunks, x_hbm, out, x_buf, sem):
    members = x_buf.shape[1]
    size = x_buf.shape[0] // chunks
    half = members // 2
    copy = chunk_copy(x_hbm, x_buf, sem, chunks)
    for i in range(chunks):
        copy(i).start()
    total = None
    for i in range(chunks):
        copy(i).wait()
        high, low = split(x_buf[i * size : (i + 1) * size, :])
        part = dot(high, jnp.concatenate([high, low], axis=1), ((0,), (0,)), None)
        total = part if total is None else total + part
    cross = total[:, members:]
    total = total[:, :members] + cross + cross.T
    quarter = half // 2
    out[:quarter, :] = total[:quarter, :half]
    out[quarter:half, :] = jnp.concatenate(
        [total[half + quarter :, half + quarter :], total[quarter:half, quarter:half]], axis=1
    )
    out[half : 2 * half, :] = total[:half, half:]
    out[2 * half :, :] = total[half : half + quarter, half:]


def gather_kernel(
    owner_s, rows_s, rows_v, observed, error_var, mean_v, gram, x_hbm, keep, send, full, picked, sem
):
    me = lax.axis_index(AXIS)
    members = picked.shape[2]
    half = members // 2

    for k in range(2):

        @pl.when(owner_s[k] == me)
        def _(k=k):
            def fetch(o, _):
                pltpu.make_async_copy(
                    x_hbm.at[pl.ds(rows_s[k, o], 1)], picked.at[k, pl.ds(o, 1)], sem.at[k]
                ).start()
                return 0

            lax.fori_loop(0, OBS, fetch, 0, unroll=32)

    innovations = []
    scales = []
    lane = lax.broadcasted_iota(jnp.int32, (OBS, LANES), 1)
    for k in range(2):
        index = column(rows_v[k : k + 1, :].astype(F32)).astype(jnp.int32)
        prior = jnp.zeros((OBS, LANES), F32)
        for r in range(mean_v.shape[0]):
            prior = prior + jnp.where(index == lane + r * LANES, mean_v[r : r + 1, :], 0.0)
        prior = jnp.sum(prior.T, axis=0, keepdims=True)
        scale = lax.rsqrt(error_var[k : k + 1, :] * (members - 1.0))
        scales.append(column(scale))
        innov = jnp.where(owner_s[k] == me, scale * (observed[k : k + 1, :] - prior), 0.0)
        innovations += [innov[:, j : j + INNOV_LANES] for j in range(0, OBS, INNOV_LANES)]

    full[G00:, :] = gram[...]
    for i, innov in enumerate(innovations):
        full[INNOV + i : INNOV + i + 1, :INNOV_LANES] = innov
    full[:G00, :] = jnp.zeros((G00, LANES), F32)
    for k, left, right in ((0, A0, A1), (1, B0, B1)):

        @pl.when(owner_s[k] == me)
        def _(k=k, left=left, right=right):
            pltpu.make_async_copy(x_hbm.at[pl.ds(0, OBS)], picked.at[k], sem.at[k]).wait()
            full[left : left + OBS, :] = picked[k, :, :half] * scales[k]
            full[right : right + OBS, :] = picked[k, :, half:] * scales[k]

    mine = me & 1
    span = PACKED // 2
    keep[...] = full[pl.ds(pl.multiple_of(mine * span, SUB), span), :]
    send[...] = full[pl.ds(pl.multiple_of((1 - mine) * span, SUB), span), :]


def tree(terms):
    while len(terms) > 1:
        terms = [terms[i] + terms[i + 1] if i + 1 < len(terms) else terms[i] for i in range(0, len(terms), 2)]
    return terms[0]


def factor(a):
    a = a * SCALE
    count = LANES // SUB
    lane = lax.broadcasted_iota(jnp.int32, (SUB, LANES), 1)
    sub = lax.broadcasted_iota(jnp.int32, (SUB, LANES), 0)
    rows = [a[SUB * i : SUB * (i + 1), :] for i in range(count)]
    out = []

    def spread(x, c):
        return jnp.broadcast_to(x[:, c : c + 1], (SUB, LANES))

    def row(x, j):
        return jnp.broadcast_to(x[j : j + 1, :], (SUB, LANES))

    groups = STEP // SUB
    for s in range(0, count, groups):
        base = SUB * s
        here = (lane >= base) & (lane < base + STEP)
        cols = [[spread(rows[s + g], base + q) for g in range(groups)] for q in range(STEP)]
        work = [
            jnp.where(here, (lane - base == sub + SUB * g).astype(F32), rows[s + g]) for g in range(groups)
        ]
        done = [jnp.zeros((SUB, LANES), F32) for _ in range(groups)]
        for p in range(0, STEP, 2):
            at, j = divmod(p, SUB)
            first, second = sub == j, sub == j + 1
            pair = first | second
            pa, pb, pc = row(cols[p][at], j), row(cols[p][at], j + 1), row(cols[p + 1][at], j + 1)
            det = pa * pc - pb * pb
            if p % 4 == 0:
                inv = pl.reciprocal(det, approx=True)
                third, fourth = cols[p + 2][at], cols[p + 3][at]
                b00, b10, b01, b11 = row(third, j), row(third, j + 1), row(fourth, j), row(fourth, j + 1)
                w00, w10 = pc * b00 - pb * b10, pa * b10 - pb * b00
                w01, w11 = pc * b01 - pb * b11, pa * b11 - pb * b01
                s0 = det * row(third, j + 2) - (b00 * w00 + b10 * w10)
                s1 = det * row(third, j + 3) - (b00 * w01 + b10 * w11)
                s2 = det * row(fourth, j + 3) - (b01 * w01 + b11 * w11)
                next_inv = (det * det) * pl.reciprocal(s0 * s2 - s1 * s1, approx=True)
            else:
                inv = next_inv
            top, low = row(work[at], j), row(work[at], j + 1)
            done[at] = jnp.where(first, top * lax.rsqrt(pa), done[at])
            done[at] = jnp.where(second, (pa * low - pb * top) * lax.rsqrt(pa * det), done[at])
            raw, scaled = [], []
            for g in range(groups):
                m0, m1 = cols[p][g], cols[p + 1][g]
                if g == at:
                    m0 = jnp.where(first, -1.0, jnp.where(second, 0.0, m0))
                    m1 = jnp.where(second, -1.0, jnp.where(first, 0.0, m1))
                u0, u1 = m0 * pc - m1 * pb, m1 * pa - m0 * pb
                raw.append((u0, u1))
                scaled.append((u0 * inv, u1 * inv))
            for q in range(p + 2, STEP + 1):
                kept = cols[q] if q < STEP else work
                t, l = row(kept[at], j), row(kept[at], j + 1)
                moved = []
                for g in range(groups):
                    old = jnp.where(pair, 0.0, kept[g]) if g == at else kept[g]
                    if q < p + 4:
                        moved.append(old - (raw[g][0] * t + raw[g][1] * l) * inv)
                    else:
                        moved.append(old - (scaled[g][0] * t + scaled[g][1] * l))
                if q < STEP:
                    cols[q] = moved
                else:
                    work = moved
        for g in range(groups):
            out.append(jnp.where(lane <= base + SUB * g + sub, done[g], 0.0))
        lines = [row(work[p // SUB], p % SUB) for p in range(STEP)]
        later = s + 2 * groups
        for i in range(s + groups, min(later, count)):
            change = tree([spread(rows[i], base + p) * lines[p] for p in range(STEP)])
            rows[i] = jnp.where(here, 0.0, rows[i]) - change
        if later < count:
            rest = jnp.concatenate(rows[later:], axis=0)
            inside = jnp.concatenate([here] * (count - later), axis=0)
            pieces = [jnp.zeros((base, LANES), F32)] if base else []
            pieces += work + [jnp.zeros((LANES - base - STEP, LANES), F32)]
            change = dot(jnp.where(inside, rest, 0.0), jnp.concatenate(pieces, axis=0))
            rest = jnp.where(inside, 0.0, rest) - change
            rows[later:] = [rest[SUB * i : SUB * (i + 1), :] for i in range(count - later)]
    return jnp.concatenate(out, axis=0) * SCALE**0.5


def blend(before, after):
    return 1.0 + RELAX * (jnp.sqrt(before / after) - 1.0)


def add_up(x):
    return jnp.sum(jnp.sum(x, axis=0, keepdims=True), axis=1, keepdims=True)


def dot3(a, b):
    a_high, a_low = split(a)
    b_high, b_low = split(b)
    left = jnp.concatenate([a_high, a_low, a_high], axis=1)
    return dot(left, jnp.concatenate([b_high, b_high, b_low], axis=0), precision=None)


def identity(size):
    return (
        lax.broadcasted_iota(jnp.int32, (size, size), 0) == lax.broadcasted_iota(jnp.int32, (size, size), 1)
    ).astype(F32)


def update_kernel(
    chunks, mine_v, other_v, mean_v, x_hbm, out_hbm, mean_out, full, x_buf, o_buf, in_sem, out_sem
):
    members = x_buf.shape[1]
    size = x_buf.shape[0] // chunks
    load = chunk_copy(x_hbm, x_buf, in_sem, chunks)
    store = chunk_copy(o_buf, out_hbm, out_sem, chunks)
    for i in range(chunks):
        load(i).start()

    mine = lax.axis_index(AXIS) & 1
    span = PACKED // 2
    full[pl.ds(pl.multiple_of(mine * span, SUB), span), :] = mine_v[...]
    full[pl.ds(pl.multiple_of((1 - mine) * span, SUB), span), :] = other_v[...]

    half = members // 2
    quarter = half // 2

    def block(at):
        return full[at : at + half, :]

    def innovation(k):
        count = OBS // INNOV_LANES
        at = INNOV + count * k
        return column(jnp.concatenate([full[at + j : at + j + 1, :INNOV_LANES] for j in range(count)], axis=1))

    first = jnp.concatenate([block(A0), block(A1)], axis=1)
    second = jnp.concatenate([block(B0), block(B1)], axis=1)
    g00, g01, top = block(G00), block(G01), full[G11:, :]
    line = lax.broadcasted_iota(jnp.int32, (half, half), 0)
    lane = lax.broadcasted_iota(jnp.int32, (half, half), 1)
    last = jnp.concatenate([jnp.zeros((quarter, quarter), F32), g00[quarter:, :quarter]], axis=1)
    corner = (line >= quarter) & (lane < quarter)
    g00 = jnp.where(corner, g00.T, g00)
    g11 = jnp.concatenate([top, last], axis=0)
    inner = (line >= INNOV - G00) & (lane >= quarter) & (lane < quarter + INNOV_LANES)
    g11 = jnp.where(corner | inner, g11.T, g11)
    gram = jnp.concatenate(
        [jnp.concatenate([g00, g01], axis=1), jnp.concatenate([g01.T, g11], axis=1)], axis=0
    )
    eye = identity(half)

    inv_m = factor(eye + dot(first, first, ((1,), (1,))))
    v_and_f = dot(inv_m, jnp.concatenate([first, innovation(0)], axis=1))
    v, f = v_and_f[:, :members], v_and_f[:, members:]
    before = add_up(eye * (g00 + g11))
    after1 = before - add_up(dot3(v, gram) * v)
    factor1 = blend(before, after1)
    increment = jnp.sum(v * jnp.concatenate([f, f], axis=1), axis=0, keepdims=True)
    innov2 = innovation(1) - jnp.sum(second * increment, axis=1, keepdims=True)

    a1 = dot(first, first, ((0,), (0,)))
    a2 = dot(second, jnp.concatenate([second, innov2], axis=1), ((0,), (0,)))
    square = factor1 * factor1
    k00 = eye + a1[:half, :half] + a2[:half, :half] * square
    k01 = a1[:half, half:] + a2[:half, half:members] * square
    k11 = eye + a1[half:, half:] + a2[half:, half:members] * square
    inv00 = factor(k00)
    u = dot(inv00, k01)
    inv11 = factor(k11 - dot(u, u, ((0,), (0,))))
    inv10 = -dot(inv11, dot(u, inv00, ((0,), (0,))))
    y0 = dot(inv00, a2[:half, members:] * square)
    y1 = dot(inv11, a2[half:, members:] * square - dot(u, y0, ((0,), (0,))))
    bottom = jnp.concatenate([inv10, inv11], axis=1)
    top_trace = add_up(dot3(inv00, g00) * inv00)
    after2 = top_trace + add_up(dot3(bottom, gram) * bottom)
    factor2 = factor1 * blend(after1, after2)
    increment0 = jnp.sum(y0 * inv00 + y1 * inv10, axis=0, keepdims=True)
    increment1 = jnp.sum(y1 * inv11, axis=0, keepdims=True)
    increment = increment + jnp.concatenate([increment0, increment1], axis=1)

    turned = jnp.concatenate(
        [jnp.concatenate([inv00.T, inv10.T], axis=1), jnp.concatenate([jnp.zeros_like(inv00), inv11.T], axis=1)], axis=0
    )
    high, low = split(turned)
    transform = jnp.concatenate([high, high, low], axis=0)
    step_line = lax.broadcasted_iota(jnp.int32, (LANES, LANES), 0)
    diagonal = step_line == lax.broadcasted_iota(jnp.int32, (LANES, LANES), 1)

    def apply(i, at):
        load(i).wait()
        x = x_buf[pl.ds(at, size), :]
        high, low = split(x)
        moved = dot(jnp.concatenate([high, low, high], axis=1), transform, precision=None)
        o_buf[pl.ds(at, size), :] = moved * factor2
        store(i).start()
        steps = jnp.sum(x * increment, axis=1, keepdims=True)
        for j in range(0, size, LANES):
            step = jnp.sum(jnp.where(diagonal, steps[j : j + LANES, :], 0.0), axis=0, keepdims=True)
            part = pl.ds(at + j, LANES)
            mean_out[:, part] = mean_v[:, part] + step

    apply(0, 0)

    def body(i, _):
        apply(i, pl.multiple_of(i * size, size))
        return 0

    lax.fori_loop(1, chunks, body, 0)
    for i in range(chunks):
        store(i).wait()


def spec(space):
    return pl.BlockSpec(memory_space=space)


def params():
    return pltpu.CompilerParams(vmem_limit_bytes=VMEM_LIMIT)


def cost(flops, bytes_accessed):
    return pl.CostEstimate(flops=flops, bytes_accessed=bytes_accessed, transcendentals=0)


def cost(flops, bytes_accessed):
    return pl.CostEstimate(flops=flops, bytes_accessed=bytes_accessed, transcendentals=0)


def gram_of(ensemble):
    rows, members = ensemble.shape
    chunks = 4
    return pl.pallas_call(
        functools.partial(gram_kernel, chunks),
        out_shape=jax.ShapeDtypeStruct((PACKED - G00, LANES), F32),
        in_specs=[spec(pltpu.HBM)],
        out_specs=spec(pltpu.VMEM),
        scratch_shapes=[pltpu.VMEM((rows, members), F32), pltpu.SemaphoreType.DMA((chunks,))],
        cost_estimate=cost(4 * rows * members * members, 4 * rows * members),
        compiler_params=params(),
    )(ensemble)


def gather(ensemble, mean_state, observed, error_var, owner, obs_rows, gram):
    members = ensemble.shape[1]
    half = jax.ShapeDtypeStruct((PACKED // 2, LANES), F32)
    return pl.pallas_call(
        gather_kernel,
        out_shape=(half, half),
        in_specs=[spec(pltpu.SMEM), spec(pltpu.SMEM)] + [spec(pltpu.VMEM)] * 5 + [spec(pltpu.HBM)],
        out_specs=[spec(pltpu.VMEM)] * 2,
        scratch_shapes=[
            pltpu.VMEM((PACKED, LANES), F32),
            pltpu.VMEM((2, OBS, members), F32),
            pltpu.SemaphoreType.DMA((2,)),
        ],
        compiler_params=params(),
    )(owner, obs_rows, obs_rows, observed, error_var, mean_state.reshape(-1, LANES), gram, ensemble)


def update(packed, ensemble, mean_state):
    rows, members = ensemble.shape
    chunks = 4
    out, mean = pl.pallas_call(
        functools.partial(update_kernel, chunks),
        out_shape=(jax.ShapeDtypeStruct((rows, members), F32), jax.ShapeDtypeStruct((1, rows), F32)),
        in_specs=[spec(pltpu.VMEM)] * 3 + [spec(pltpu.HBM)],
        out_specs=(spec(pltpu.HBM), spec(pltpu.VMEM)),
        scratch_shapes=[
            pltpu.VMEM((PACKED, LANES), F32),
            pltpu.VMEM((rows, members), F32),
            pltpu.VMEM((rows, members), F32),
            pltpu.SemaphoreType.DMA((chunks,)),
            pltpu.SemaphoreType.DMA((chunks,)),
        ],
        compiler_params=params(),
    )(*packed, mean_state.reshape(1, rows), ensemble)
    return out, mean.reshape(rows)


def swap(value, count, mask):
    return lax.ppermute(value, AXIS, [(i, i ^ mask) for i in range(count)])


def total(keep, send, count):
    odd = ((lax.axis_index(AXIS) >> 1) & 1) == 1
    value = keep + swap(send, count, 1)
    low, high = jnp.split(value, 2, axis=0)
    value = jnp.where(odd, high, low) + swap(jnp.where(odd, low, high), count, 2)
    mask = 4
    while mask < count:
        value = value + swap(value, count, mask)
        mask *= 2
    got = swap(value, count, 2)
    value = jnp.concatenate([jnp.where(odd, got, value), jnp.where(odd, value, got)], axis=0)
    return value, swap(value, count, 1)


def on_device(count, ensemble, mean_state, observed, error_var, owner, obs_rows):
    gram = gram_of(ensemble)
    keep, send = gather(ensemble, mean_state, observed, error_var, owner, obs_rows, gram)
    return update(total(keep, send, count), ensemble, mean_state)


def solution(mesh):
    count = mesh.shape[AXIS]
    in_specs = (
        P(("groups", "rows"), None),
        P(("groups", "rows")),
        P("groups", None),
        P("groups", None),
        P("groups"),
        P("groups", None),
    )
    out_specs = (P(("groups", "rows"), None), P(("groups", "rows")))

    def body(*args):
        return on_device(count, *args)

    return jax.shard_map(body, mesh=mesh, in_specs=in_specs, out_specs=out_specs, check_vma=False)
```

```python
import functools

import jax
import jax.numpy as jnp
from jax import lax
from jax.experimental import pallas as pl
from jax.experimental.pallas import tpu as pltpu
from jax.sharding import PartitionSpec as P

RELAX = 0.6
HI = lax.Precision.HIGHEST
AXIS = "rows"
F32 = jnp.float32
BF16 = jnp.bfloat16
LANES = 128
SUB = 8
OBS = 128
VMEM_LIMIT = 51 * 1024 * 1024
STEP = 16
SCALE = 2.0**-16

A0, A1, B0, B1, G00, G01, G11 = range(0, 7 * 128, 128)
PACKED = G11 + 64
INNOV = G00 + 96
INNOV_LANES = 32


def dot(a, b, dims=((1,), (0,)), precision=HI):
    return lax.dot_general(a, b, (dims, ((), ())), precision=precision, preferred_element_type=F32)


def column(row):
    return jnp.broadcast_to(row, (LANES, LANES)).T


def parity():
    me = lax.axis_index(AXIS)
    bits = me & 1
    for i in range(1, 10):
        bits = bits ^ ((me >> i) & 1)
    return bits


def split(x):
    high = x.astype(BF16)
    return high, (x - high.astype(F32)).astype(BF16)


def chunk_copy(source, target, sem, chunks):
    size = source.shape[0] // chunks

    def copy(i):
        part = pl.ds(i * size, size)
        return pltpu.make_async_copy(source.at[part], target.at[part], sem.at[i])

    return copy


def gram_kernel(chunks, x_hbm, out, x_buf, sem):
    members = x_buf.shape[1]
    size = x_buf.shape[0] // chunks
    half = members // 2
    copy = chunk_copy(x_hbm, x_buf, sem, chunks)
    for i in range(chunks):
        copy(i).start()
    total = None
    for i in range(chunks):
        copy(i).wait()
        high, low = split(x_buf[i * size : (i + 1) * size, :])
        part = dot(high, jnp.concatenate([high, low], axis=1), ((0,), (0,)), None)
        total = part if total is None else total + part
    cross = total[:, members:]
    total = total[:, :members] + cross + cross.T
    quarter = half // 2
    out[:quarter, :] = total[:quarter, :half]
    out[quarter:half, :] = jnp.concatenate(
        [total[half + quarter :, half + quarter :], total[quarter:half, quarter:half]], axis=1
    )
    out[half : 2 * half, :] = total[:half, half:]
    out[2 * half :, :] = total[half : half + quarter, half:]


def gather_kernel(
    owner_s, rows_s, rows_v, observed, error_var, mean_v, gram, x_hbm, keep, send, full, picked, sem
):
    me = lax.axis_index(AXIS)
    members = picked.shape[2]
    half = members // 2

    for k in range(2):

        @pl.when(owner_s[k] == me)
        def _(k=k):
            def fetch(o, _):
                pltpu.make_async_copy(
                    x_hbm.at[pl.ds(rows_s[k, o], 1)], picked.at[k, pl.ds(o, 1)], sem.at[k]
                ).start()
                return 0

            lax.fori_loop(0, OBS, fetch, 0, unroll=32)

    innovations = []
    scales = []
    lane = lax.broadcasted_iota(jnp.int32, (OBS, LANES), 1)
    for k in range(2):
        index = column(rows_v[k : k + 1, :].astype(F32)).astype(jnp.int32)
        prior = jnp.zeros((OBS, LANES), F32)
        for r in range(mean_v.shape[0]):
            prior = prior + jnp.where(index == lane + r * LANES, mean_v[r : r + 1, :], 0.0)
        prior = jnp.sum(prior.T, axis=0, keepdims=True)
        scale = lax.rsqrt(error_var[k : k + 1, :] * (members - 1.0))
        scales.append(column(scale))
        innov = jnp.where(owner_s[k] == me, scale * (observed[k : k + 1, :] - prior), 0.0)
        innovations += [innov[:, j : j + INNOV_LANES] for j in range(0, OBS, INNOV_LANES)]

    full[G00:, :] = gram[...]
    for i, innov in enumerate(innovations):
        full[INNOV + i : INNOV + i + 1, :INNOV_LANES] = innov
    full[:G00, :] = jnp.zeros((G00, LANES), F32)
    for k, left, right in ((0, A0, A1), (1, B0, B1)):

        @pl.when(owner_s[k] == me)
        def _(k=k, left=left, right=right):
            pltpu.make_async_copy(x_hbm.at[pl.ds(0, OBS)], picked.at[k], sem.at[k]).wait()
            full[left : left + OBS, :] = picked[k, :, :half] * scales[k]
            full[right : right + OBS, :] = picked[k, :, half:] * scales[k]

    mine = parity()
    span = PACKED // 2
    keep[...] = full[pl.ds(pl.multiple_of(mine * span, SUB), span), :]
    send[...] = full[pl.ds(pl.multiple_of((1 - mine) * span, SUB), span), :]


def tree(terms):
    while len(terms) > 1:
        terms = [terms[i] + terms[i + 1] if i + 1 < len(terms) else terms[i] for i in range(0, len(terms), 2)]
    return terms[0]


def factor(a):
    a = a * SCALE
    count = LANES // SUB
    lane = lax.broadcasted_iota(jnp.int32, (SUB, LANES), 1)
    sub = lax.broadcasted_iota(jnp.int32, (SUB, LANES), 0)
    rows = [a[SUB * i : SUB * (i + 1), :] for i in range(count)]
    out = []

    def spread(x, c):
        return jnp.broadcast_to(x[:, c : c + 1], (SUB, LANES))

    def row(x, j):
        return jnp.broadcast_to(x[j : j + 1, :], (SUB, LANES))

    groups = STEP // SUB
    for s in range(0, count, groups):
        base = SUB * s
        here = (lane >= base) & (lane < base + STEP)
        cols = [[spread(rows[s + g], base + q) for g in range(groups)] for q in range(STEP)]
        work = [
            jnp.where(here, (lane - base == sub + SUB * g).astype(F32), rows[s + g]) for g in range(groups)
        ]
        done = [jnp.zeros((SUB, LANES), F32) for _ in range(groups)]
        for p in range(0, STEP, 2):
            at, j = divmod(p, SUB)
            first, second = sub == j, sub == j + 1
            pair = first | second
            pa, pb, pc = row(cols[p][at], j), row(cols[p][at], j + 1), row(cols[p + 1][at], j + 1)
            det = pa * pc - pb * pb
            if p % 4 == 0:
                inv = pl.reciprocal(det, approx=True)
                third, fourth = cols[p + 2][at], cols[p + 3][at]
                b00, b10, b01, b11 = row(third, j), row(third, j + 1), row(fourth, j), row(fourth, j + 1)
                w00, w10 = pc * b00 - pb * b10, pa * b10 - pb * b00
                w01, w11 = pc * b01 - pb * b11, pa * b11 - pb * b01
                s0 = det * row(third, j + 2) - (b00 * w00 + b10 * w10)
                s1 = det * row(third, j + 3) - (b00 * w01 + b10 * w11)
                s2 = det * row(fourth, j + 3) - (b01 * w01 + b11 * w11)
                next_inv = (det * det) * pl.reciprocal(s0 * s2 - s1 * s1, approx=True)
            else:
                inv = next_inv
            top, low = row(work[at], j), row(work[at], j + 1)
            done[at] = jnp.where(first, top * lax.rsqrt(pa), done[at])
            done[at] = jnp.where(second, (pa * low - pb * top) * lax.rsqrt(pa * det), done[at])
            raw, scaled = [], []
            for g in range(groups):
                m0, m1 = cols[p][g], cols[p + 1][g]
                if g == at:
                    m0 = jnp.where(first, -1.0, jnp.where(second, 0.0, m0))
                    m1 = jnp.where(second, -1.0, jnp.where(first, 0.0, m1))
                u0, u1 = m0 * pc - m1 * pb, m1 * pa - m0 * pb
                raw.append((u0, u1))
                scaled.append((u0 * inv, u1 * inv))
            for q in range(p + 2, STEP + 1):
                kept = cols[q] if q < STEP else work
                t, l = row(kept[at], j), row(kept[at], j + 1)
                moved = []
                for g in range(groups):
                    old = jnp.where(pair, 0.0, kept[g]) if g == at else kept[g]
                    if q < p + 4:
                        moved.append(old - (raw[g][0] * t + raw[g][1] * l) * inv)
                    else:
                        moved.append(old - (scaled[g][0] * t + scaled[g][1] * l))
                if q < STEP:
                    cols[q] = moved
                else:
                    work = moved
        for g in range(groups):
            out.append(jnp.where(lane <= base + SUB * g + sub, done[g], 0.0))
        lines = [row(work[p // SUB], p % SUB) for p in range(STEP)]
        later = s + 2 * groups
        for i in range(s + groups, min(later, count)):
            change = tree([spread(rows[i], base + p) * lines[p] for p in range(STEP)])
            rows[i] = jnp.where(here, 0.0, rows[i]) - change
        if later < count:
            rest = jnp.concatenate(rows[later:], axis=0)
            inside = jnp.concatenate([here] * (count - later), axis=0)
            pieces = [jnp.zeros((base, LANES), F32)] if base else []
            pieces += work + [jnp.zeros((LANES - base - STEP, LANES), F32)]
            change = dot(jnp.where(inside, rest, 0.0), jnp.concatenate(pieces, axis=0))
            rest = jnp.where(inside, 0.0, rest) - change
            rows[later:] = [rest[SUB * i : SUB * (i + 1), :] for i in range(count - later)]
    return jnp.concatenate(out, axis=0) * SCALE**0.5


def blend(before, after):
    return 1.0 + RELAX * (jnp.sqrt(before / after) - 1.0)


def add_up(x):
    return jnp.sum(jnp.sum(x, axis=0, keepdims=True), axis=1, keepdims=True)


def dot3(a, b):
    a_high, a_low = split(a)
    b_high, b_low = split(b)
    left = jnp.concatenate([a_high, a_low, a_high], axis=1)
    return dot(left, jnp.concatenate([b_high, b_high, b_low], axis=0), precision=None)


def identity(size):
    return (
        lax.broadcasted_iota(jnp.int32, (size, size), 0) == lax.broadcasted_iota(jnp.int32, (size, size), 1)
    ).astype(F32)


def update_kernel(
    chunks, mine_v, other_v, mean_v, x_hbm, out_hbm, mean_out, full, x_buf, o_buf, in_sem, out_sem
):
    members = x_buf.shape[1]
    size = x_buf.shape[0] // chunks
    load = chunk_copy(x_hbm, x_buf, in_sem, chunks)
    store = chunk_copy(o_buf, out_hbm, out_sem, chunks)
    for i in range(chunks):
        load(i).start()

    mine = parity()
    span = PACKED // 2
    full[pl.ds(pl.multiple_of(mine * span, SUB), span), :] = mine_v[...]
    full[pl.ds(pl.multiple_of((1 - mine) * span, SUB), span), :] = other_v[...]

    half = members // 2
    quarter = half // 2

    def block(at):
        return full[at : at + half, :]

    def innovation(k):
        count = OBS // INNOV_LANES
        at = INNOV + count * k
        return column(jnp.concatenate([full[at + j : at + j + 1, :INNOV_LANES] for j in range(count)], axis=1))

    first = jnp.concatenate([block(A0), block(A1)], axis=1)
    second = jnp.concatenate([block(B0), block(B1)], axis=1)
    g00, g01, top = block(G00), block(G01), full[G11:, :]
    line = lax.broadcasted_iota(jnp.int32, (half, half), 0)
    lane = lax.broadcasted_iota(jnp.int32, (half, half), 1)
    last = jnp.concatenate([jnp.zeros((quarter, quarter), F32), g00[quarter:, :quarter]], axis=1)
    corner = (line >= quarter) & (lane < quarter)
    g00 = jnp.where(corner, g00.T, g00)
    g11 = jnp.concatenate([top, last], axis=0)
    inner = (line >= INNOV - G00) & (lane >= quarter) & (lane < quarter + INNOV_LANES)
    g11 = jnp.where(corner | inner, g11.T, g11)
    gram = jnp.concatenate(
        [jnp.concatenate([g00, g01], axis=1), jnp.concatenate([g01.T, g11], axis=1)], axis=0
    )
    eye = identity(half)

    inv_m = factor(eye + dot(first, first, ((1,), (1,))))
    v_and_f = dot(inv_m, jnp.concatenate([first, innovation(0)], axis=1))
    v, f = v_and_f[:, :members], v_and_f[:, members:]
    before = add_up(eye * (g00 + g11))
    after1 = before - add_up(dot3(v, gram) * v)
    factor1 = blend(before, after1)
    increment = jnp.sum(v * jnp.concatenate([f, f], axis=1), axis=0, keepdims=True)
    innov2 = innovation(1) - jnp.sum(second * increment, axis=1, keepdims=True)

    a1 = dot(first, first, ((0,), (0,)))
    a2 = dot(second, jnp.concatenate([second, innov2], axis=1), ((0,), (0,)))
    square = factor1 * factor1
    k00 = eye + a1[:half, :half] + a2[:half, :half] * square
    k01 = a1[:half, half:] + a2[:half, half:members] * square
    k11 = eye + a1[half:, half:] + a2[half:, half:members] * square
    inv00 = factor(k00)
    u = dot(inv00, k01)
    inv11 = factor(k11 - dot(u, u, ((0,), (0,))))
    inv10 = -dot(inv11, dot(u, inv00, ((0,), (0,))))
    y0 = dot(inv00, a2[:half, members:] * square)
    y1 = dot(inv11, a2[half:, members:] * square - dot(u, y0, ((0,), (0,))))
    bottom = jnp.concatenate([inv10, inv11], axis=1)
    top_trace = add_up(dot3(inv00, g00) * inv00)
    after2 = top_trace + add_up(dot3(bottom, gram) * bottom)
    factor2 = factor1 * blend(after1, after2)
    increment0 = jnp.sum(y0 * inv00 + y1 * inv10, axis=0, keepdims=True)
    increment1 = jnp.sum(y1 * inv11, axis=0, keepdims=True)
    increment = increment + jnp.concatenate([increment0, increment1], axis=1)

    turned = jnp.concatenate(
        [jnp.concatenate([inv00.T, inv10.T], axis=1), jnp.concatenate([jnp.zeros_like(inv00), inv11.T], axis=1)], axis=0
    )
    high, low = split(turned)
    transform = jnp.concatenate([high, high, low], axis=0)
    step_line = lax.broadcasted_iota(jnp.int32, (LANES, LANES), 0)
    diagonal = step_line == lax.broadcasted_iota(jnp.int32, (LANES, LANES), 1)

    def apply(i, at):
        load(i).wait()
        x = x_buf[pl.ds(at, size), :]
        high, low = split(x)
        moved = dot(jnp.concatenate([high, low, high], axis=1), transform, precision=None)
        o_buf[pl.ds(at, size), :] = moved * factor2
        store(i).start()
        steps = jnp.sum(x * increment, axis=1, keepdims=True)
        for j in range(0, size, LANES):
            step = jnp.sum(jnp.where(diagonal, steps[j : j + LANES, :], 0.0), axis=0, keepdims=True)
            part = pl.ds(at + j, LANES)
            mean_out[:, part] = mean_v[:, part] + step

    apply(0, 0)

    def body(i, _):
        apply(i, pl.multiple_of(i * size, size))
        return 0

    lax.fori_loop(1, chunks, body, 0)
    for i in range(chunks):
        store(i).wait()


def spec(space):
    return pl.BlockSpec(memory_space=space)


def params():
    return pltpu.CompilerParams(vmem_limit_bytes=VMEM_LIMIT)


def cost(flops, bytes_accessed):
    return pl.CostEstimate(flops=flops, bytes_accessed=bytes_accessed, transcendentals=0)


def cost(flops, bytes_accessed):
    return pl.CostEstimate(flops=flops, bytes_accessed=bytes_accessed, transcendentals=0)


def gram_of(ensemble):
    rows, members = ensemble.shape
    chunks = 4
    return pl.pallas_call(
        functools.partial(gram_kernel, chunks),
        out_shape=jax.ShapeDtypeStruct((PACKED - G00, LANES), F32),
        in_specs=[spec(pltpu.HBM)],
        out_specs=spec(pltpu.VMEM),
        scratch_shapes=[pltpu.VMEM((rows, members), F32), pltpu.SemaphoreType.DMA((chunks,))],
        cost_estimate=cost(4 * rows * members * members, 4 * rows * members),
        compiler_params=params(),
    )(ensemble)


def gather(ensemble, mean_state, observed, error_var, owner, obs_rows, gram):
    members = ensemble.shape[1]
    half = jax.ShapeDtypeStruct((PACKED // 2, LANES), F32)
    return pl.pallas_call(
        gather_kernel,
        out_shape=(half, half),
        in_specs=[spec(pltpu.SMEM), spec(pltpu.SMEM)] + [spec(pltpu.VMEM)] * 5 + [spec(pltpu.HBM)],
        out_specs=[spec(pltpu.VMEM)] * 2,
        scratch_shapes=[
            pltpu.VMEM((PACKED, LANES), F32),
            pltpu.VMEM((2, OBS, members), F32),
            pltpu.SemaphoreType.DMA((2,)),
        ],
        compiler_params=params(),
    )(owner, obs_rows, obs_rows, observed, error_var, mean_state.reshape(-1, LANES), gram, ensemble)


def update(packed, ensemble, mean_state):
    rows, members = ensemble.shape
    chunks = 4
    out, mean = pl.pallas_call(
        functools.partial(update_kernel, chunks),
        out_shape=(jax.ShapeDtypeStruct((rows, members), F32), jax.ShapeDtypeStruct((1, rows), F32)),
        in_specs=[spec(pltpu.VMEM)] * 3 + [spec(pltpu.HBM)],
        out_specs=(spec(pltpu.HBM), spec(pltpu.VMEM)),
        scratch_shapes=[
            pltpu.VMEM((PACKED, LANES), F32),
            pltpu.VMEM((rows, members), F32),
            pltpu.VMEM((rows, members), F32),
            pltpu.SemaphoreType.DMA((chunks,)),
            pltpu.SemaphoreType.DMA((chunks,)),
        ],
        compiler_params=params(),
    )(*packed, mean_state.reshape(1, rows), ensemble)
    return out, mean.reshape(rows)


def swap(value, count, mask):
    return lax.ppermute(value, AXIS, [(i, i ^ mask) for i in range(count)])


def total(keep, send, count):
    odd = ((lax.axis_index(AXIS) >> 1) & 1) == 1
    value = keep + swap(send, count, 1)
    low, high = jnp.split(value, 2, axis=0)
    value = jnp.where(odd, high, low) + swap(jnp.where(odd, low, high), count, 2 | 1)
    mask = 4
    while mask < count:
        value = value + swap(value, count, mask | 1)
        mask *= 2
    got = swap(value, count, 2 | 1)
    value = jnp.concatenate([jnp.where(odd, got, value), jnp.where(odd, value, got)], axis=0)
    return value, swap(value, count, 1)


def on_device(count, ensemble, mean_state, observed, error_var, owner, obs_rows):
    gram = gram_of(ensemble)
    keep, send = gather(ensemble, mean_state, observed, error_var, owner, obs_rows, gram)
    return update(total(keep, send, count), ensemble, mean_state)


def solution(mesh):
    count = mesh.shape[AXIS]
    in_specs = (
        P(("groups", "rows"), None),
        P(("groups", "rows")),
        P("groups", None),
        P("groups", None),
        P("groups"),
        P("groups", None),
    )
    out_specs = (P(("groups", "rows"), None), P(("groups", "rows")))

    def body(*args):
        return on_device(count, *args)

    return jax.shard_map(body, mesh=mesh, in_specs=in_specs, out_specs=out_specs, check_vma=False)
```

```python
import functools

import jax
import jax.numpy as jnp
from jax import lax
from jax.experimental import pallas as pl
from jax.experimental.pallas import tpu as pltpu
from jax.sharding import PartitionSpec as P

RELAX = 0.6
HI = lax.Precision.HIGHEST
AXIS = "rows"
F32 = jnp.float32
BF16 = jnp.bfloat16
LANES = 128
SUB = 8
OBS = 128
VMEM_LIMIT = 51 * 1024 * 1024
STEP = 16
SCALE = 2.0**-16

A0, A1, B0, B1, G00, G01, G11 = range(0, 7 * 128, 128)
PACKED = G11 + 64
INNOV = G00 + 96
INNOV_LANES = 32


def dot(a, b, dims=((1,), (0,)), precision=HI):
    return lax.dot_general(a, b, (dims, ((), ())), precision=precision, preferred_element_type=F32)


def column(row):
    return jnp.broadcast_to(row, (LANES, LANES)).T


def split(x):
    high = x.astype(BF16)
    return high, (x - high.astype(F32)).astype(BF16)


def chunk_copy(source, target, sem, chunks):
    size = source.shape[0] // chunks

    def copy(i):
        part = pl.ds(i * size, size)
        return pltpu.make_async_copy(source.at[part], target.at[part], sem.at[i])

    return copy


def gram_kernel(chunks, x_hbm, out, x_buf, sem):
    members = x_buf.shape[1]
    size = x_buf.shape[0] // chunks
    half = members // 2
    copy = chunk_copy(x_hbm, x_buf, sem, chunks)
    for i in range(chunks):
        copy(i).start()
    total = None
    for i in range(chunks):
        copy(i).wait()
        high, low = split(x_buf[i * size : (i + 1) * size, :])
        part = dot(high, jnp.concatenate([high, low], axis=1), ((0,), (0,)), None)
        total = part if total is None else total + part
    cross = total[:, members:]
    total = total[:, :members] + cross + cross.T
    quarter = half // 2
    out[:quarter, :] = total[:quarter, :half]
    out[quarter:half, :] = jnp.concatenate(
        [total[half + quarter :, half + quarter :], total[quarter:half, quarter:half]], axis=1
    )
    out[half : 2 * half, :] = total[:half, half:]
    out[2 * half :, :] = total[half : half + quarter, half:]


def gather_kernel(
    owner_s, rows_s, rows_v, observed, error_var, mean_v, gram, x_hbm, keep, send, full, picked, sem
):
    me = lax.axis_index(AXIS)
    members = picked.shape[2]
    half = members // 2

    full[:G00, :] = jnp.zeros((G00, LANES), F32)
    full[G00:, :] = gram[...]
    full[INNOV : INNOV + 2 * OBS // INNOV_LANES, :INNOV_LANES] = jnp.zeros((2 * OBS // INNOV_LANES, INNOV_LANES), F32)
    lane = lax.broadcasted_iota(jnp.int32, (OBS, LANES), 1)
    lines = mean_v.shape[0]
    fetches = OBS // lines

    for k, left, right in ((0, A0, A1), (1, B0, B1)):

        @pl.when(owner_s[k] == me)
        def _(k=k, left=left, right=right):
            index = column(rows_v[k : k + 1, :].astype(F32)).astype(jnp.int32) - lane

            def look(r, prior):
                for j in range(fetches):
                    o = r * fetches + j
                    pltpu.make_async_copy(
                        x_hbm.at[pl.ds(rows_s[k, o], 1)], picked.at[k, pl.ds(o, 1)], sem.at[k]
                    ).start()
                return prior + jnp.where(index == r * LANES, mean_v[pl.ds(r, 1), :], 0.0)

            prior = lax.fori_loop(0, lines, look, jnp.zeros((OBS, LANES), F32), unroll=8)
            prior = jnp.sum(prior.T, axis=0, keepdims=True)
            scale = lax.rsqrt(error_var[k : k + 1, :] * (members - 1.0))
            innov = scale * (observed[k : k + 1, :] - prior)
            count = OBS // INNOV_LANES
            for j in range(count):
                at = INNOV + count * k + j
                full[at : at + 1, :INNOV_LANES] = innov[:, j * INNOV_LANES : (j + 1) * INNOV_LANES]
            scales = column(scale)
            pltpu.make_async_copy(x_hbm.at[pl.ds(0, OBS)], picked.at[k], sem.at[k]).wait()
            full[left : left + OBS, :] = picked[k, :, :half] * scales
            full[right : right + OBS, :] = picked[k, :, half:] * scales

    mine = me & 1
    span = PACKED // 2
    keep[...] = full[pl.ds(pl.multiple_of(mine * span, SUB), span), :]
    send[...] = full[pl.ds(pl.multiple_of((1 - mine) * span, SUB), span), :]


def tree(terms):
    while len(terms) > 1:
        terms = [terms[i] + terms[i + 1] if i + 1 < len(terms) else terms[i] for i in range(0, len(terms), 2)]
    return terms[0]


def factor(a):
    a = a * SCALE
    count = LANES // SUB
    lane = lax.broadcasted_iota(jnp.int32, (SUB, LANES), 1)
    sub = lax.broadcasted_iota(jnp.int32, (SUB, LANES), 0)
    rows = [a[SUB * i : SUB * (i + 1), :] for i in range(count)]
    out = []

    def spread(x, c):
        return jnp.broadcast_to(x[:, c : c + 1], (SUB, LANES))

    def row(x, j):
        return jnp.broadcast_to(x[j : j + 1, :], (SUB, LANES))

    groups = STEP // SUB
    for s in range(0, count, groups):
        base = SUB * s
        here = (lane >= base) & (lane < base + STEP)
        cols = [[spread(rows[s + g], base + q) for g in range(groups)] for q in range(STEP)]
        work = [
            jnp.where(here, (lane - base == sub + SUB * g).astype(F32), rows[s + g]) for g in range(groups)
        ]
        done = [jnp.zeros((SUB, LANES), F32) for _ in range(groups)]
        for p in range(0, STEP, 2):
            at, j = divmod(p, SUB)
            first, second = sub == j, sub == j + 1
            pair = first | second
            pa, pb, pc = row(cols[p][at], j), row(cols[p][at], j + 1), row(cols[p + 1][at], j + 1)
            det = pa * pc - pb * pb
            if p % 4 == 0:
                inv = pl.reciprocal(det, approx=True)
                third, fourth = cols[p + 2][at], cols[p + 3][at]
                b00, b10, b01, b11 = row(third, j), row(third, j + 1), row(fourth, j), row(fourth, j + 1)
                w00, w10 = pc * b00 - pb * b10, pa * b10 - pb * b00
                w01, w11 = pc * b01 - pb * b11, pa * b11 - pb * b01
                s0 = det * row(third, j + 2) - (b00 * w00 + b10 * w10)
                s1 = det * row(third, j + 3) - (b00 * w01 + b10 * w11)
                s2 = det * row(fourth, j + 3) - (b01 * w01 + b11 * w11)
                next_inv = (det * det) * pl.reciprocal(s0 * s2 - s1 * s1, approx=True)
            else:
                inv = next_inv
            top, low = row(work[at], j), row(work[at], j + 1)
            done[at] = jnp.where(first, top * lax.rsqrt(pa), done[at])
            done[at] = jnp.where(second, (pa * low - pb * top) * lax.rsqrt(pa * det), done[at])
            raw, scaled = [], []
            for g in range(groups):
                m0, m1 = cols[p][g], cols[p + 1][g]
                if g == at:
                    m0 = jnp.where(first, -1.0, jnp.where(second, 0.0, m0))
                    m1 = jnp.where(second, -1.0, jnp.where(first, 0.0, m1))
                u0, u1 = m0 * pc - m1 * pb, m1 * pa - m0 * pb
                raw.append((u0, u1))
                scaled.append((u0 * inv, u1 * inv))
            for q in range(p + 2, STEP + 1):
                kept = cols[q] if q < STEP else work
                t, l = row(kept[at], j), row(kept[at], j + 1)
                moved = []
                for g in range(groups):
                    old = jnp.where(pair, 0.0, kept[g]) if g == at else kept[g]
                    if q < p + 4:
                        moved.append(old - (raw[g][0] * t + raw[g][1] * l) * inv)
                    else:
                        moved.append(old - (scaled[g][0] * t + scaled[g][1] * l))
                if q < STEP:
                    cols[q] = moved
                else:
                    work = moved
        for g in range(groups):
            out.append(jnp.where(lane <= base + SUB * g + sub, done[g], 0.0))
        lines = [row(work[p // SUB], p % SUB) for p in range(STEP)]
        later = s + 2 * groups
        for i in range(s + groups, min(later, count)):
            change = tree([spread(rows[i], base + p) * lines[p] for p in range(STEP)])
            rows[i] = jnp.where(here, 0.0, rows[i]) - change
        if later < count:
            rest = jnp.concatenate(rows[later:], axis=0)
            inside = jnp.concatenate([here] * (count - later), axis=0)
            pieces = [jnp.zeros((base, LANES), F32)] if base else []
            pieces += work + [jnp.zeros((LANES - base - STEP, LANES), F32)]
            change = dot(jnp.where(inside, rest, 0.0), jnp.concatenate(pieces, axis=0))
            rest = jnp.where(inside, 0.0, rest) - change
            rows[later:] = [rest[SUB * i : SUB * (i + 1), :] for i in range(count - later)]
    return jnp.concatenate(out, axis=0) * SCALE**0.5


def blend(before, after):
    return 1.0 + RELAX * (jnp.sqrt(before / after) - 1.0)


def add_up(x):
    return jnp.sum(jnp.sum(x, axis=0, keepdims=True), axis=1, keepdims=True)


def dot3(a, b):
    a_high, a_low = split(a)
    b_high, b_low = split(b)
    left = jnp.concatenate([a_high, a_low, a_high], axis=1)
    return dot(left, jnp.concatenate([b_high, b_high, b_low], axis=0), precision=None)


def identity(size):
    return (
        lax.broadcasted_iota(jnp.int32, (size, size), 0) == lax.broadcasted_iota(jnp.int32, (size, size), 1)
    ).astype(F32)


def update_kernel(
    chunks, mine_v, other_v, mean_v, x_hbm, out_hbm, mean_out, full, x_buf, o_buf, in_sem, out_sem
):
    members = x_buf.shape[1]
    size = x_buf.shape[0] // chunks
    load = chunk_copy(x_hbm, x_buf, in_sem, chunks)
    store = chunk_copy(o_buf, out_hbm, out_sem, chunks)
    for i in range(chunks):
        load(i).start()

    mine = lax.axis_index(AXIS) & 1
    span = PACKED // 2
    full[pl.ds(pl.multiple_of(mine * span, SUB), span), :] = mine_v[...]
    full[pl.ds(pl.multiple_of((1 - mine) * span, SUB), span), :] = other_v[...]

    half = members // 2
    quarter = half // 2

    def block(at):
        return full[at : at + half, :]

    def innovation(k):
        count = OBS // INNOV_LANES
        at = INNOV + count * k
        return column(jnp.concatenate([full[at + j : at + j + 1, :INNOV_LANES] for j in range(count)], axis=1))

    first = jnp.concatenate([block(A0), block(A1)], axis=1)
    second = jnp.concatenate([block(B0), block(B1)], axis=1)
    g00, g01, top = block(G00), block(G01), full[G11:, :]
    line = lax.broadcasted_iota(jnp.int32, (half, half), 0)
    lane = lax.broadcasted_iota(jnp.int32, (half, half), 1)
    last = jnp.concatenate([jnp.zeros((quarter, quarter), F32), g00[quarter:, :quarter]], axis=1)
    corner = (line >= quarter) & (lane < quarter)
    g00 = jnp.where(corner, g00.T, g00)
    g11 = jnp.concatenate([top, last], axis=0)
    inner = (line >= INNOV - G00) & (lane >= quarter) & (lane < quarter + INNOV_LANES)
    g11 = jnp.where(corner | inner, g11.T, g11)
    gram = jnp.concatenate(
        [jnp.concatenate([g00, g01], axis=1), jnp.concatenate([g01.T, g11], axis=1)], axis=0
    )
    eye = identity(half)

    inv_m = factor(eye + dot(first, first, ((1,), (1,))))
    v_and_f = dot(inv_m, jnp.concatenate([first, innovation(0)], axis=1))
    v, f = v_and_f[:, :members], v_and_f[:, members:]
    before = add_up(eye * (g00 + g11))
    after1 = before - add_up(dot3(v, gram) * v)
    factor1 = blend(before, after1)
    increment = jnp.sum(v * jnp.concatenate([f, f], axis=1), axis=0, keepdims=True)
    innov2 = innovation(1) - jnp.sum(second * increment, axis=1, keepdims=True)

    a1 = dot(first, first, ((0,), (0,)))
    a2 = dot(second, second, ((0,), (0,)))
    square = factor1 * factor1
    k00 = eye + a1[:half, :half] + a2[:half, :half] * square
    k01 = a1[:half, half:] + a2[:half, half:] * square
    k11 = eye + a1[half:, half:] + a2[half:, half:] * square
    inv00 = factor(k00)
    u = dot(inv00, k01)
    inv11 = factor(k11 - dot(u, u, ((0,), (0,))))
    inv10 = -dot(inv11, dot(u, inv00, ((0,), (0,))))
    target = dot(second, innov2, ((0,), (0,))) * square
    y0 = dot(inv00, target[:half, :])
    y1 = dot(inv11, target[half:, :] - dot(u, y0, ((0,), (0,))))
    bottom = jnp.concatenate([inv10, inv11], axis=1)
    top_trace = add_up(dot3(inv00, g00) * inv00)
    after2 = top_trace + add_up(dot3(bottom, gram) * bottom)
    factor2 = factor1 * blend(after1, after2)
    increment0 = jnp.sum(y0 * inv00 + y1 * inv10, axis=0, keepdims=True)
    increment1 = jnp.sum(y1 * inv11, axis=0, keepdims=True)
    increment = increment + jnp.concatenate([increment0, increment1], axis=1)

    turned = jnp.concatenate(
        [jnp.concatenate([inv00.T, inv10.T], axis=1), jnp.concatenate([jnp.zeros_like(inv00), inv11.T], axis=1)], axis=0
    )
    high, low = split(turned)
    transform = jnp.concatenate([high, high, low], axis=0)
    step_line = lax.broadcasted_iota(jnp.int32, (LANES, LANES), 0)
    diagonal = step_line == lax.broadcasted_iota(jnp.int32, (LANES, LANES), 1)

    def apply(i, at):
        load(i).wait()
        x = x_buf[pl.ds(at, size), :]
        high, low = split(x)
        moved = dot(jnp.concatenate([high, low, high], axis=1), transform, precision=None)
        o_buf[pl.ds(at, size), :] = moved * factor2
        store(i).start()
        steps = jnp.sum(x * increment, axis=1, keepdims=True)
        for j in range(0, size, LANES):
            step = jnp.sum(jnp.where(diagonal, steps[j : j + LANES, :], 0.0), axis=0, keepdims=True)
            part = pl.ds(at + j, LANES)
            mean_out[:, part] = mean_v[:, part] + step

    apply(0, 0)

    def body(i, _):
        apply(i, pl.multiple_of(i * size, size))
        return 0

    lax.fori_loop(1, chunks, body, 0)
    for i in range(chunks):
        store(i).wait()


def spec(space):
    return pl.BlockSpec(memory_space=space)


def params():
    return pltpu.CompilerParams(vmem_limit_bytes=VMEM_LIMIT)


def cost(flops, bytes_accessed):
    return pl.CostEstimate(flops=flops, bytes_accessed=bytes_accessed, transcendentals=0)


def cost(flops, bytes_accessed):
    return pl.CostEstimate(flops=flops, bytes_accessed=bytes_accessed, transcendentals=0)


def gram_of(ensemble):
    rows, members = ensemble.shape
    chunks = 4
    return pl.pallas_call(
        functools.partial(gram_kernel, chunks),
        out_shape=jax.ShapeDtypeStruct((PACKED - G00, LANES), F32),
        in_specs=[spec(pltpu.HBM)],
        out_specs=spec(pltpu.VMEM),
        scratch_shapes=[pltpu.VMEM((rows, members), F32), pltpu.SemaphoreType.DMA((chunks,))],
        cost_estimate=cost(4 * rows * members * members, 4 * rows * members),
        compiler_params=params(),
    )(ensemble)


def gather(ensemble, mean_state, observed, error_var, owner, obs_rows, gram):
    members = ensemble.shape[1]
    half = jax.ShapeDtypeStruct((PACKED // 2, LANES), F32)
    return pl.pallas_call(
        gather_kernel,
        out_shape=(half, half),
        in_specs=[spec(pltpu.SMEM), spec(pltpu.SMEM)] + [spec(pltpu.VMEM)] * 5 + [spec(pltpu.HBM)],
        out_specs=[spec(pltpu.VMEM)] * 2,
        scratch_shapes=[
            pltpu.VMEM((PACKED, LANES), F32),
            pltpu.VMEM((2, OBS, members), F32),
            pltpu.SemaphoreType.DMA((2,)),
        ],
        compiler_params=params(),
    )(owner, obs_rows, obs_rows, observed, error_var, mean_state.reshape(-1, LANES), gram, ensemble)


def update(packed, ensemble, mean_state):
    rows, members = ensemble.shape
    chunks = 4
    out, mean = pl.pallas_call(
        functools.partial(update_kernel, chunks),
        out_shape=(jax.ShapeDtypeStruct((rows, members), F32), jax.ShapeDtypeStruct((1, rows), F32)),
        in_specs=[spec(pltpu.VMEM)] * 3 + [spec(pltpu.HBM)],
        out_specs=(spec(pltpu.HBM), spec(pltpu.VMEM)),
        scratch_shapes=[
            pltpu.VMEM((PACKED, LANES), F32),
            pltpu.VMEM((rows, members), F32),
            pltpu.VMEM((rows, members), F32),
            pltpu.SemaphoreType.DMA((chunks,)),
            pltpu.SemaphoreType.DMA((chunks,)),
        ],
        compiler_params=params(),
    )(*packed, mean_state.reshape(1, rows), ensemble)
    return out, mean.reshape(rows)


def swap(value, count, mask):
    return lax.ppermute(value, AXIS, [(i, i ^ mask) for i in range(count)])


def total(keep, send, count):
    odd = ((lax.axis_index(AXIS) >> 1) & 1) == 1
    value = keep + swap(send, count, 1)
    low, high = jnp.split(value, 2, axis=0)
    value = jnp.where(odd, high, low) + swap(jnp.where(odd, low, high), count, 2)
    mask = 4
    while mask < count:
        value = value + swap(value, count, mask)
        mask *= 2
    got = swap(value, count, 2)
    value = jnp.concatenate([jnp.where(odd, got, value), jnp.where(odd, value, got)], axis=0)
    return value, swap(value, count, 1)


def on_device(count, ensemble, mean_state, observed, error_var, owner, obs_rows):
    gram = gram_of(ensemble)
    keep, send = gather(ensemble, mean_state, observed, error_var, owner, obs_rows, gram)
    return update(total(keep, send, count), ensemble, mean_state)


def solution(mesh):
    count = mesh.shape[AXIS]
    in_specs = (
        P(("groups", "rows"), None),
        P(("groups", "rows")),
        P("groups", None),
        P("groups", None),
        P("groups"),
        P("groups", None),
    )
    out_specs = (P(("groups", "rows"), None), P(("groups", "rows")))

    def body(*args):
        return on_device(count, *args)

    return jax.shard_map(body, mesh=mesh, in_specs=in_specs, out_specs=out_specs, check_vma=False)
```

```python
import functools

import jax
import jax.numpy as jnp
from jax import lax
from jax.experimental import pallas as pl
from jax.experimental.pallas import tpu as pltpu
from jax.sharding import PartitionSpec as P

RELAX = 0.6
HI = lax.Precision.HIGHEST
AXIS = "rows"
F32 = jnp.float32
BF16 = jnp.bfloat16
LANES = 128
SUB = 8
OBS = 128
VMEM_LIMIT = 51 * 1024 * 1024
STEP = 16
SCALE = 2.0**-16

A0, A1, B0, B1, G00, G01, G11 = range(0, 7 * 128, 128)
PACKED = G11 + 64
INNOV = G00 + 96
INNOV_LANES = 32


def dot(a, b, dims=((1,), (0,)), precision=HI):
    return lax.dot_general(a, b, (dims, ((), ())), precision=precision, preferred_element_type=F32)


def column(row):
    return jnp.broadcast_to(row, (LANES, LANES)).T


def split(x):
    high = x.astype(BF16)
    return high, (x - high.astype(F32)).astype(BF16)


def chunk_copy(source, target, sem, chunks):
    size = source.shape[0] // chunks

    def copy(i):
        part = pl.ds(i * size, size)
        return pltpu.make_async_copy(source.at[part], target.at[part], sem.at[i])

    return copy


def piece_copy(source, target, sem, pieces):
    def copy(i, at, size):
        part = pl.ds(at, size)
        return pltpu.make_async_copy(source.at[part], target.at[part], sem.at[i])

    def every(act):
        for i, (at, size) in enumerate(pieces):
            act(copy(i, at, size))

    return copy, every


def gram_kernel(chunks, x_hbm, out, x_buf, sem):
    members = x_buf.shape[1]
    size = x_buf.shape[0] // chunks
    half = members // 2
    copy = chunk_copy(x_hbm, x_buf, sem, chunks)
    for i in range(chunks):
        copy(i).start()
    total = None
    for i in range(chunks):
        copy(i).wait()
        high, low = split(x_buf[i * size : (i + 1) * size, :])
        part = dot(high, jnp.concatenate([high, low], axis=1), ((0,), (0,)), None)
        total = part if total is None else total + part
    cross = total[:, members:]
    total = total[:, :members] + cross + cross.T
    quarter = half // 2
    out[:quarter, :] = total[:quarter, :half]
    out[quarter:half, :] = jnp.concatenate(
        [total[half + quarter :, half + quarter :], total[quarter:half, quarter:half]], axis=1
    )
    out[half : 2 * half, :] = total[:half, half:]
    out[2 * half :, :] = total[half : half + quarter, half:]


def gather_kernel(
    owner_s, rows_s, rows_v, observed, error_var, mean_v, gram, x_hbm, keep, send, full, picked, sem
):
    me = lax.axis_index(AXIS)
    members = picked.shape[2]
    half = members // 2

    full[:G00, :] = jnp.zeros((G00, LANES), F32)
    full[G00:, :] = gram[...]
    full[INNOV : INNOV + 2 * OBS // INNOV_LANES, :INNOV_LANES] = jnp.zeros((2 * OBS // INNOV_LANES, INNOV_LANES), F32)
    lane = lax.broadcasted_iota(jnp.int32, (OBS, LANES), 1)
    lines = mean_v.shape[0]
    fetches = OBS // lines

    for k, left, right in ((0, A0, A1), (1, B0, B1)):

        @pl.when(owner_s[k] == me)
        def _(k=k, left=left, right=right):
            index = column(rows_v[k : k + 1, :].astype(F32)).astype(jnp.int32) - lane

            def look(r, prior):
                for j in range(fetches):
                    o = r * fetches + j
                    pltpu.make_async_copy(
                        x_hbm.at[pl.ds(rows_s[k, o], 1)], picked.at[k, pl.ds(o, 1)], sem.at[k]
                    ).start()
                return prior + jnp.where(index == r * LANES, mean_v[pl.ds(r, 1), :], 0.0)

            prior = lax.fori_loop(0, lines, look, jnp.zeros((OBS, LANES), F32), unroll=8)
            prior = jnp.sum(prior.T, axis=0, keepdims=True)
            scale = lax.rsqrt(error_var[k : k + 1, :] * (members - 1.0))
            innov = scale * (observed[k : k + 1, :] - prior)
            count = OBS // INNOV_LANES
            for j in range(count):
                at = INNOV + count * k + j
                full[at : at + 1, :INNOV_LANES] = innov[:, j * INNOV_LANES : (j + 1) * INNOV_LANES]
            scales = column(scale)
            pltpu.make_async_copy(x_hbm.at[pl.ds(0, OBS)], picked.at[k], sem.at[k]).wait()
            full[left : left + OBS, :] = picked[k, :, :half] * scales
            full[right : right + OBS, :] = picked[k, :, half:] * scales

    mine = me & 1
    span = PACKED // 2
    keep[...] = full[pl.ds(pl.multiple_of(mine * span, SUB), span), :]
    send[...] = full[pl.ds(pl.multiple_of((1 - mine) * span, SUB), span), :]


def tree(terms):
    while len(terms) > 1:
        terms = [terms[i] + terms[i + 1] if i + 1 < len(terms) else terms[i] for i in range(0, len(terms), 2)]
    return terms[0]


def factor(a):
    a = a * SCALE
    count = LANES // SUB
    lane = lax.broadcasted_iota(jnp.int32, (SUB, LANES), 1)
    sub = lax.broadcasted_iota(jnp.int32, (SUB, LANES), 0)
    rows = [a[SUB * i : SUB * (i + 1), :] for i in range(count)]
    out = []

    def spread(x, c):
        return jnp.broadcast_to(x[:, c : c + 1], (SUB, LANES))

    def row(x, j):
        return jnp.broadcast_to(x[j : j + 1, :], (SUB, LANES))

    groups = STEP // SUB
    for s in range(0, count, groups):
        base = SUB * s
        here = (lane >= base) & (lane < base + STEP)
        cols = [[spread(rows[s + g], base + q) for g in range(groups)] for q in range(STEP)]
        work = [
            jnp.where(here, (lane - base == sub + SUB * g).astype(F32), rows[s + g]) for g in range(groups)
        ]
        done = [jnp.zeros((SUB, LANES), F32) for _ in range(groups)]
        for p in range(0, STEP, 2):
            at, j = divmod(p, SUB)
            first, second = sub == j, sub == j + 1
            pair = first | second
            pa, pb, pc = row(cols[p][at], j), row(cols[p][at], j + 1), row(cols[p + 1][at], j + 1)
            det = pa * pc - pb * pb
            if p % 4 == 0:
                inv = pl.reciprocal(det, approx=True)
                third, fourth = cols[p + 2][at], cols[p + 3][at]
                b00, b10, b01, b11 = row(third, j), row(third, j + 1), row(fourth, j), row(fourth, j + 1)
                w00, w10 = pc * b00 - pb * b10, pa * b10 - pb * b00
                w01, w11 = pc * b01 - pb * b11, pa * b11 - pb * b01
                s0 = det * row(third, j + 2) - (b00 * w00 + b10 * w10)
                s1 = det * row(third, j + 3) - (b00 * w01 + b10 * w11)
                s2 = det * row(fourth, j + 3) - (b01 * w01 + b11 * w11)
                next_inv = (det * det) * pl.reciprocal(s0 * s2 - s1 * s1, approx=True)
            else:
                inv = next_inv
            top, low = row(work[at], j), row(work[at], j + 1)
            done[at] = jnp.where(first, top * lax.rsqrt(pa), done[at])
            done[at] = jnp.where(second, (pa * low - pb * top) * lax.rsqrt(pa * det), done[at])
            raw, scaled = [], []
            for g in range(groups):
                m0, m1 = cols[p][g], cols[p + 1][g]
                if g == at:
                    m0 = jnp.where(first, -1.0, jnp.where(second, 0.0, m0))
                    m1 = jnp.where(second, -1.0, jnp.where(first, 0.0, m1))
                u0, u1 = m0 * pc - m1 * pb, m1 * pa - m0 * pb
                raw.append((u0, u1))
                scaled.append((u0 * inv, u1 * inv))
            for q in range(p + 2, STEP + 1):
                kept = cols[q] if q < STEP else work
                t, l = row(kept[at], j), row(kept[at], j + 1)
                moved = []
                for g in range(groups):
                    old = jnp.where(pair, 0.0, kept[g]) if g == at else kept[g]
                    if q < p + 4:
                        moved.append(old - (raw[g][0] * t + raw[g][1] * l) * inv)
                    else:
                        moved.append(old - (scaled[g][0] * t + scaled[g][1] * l))
                if q < STEP:
                    cols[q] = moved
                else:
                    work = moved
        for g in range(groups):
            out.append(jnp.where(lane <= base + SUB * g + sub, done[g], 0.0))
        lines = [row(work[p // SUB], p % SUB) for p in range(STEP)]
        later = s + 2 * groups
        for i in range(s + groups, min(later, count)):
            change = tree([spread(rows[i], base + p) * lines[p] for p in range(STEP)])
            rows[i] = jnp.where(here, 0.0, rows[i]) - change
        if later < count:
            rest = jnp.concatenate(rows[later:], axis=0)
            inside = jnp.concatenate([here] * (count - later), axis=0)
            pieces = [jnp.zeros((base, LANES), F32)] if base else []
            pieces += work + [jnp.zeros((LANES - base - STEP, LANES), F32)]
            change = dot(jnp.where(inside, rest, 0.0), jnp.concatenate(pieces, axis=0))
            rest = jnp.where(inside, 0.0, rest) - change
            rows[later:] = [rest[SUB * i : SUB * (i + 1), :] for i in range(count - later)]
    return jnp.concatenate(out, axis=0) * SCALE**0.5


def blend(before, after):
    return 1.0 + RELAX * (jnp.sqrt(before / after) - 1.0)


def add_up(x):
    return jnp.sum(jnp.sum(x, axis=0, keepdims=True), axis=1, keepdims=True)


def dot3(a, b):
    a_high, a_low = split(a)
    b_high, b_low = split(b)
    left = jnp.concatenate([a_high, a_low, a_high], axis=1)
    return dot(left, jnp.concatenate([b_high, b_high, b_low], axis=0), precision=None)


def identity(size):
    return (
        lax.broadcasted_iota(jnp.int32, (size, size), 0) == lax.broadcasted_iota(jnp.int32, (size, size), 1)
    ).astype(F32)


def update_kernel(
    chunks, mine_v, other_v, mean_v, x_hbm, out_hbm, mean_out, full, x_buf, o_buf, in_sem, out_sem
):
    members = x_buf.shape[1]
    rows = x_buf.shape[0]
    size = rows // chunks
    pieces = [(0, size // 2)] + [(size // 2 + i * size, size) for i in range(chunks - 1)] + [(rows - size // 2, size // 2)]
    load, every_load = piece_copy(x_hbm, x_buf, in_sem, pieces)
    store, every_store = piece_copy(o_buf, out_hbm, out_sem, pieces)
    every_load(lambda copy: copy.start())

    mine = lax.axis_index(AXIS) & 1
    span = PACKED // 2
    full[pl.ds(pl.multiple_of(mine * span, SUB), span), :] = mine_v[...]
    full[pl.ds(pl.multiple_of((1 - mine) * span, SUB), span), :] = other_v[...]

    half = members // 2
    quarter = half // 2

    def block(at):
        return full[at : at + half, :]

    def innovation(k):
        count = OBS // INNOV_LANES
        at = INNOV + count * k
        return column(jnp.concatenate([full[at + j : at + j + 1, :INNOV_LANES] for j in range(count)], axis=1))

    first = jnp.concatenate([block(A0), block(A1)], axis=1)
    second = jnp.concatenate([block(B0), block(B1)], axis=1)
    g00, g01, top = block(G00), block(G01), full[G11:, :]
    line = lax.broadcasted_iota(jnp.int32, (half, half), 0)
    lane = lax.broadcasted_iota(jnp.int32, (half, half), 1)
    last = jnp.concatenate([jnp.zeros((quarter, quarter), F32), g00[quarter:, :quarter]], axis=1)
    corner = (line >= quarter) & (lane < quarter)
    g00 = jnp.where(corner, g00.T, g00)
    g11 = jnp.concatenate([top, last], axis=0)
    inner = (line >= INNOV - G00) & (lane >= quarter) & (lane < quarter + INNOV_LANES)
    g11 = jnp.where(corner | inner, g11.T, g11)
    gram = jnp.concatenate(
        [jnp.concatenate([g00, g01], axis=1), jnp.concatenate([g01.T, g11], axis=1)], axis=0
    )
    eye = identity(half)

    inv_m = factor(eye + dot(first, first, ((1,), (1,))))
    v_and_f = dot3(inv_m, jnp.concatenate([first, innovation(0)], axis=1))
    v, f = v_and_f[:, :members], v_and_f[:, members:]
    before = add_up(eye * (g00 + g11))
    after1 = before - add_up(dot3(v, gram) * v)
    factor1 = blend(before, after1)
    increment = jnp.sum(v * jnp.concatenate([f, f], axis=1), axis=0, keepdims=True)
    innov2 = innovation(1) - jnp.sum(second * increment, axis=1, keepdims=True)

    a1 = dot(first, first, ((0,), (0,)))
    a2 = dot(second, second, ((0,), (0,)))
    square = factor1 * factor1
    k00 = eye + a1[:half, :half] + a2[:half, :half] * square
    k10 = a1[half:, :half] + a2[half:, :half] * square
    k11 = eye + a1[half:, half:] + a2[half:, half:] * square
    inv00 = factor(k00)
    l10 = dot(k10, inv00, ((1,), (1,)))
    inv11 = factor(k11 - dot(l10, l10, ((1,), (1,))))
    inv10 = -dot(inv11, dot(l10, inv00))
    target = dot(second, innov2, ((0,), (0,))) * square
    y0 = dot3(inv00, target[:half, :])
    y1 = dot3(inv11, target[half:, :] - dot3(l10, y0))
    bottom = jnp.concatenate([inv10, inv11], axis=1)
    top_trace = add_up(dot3(inv00, g00) * inv00)
    after2 = top_trace + add_up(dot3(bottom, gram) * bottom)
    factor2 = factor1 * blend(after1, after2)
    increment0 = jnp.sum(y0 * inv00 + y1 * inv10, axis=0, keepdims=True)
    increment1 = jnp.sum(y1 * inv11, axis=0, keepdims=True)
    increment = increment + jnp.concatenate([increment0, increment1], axis=1)

    turned = jnp.concatenate(
        [jnp.concatenate([inv00.T, inv10.T], axis=1), jnp.concatenate([jnp.zeros_like(inv00), inv11.T], axis=1)], axis=0
    )
    high, low = split(turned)
    transform = jnp.concatenate([high, high, low], axis=0)
    step_line = lax.broadcasted_iota(jnp.int32, (LANES, LANES), 0)
    diagonal = step_line == lax.broadcasted_iota(jnp.int32, (LANES, LANES), 1)

    def apply(i, at, size):
        load(i, at, size).wait()
        x = x_buf[pl.ds(at, size), :]
        high, low = split(x)
        moved = dot(jnp.concatenate([high, low, high], axis=1), transform, precision=None)
        o_buf[pl.ds(at, size), :] = moved * factor2
        store(i, at, size).start()
        steps = jnp.sum(x * increment, axis=1, keepdims=True)
        for j in range(0, size, LANES):
            step = jnp.sum(jnp.where(diagonal, steps[j : j + LANES, :], 0.0), axis=0, keepdims=True)
            part = pl.ds(at + j, LANES)
            mean_out[:, part] = mean_v[:, part] + step

    apply(0, *pieces[0])

    def body(i, _):
        apply(i, pl.multiple_of(i * size - size // 2, size // 2), size)
        return 0

    lax.fori_loop(1, chunks, body, 0)
    apply(chunks, *pieces[-1])
    every_store(lambda copy: copy.wait())


def spec(space):
    return pl.BlockSpec(memory_space=space)


def params():
    return pltpu.CompilerParams(vmem_limit_bytes=VMEM_LIMIT)


def cost(flops, bytes_accessed):
    return pl.CostEstimate(flops=flops, bytes_accessed=bytes_accessed, transcendentals=0)


def cost(flops, bytes_accessed):
    return pl.CostEstimate(flops=flops, bytes_accessed=bytes_accessed, transcendentals=0)


def gram_of(ensemble):
    rows, members = ensemble.shape
    chunks = 4
    return pl.pallas_call(
        functools.partial(gram_kernel, chunks),
        out_shape=jax.ShapeDtypeStruct((PACKED - G00, LANES), F32),
        in_specs=[spec(pltpu.HBM)],
        out_specs=spec(pltpu.VMEM),
        scratch_shapes=[pltpu.VMEM((rows, members), F32), pltpu.SemaphoreType.DMA((chunks,))],
        cost_estimate=cost(4 * rows * members * members, 4 * rows * members),
        compiler_params=params(),
    )(ensemble)


def gather(ensemble, mean_state, observed, error_var, owner, obs_rows, gram):
    members = ensemble.shape[1]
    half = jax.ShapeDtypeStruct((PACKED // 2, LANES), F32)
    return pl.pallas_call(
        gather_kernel,
        out_shape=(half, half),
        in_specs=[spec(pltpu.SMEM), spec(pltpu.SMEM)] + [spec(pltpu.VMEM)] * 5 + [spec(pltpu.HBM)],
        out_specs=[spec(pltpu.VMEM)] * 2,
        scratch_shapes=[
            pltpu.VMEM((PACKED, LANES), F32),
            pltpu.VMEM((2, OBS, members), F32),
            pltpu.SemaphoreType.DMA((2,)),
        ],
        compiler_params=params(),
    )(owner, obs_rows, obs_rows, observed, error_var, mean_state.reshape(-1, LANES), gram, ensemble)


def update(packed, ensemble, mean_state):
    rows, members = ensemble.shape
    chunks = 4
    out, mean = pl.pallas_call(
        functools.partial(update_kernel, chunks),
        out_shape=(jax.ShapeDtypeStruct((rows, members), F32), jax.ShapeDtypeStruct((1, rows), F32)),
        in_specs=[spec(pltpu.VMEM)] * 3 + [spec(pltpu.HBM)],
        out_specs=(spec(pltpu.HBM), spec(pltpu.VMEM)),
        scratch_shapes=[
            pltpu.VMEM((PACKED, LANES), F32),
            pltpu.VMEM((rows, members), F32),
            pltpu.VMEM((rows, members), F32),
            pltpu.SemaphoreType.DMA((chunks + 1,)),
            pltpu.SemaphoreType.DMA((chunks + 1,)),
        ],
        compiler_params=params(),
    )(*packed, mean_state.reshape(1, rows), ensemble)
    return out, mean.reshape(rows)


def swap(value, count, mask):
    return lax.ppermute(value, AXIS, [(i, i ^ mask) for i in range(count)])


def total(keep, send, count):
    odd = ((lax.axis_index(AXIS) >> 1) & 1) == 1
    value = keep + swap(send, count, 1)
    low, high = jnp.split(value, 2, axis=0)
    value = jnp.where(odd, high, low) + swap(jnp.where(odd, low, high), count, 2)
    mask = 4
    while mask < count:
        value = value + swap(value, count, mask)
        mask *= 2
    got = swap(value, count, 2)
    value = jnp.concatenate([jnp.where(odd, got, value), jnp.where(odd, value, got)], axis=0)
    return value, swap(value, count, 1)


def on_device(count, ensemble, mean_state, observed, error_var, owner, obs_rows):
    gram = gram_of(ensemble)
    keep, send = gather(ensemble, mean_state, observed, error_var, owner, obs_rows, gram)
    return update(total(keep, send, count), ensemble, mean_state)


def solution(mesh):
    count = mesh.shape[AXIS]
    in_specs = (
        P(("groups", "rows"), None),
        P(("groups", "rows")),
        P("groups", None),
        P("groups", None),
        P("groups"),
        P("groups", None),
    )
    out_specs = (P(("groups", "rows"), None), P(("groups", "rows")))

    def body(*args):
        return on_device(count, *args)

    return jax.shard_map(body, mesh=mesh, in_specs=in_specs, out_specs=out_specs, check_vma=False)
```

```python
import functools

import jax
import jax.numpy as jnp
from jax import lax
from jax.experimental import pallas as pl
from jax.experimental.pallas import tpu as pltpu
from jax.sharding import PartitionSpec as P

RELAX = 0.6
HI = lax.Precision.HIGHEST
AXIS = "rows"
F32 = jnp.float32
BF16 = jnp.bfloat16
LANES = 128
SUB = 8
OBS = 128
VMEM_LIMIT = 51 * 1024 * 1024
STEP = 16
SCALE = 2.0**-16

A0, A1, B0, B1, G00, G01, G11 = range(0, 7 * 128, 128)
PACKED = G11 + 64
INNOV = G00 + 96
INNOV_LANES = 32


def dot(a, b, dims=((1,), (0,)), precision=HI):
    return lax.dot_general(a, b, (dims, ((), ())), precision=precision, preferred_element_type=F32)


def column(row):
    return jnp.broadcast_to(row, (LANES, LANES)).T


def split(x):
    high = x.astype(BF16)
    return high, (x - high.astype(F32)).astype(BF16)


def piece_copy(source, target, sem, pieces):
    def copy(i, at, size):
        part = pl.ds(at, size)
        return pltpu.make_async_copy(source.at[part], target.at[part], sem.at[i])

    def every(act):
        for i, (at, size) in enumerate(pieces):
            act(copy(i, at, size))

    return copy, every


def gram_kernel(x_hbm, out, x_buf, sem):
    rows, members = x_buf.shape
    half = members // 2
    quarter = rows // 4
    pieces = [(0, quarter), (quarter, quarter), (2 * quarter, rows - 2 * quarter)]
    load, every_load = piece_copy(x_hbm, x_buf, sem, pieces)
    every_load(lambda copy: copy.start())
    total = None
    for i, (at, size) in enumerate(pieces):
        load(i, at, size).wait()
        high, low = split(x_buf[at : at + size, :])
        part = dot(high, jnp.concatenate([high, low], axis=1), ((0,), (0,)), None)
        total = part if total is None else total + part
    cross = total[:, members:]
    total = total[:, :members] + cross + cross.T
    quarter = half // 2
    out[:quarter, :] = total[:quarter, :half]
    out[quarter:half, :] = jnp.concatenate(
        [total[half + quarter :, half + quarter :], total[quarter:half, quarter:half]], axis=1
    )
    out[half : 2 * half, :] = total[:half, half:]
    out[2 * half :, :] = total[half : half + quarter, half:]


def gather_kernel(
    owner_s, rows_s, rows_v, observed, error_var, mean_v, gram, x_hbm, keep, send, full, picked, sem
):
    me = lax.axis_index(AXIS)
    members = picked.shape[2]
    half = members // 2

    full[:G00, :] = jnp.zeros((G00, LANES), F32)
    full[G00:, :] = gram[...]
    full[INNOV : INNOV + 2 * OBS // INNOV_LANES, :INNOV_LANES] = jnp.zeros((2 * OBS // INNOV_LANES, INNOV_LANES), F32)
    lane = lax.broadcasted_iota(jnp.int32, (OBS, LANES), 1)

    for k, left, right in ((0, A0, A1), (1, B0, B1)):

        @pl.when(owner_s[k] == me)
        def _(k=k, left=left, right=right):
            for o in range(OBS):
                pltpu.make_async_copy(
                    x_hbm.at[pl.ds(rows_s[k, o], 1)], picked.at[k, pl.ds(o, 1)], sem.at[k]
                ).start()
            index = column(rows_v[k : k + 1, :].astype(F32)).astype(jnp.int32) - lane
            prior = jnp.zeros((OBS, LANES), F32)
            for r in range(mean_v.shape[0]):
                prior = prior + jnp.where(index == r * LANES, mean_v[r : r + 1, :], 0.0)
            prior = jnp.sum(prior.T, axis=0, keepdims=True)
            scale = lax.rsqrt(error_var[k : k + 1, :] * (members - 1.0))
            innov = scale * (observed[k : k + 1, :] - prior)
            count = OBS // INNOV_LANES
            for j in range(count):
                at = INNOV + count * k + j
                full[at : at + 1, :INNOV_LANES] = innov[:, j * INNOV_LANES : (j + 1) * INNOV_LANES]
            scales = column(scale)
            pltpu.make_async_copy(x_hbm.at[pl.ds(0, OBS)], picked.at[k], sem.at[k]).wait()
            full[left : left + OBS, :] = picked[k, :, :half] * scales
            full[right : right + OBS, :] = picked[k, :, half:] * scales

    mine = me & 1
    span = PACKED // 2
    keep[...] = full[pl.ds(pl.multiple_of(mine * span, SUB), span), :]
    send[...] = full[pl.ds(pl.multiple_of((1 - mine) * span, SUB), span), :]


def tree(terms):
    while len(terms) > 1:
        terms = [terms[i] + terms[i + 1] if i + 1 < len(terms) else terms[i] for i in range(0, len(terms), 2)]
    return terms[0]


def factor(a):
    a = a * SCALE
    count = LANES // SUB
    lane = lax.broadcasted_iota(jnp.int32, (SUB, LANES), 1)
    sub = lax.broadcasted_iota(jnp.int32, (SUB, LANES), 0)
    rows = [a[SUB * i : SUB * (i + 1), :] for i in range(count)]
    out = []

    def spread(x, c):
        return jnp.broadcast_to(x[:, c : c + 1], (SUB, LANES))

    def row(x, j):
        return jnp.broadcast_to(x[j : j + 1, :], (SUB, LANES))

    groups = STEP // SUB
    for s in range(0, count, groups):
        base = SUB * s
        here = (lane >= base) & (lane < base + STEP)
        cols = [[spread(rows[s + g], base + q) for g in range(groups)] for q in range(STEP)]
        work = [
            jnp.where(here, (lane - base == sub + SUB * g).astype(F32), rows[s + g]) for g in range(groups)
        ]
        done = [jnp.zeros((SUB, LANES), F32) for _ in range(groups)]
        for p in range(0, STEP, 2):
            at, j = divmod(p, SUB)
            first, second = sub == j, sub == j + 1
            pair = first | second
            pa, pb, pc = row(cols[p][at], j), row(cols[p][at], j + 1), row(cols[p + 1][at], j + 1)
            det = pa * pc - pb * pb
            if p % 4 == 0:
                inv = pl.reciprocal(det, approx=True)
                third, fourth = cols[p + 2][at], cols[p + 3][at]
                b00, b10, b01, b11 = row(third, j), row(third, j + 1), row(fourth, j), row(fourth, j + 1)
                w00, w10 = pc * b00 - pb * b10, pa * b10 - pb * b00
                w01, w11 = pc * b01 - pb * b11, pa * b11 - pb * b01
                s0 = det * row(third, j + 2) - (b00 * w00 + b10 * w10)
                s1 = det * row(third, j + 3) - (b00 * w01 + b10 * w11)
                s2 = det * row(fourth, j + 3) - (b01 * w01 + b11 * w11)
                next_inv = (det * det) * pl.reciprocal(s0 * s2 - s1 * s1, approx=True)
            else:
                inv = next_inv
            top, low = row(work[at], j), row(work[at], j + 1)
            done[at] = jnp.where(first, top * lax.rsqrt(pa), done[at])
            done[at] = jnp.where(second, (pa * low - pb * top) * lax.rsqrt(pa * det), done[at])
            raw, scaled = [], []
            for g in range(groups):
                m0, m1 = cols[p][g], cols[p + 1][g]
                if g == at:
                    m0 = jnp.where(first, -1.0, jnp.where(second, 0.0, m0))
                    m1 = jnp.where(second, -1.0, jnp.where(first, 0.0, m1))
                u0, u1 = m0 * pc - m1 * pb, m1 * pa - m0 * pb
                raw.append((u0, u1))
                scaled.append((u0 * inv, u1 * inv))
            for q in range(p + 2, STEP + 1):
                kept = cols[q] if q < STEP else work
                t, l = row(kept[at], j), row(kept[at], j + 1)
                moved = []
                for g in range(groups):
                    old = jnp.where(pair, 0.0, kept[g]) if g == at else kept[g]
                    if q < p + 4:
                        moved.append(old - (raw[g][0] * t + raw[g][1] * l) * inv)
                    else:
                        moved.append(old - (scaled[g][0] * t + scaled[g][1] * l))
                if q < STEP:
                    cols[q] = moved
                else:
                    work = moved
        for g in range(groups):
            out.append(jnp.where(lane <= base + SUB * g + sub, done[g], 0.0))
        lines = [row(work[p // SUB], p % SUB) for p in range(STEP)]
        later = s + 2 * groups
        for i in range(s + groups, min(later, count)):
            change = tree([spread(rows[i], base + p) * lines[p] for p in range(STEP)])
            rows[i] = jnp.where(here, 0.0, rows[i]) - change
        if later < count:
            rest = jnp.concatenate(rows[later:], axis=0)
            inside = jnp.concatenate([here] * (count - later), axis=0)
            pieces = [jnp.zeros((base, LANES), F32)] if base else []
            pieces += work + [jnp.zeros((LANES - base - STEP, LANES), F32)]
            change = dot(jnp.where(inside, rest, 0.0), jnp.concatenate(pieces, axis=0))
            rest = jnp.where(inside, 0.0, rest) - change
            rows[later:] = [rest[SUB * i : SUB * (i + 1), :] for i in range(count - later)]
    return jnp.concatenate(out, axis=0) * SCALE**0.5


def blend(before, after):
    return 1.0 + RELAX * (jnp.sqrt(before / after) - 1.0)


def add_up(x):
    return jnp.sum(jnp.sum(x, axis=0, keepdims=True), axis=1, keepdims=True)


def dot3(a, b):
    a_high, a_low = split(a)
    b_high, b_low = split(b)
    left = jnp.concatenate([a_high, a_low, a_high], axis=1)
    return dot(left, jnp.concatenate([b_high, b_high, b_low], axis=0), precision=None)


def identity(size):
    return (
        lax.broadcasted_iota(jnp.int32, (size, size), 0) == lax.broadcasted_iota(jnp.int32, (size, size), 1)
    ).astype(F32)


def update_kernel(
    chunks, mine_v, other_v, mean_v, x_hbm, out_hbm, mean_out, full, x_buf, o_buf, in_sem, out_sem
):
    members = x_buf.shape[1]
    rows = x_buf.shape[0]
    size = rows // chunks
    pieces = [(0, size // 2)] + [(size // 2 + i * size, size) for i in range(chunks - 1)] + [(rows - size // 2, size // 2)]
    load, every_load = piece_copy(x_hbm, x_buf, in_sem, pieces)
    store, every_store = piece_copy(o_buf, out_hbm, out_sem, pieces)
    every_load(lambda copy: copy.start())

    mine = lax.axis_index(AXIS) & 1
    span = PACKED // 2
    full[pl.ds(pl.multiple_of(mine * span, SUB), span), :] = mine_v[...]
    full[pl.ds(pl.multiple_of((1 - mine) * span, SUB), span), :] = other_v[...]

    half = members // 2
    quarter = half // 2

    def block(at):
        return full[at : at + half, :]

    def innovation(k):
        count = OBS // INNOV_LANES
        at = INNOV + count * k
        return column(jnp.concatenate([full[at + j : at + j + 1, :INNOV_LANES] for j in range(count)], axis=1))

    first = jnp.concatenate([block(A0), block(A1)], axis=1)
    second = jnp.concatenate([block(B0), block(B1)], axis=1)
    g00, g01, top = block(G00), block(G01), full[G11:, :]
    line = lax.broadcasted_iota(jnp.int32, (half, half), 0)
    lane = lax.broadcasted_iota(jnp.int32, (half, half), 1)
    last = jnp.concatenate([jnp.zeros((quarter, quarter), F32), g00[quarter:, :quarter]], axis=1)
    corner = (line >= quarter) & (lane < quarter)
    g00 = jnp.where(corner, g00.T, g00)
    g11 = jnp.concatenate([top, last], axis=0)
    inner = (line >= INNOV - G00) & (lane >= quarter) & (lane < quarter + INNOV_LANES)
    g11 = jnp.where(corner | inner, g11.T, g11)
    gram = jnp.concatenate(
        [jnp.concatenate([g00, g01], axis=1), jnp.concatenate([g01.T, g11], axis=1)], axis=0
    )
    eye = identity(half)

    inv_m = factor(eye + dot(first, first, ((1,), (1,))))
    v_and_f = dot3(inv_m, jnp.concatenate([first, innovation(0)], axis=1))
    v, f = v_and_f[:, :members], v_and_f[:, members:]
    before = add_up(eye * (g00 + g11))
    after1 = before - add_up(dot3(v, gram) * v)
    factor1 = blend(before, after1)
    increment = jnp.sum(v * jnp.concatenate([f, f], axis=1), axis=0, keepdims=True)
    innov2 = innovation(1) - jnp.sum(second * increment, axis=1, keepdims=True)

    a1 = dot(first, first, ((0,), (0,)))
    a2 = dot(second, second, ((0,), (0,)))
    square = factor1 * factor1
    k00 = eye + a1[:half, :half] + a2[:half, :half] * square
    k10 = a1[half:, :half] + a2[half:, :half] * square
    k11 = eye + a1[half:, half:] + a2[half:, half:] * square
    inv00 = factor(k00)
    l10 = dot(k10, inv00, ((1,), (1,)))
    inv11 = factor(k11 - dot(l10, l10, ((1,), (1,))))
    inv10 = -dot(inv11, dot(l10, inv00))
    target = dot(second, innov2, ((0,), (0,))) * square
    y0 = dot3(inv00, target[:half, :])
    y1 = dot3(inv11, target[half:, :] - dot3(l10, y0))
    bottom = jnp.concatenate([inv10, inv11], axis=1)
    top_trace = add_up(dot3(inv00, g00) * inv00)
    after2 = top_trace + add_up(dot3(bottom, gram) * bottom)
    factor2 = factor1 * blend(after1, after2)
    increment0 = jnp.sum(y0 * inv00 + y1 * inv10, axis=0, keepdims=True)
    increment1 = jnp.sum(y1 * inv11, axis=0, keepdims=True)
    increment = increment + jnp.concatenate([increment0, increment1], axis=1)

    turned = jnp.concatenate(
        [jnp.concatenate([inv00.T, inv10.T], axis=1), jnp.concatenate([jnp.zeros_like(inv00), inv11.T], axis=1)], axis=0
    )
    high, low = split(turned)
    transform = jnp.concatenate([high, high, low], axis=0)
    step_line = lax.broadcasted_iota(jnp.int32, (LANES, LANES), 0)
    diagonal = step_line == lax.broadcasted_iota(jnp.int32, (LANES, LANES), 1)

    def apply(i, at, size):
        load(i, at, size).wait()
        x = x_buf[pl.ds(at, size), :]
        high, low = split(x)
        moved = dot(jnp.concatenate([high, low, high], axis=1), transform, precision=None)
        o_buf[pl.ds(at, size), :] = moved * factor2
        store(i, at, size).start()
        steps = jnp.sum(x * increment, axis=1, keepdims=True)
        for j in range(0, size, LANES):
            step = jnp.sum(jnp.where(diagonal, steps[j : j + LANES, :], 0.0), axis=0, keepdims=True)
            part = pl.ds(at + j, LANES)
            mean_out[:, part] = mean_v[:, part] + step

    apply(0, *pieces[0])

    def body(i, _):
        apply(i, pl.multiple_of(i * size - size // 2, size // 2), size)
        return 0

    lax.fori_loop(1, chunks, body, 0)
    apply(chunks, *pieces[-1])
    every_store(lambda copy: copy.wait())


def spec(space):
    return pl.BlockSpec(memory_space=space)


def params():
    return pltpu.CompilerParams(vmem_limit_bytes=VMEM_LIMIT)


def cost(flops, bytes_accessed):
    return pl.CostEstimate(flops=flops, bytes_accessed=bytes_accessed, transcendentals=0)


def cost(flops, bytes_accessed):
    return pl.CostEstimate(flops=flops, bytes_accessed=bytes_accessed, transcendentals=0)


def gram_of(ensemble):
    rows, members = ensemble.shape
    return pl.pallas_call(
        gram_kernel,
        out_shape=jax.ShapeDtypeStruct((PACKED - G00, LANES), F32),
        in_specs=[spec(pltpu.HBM)],
        out_specs=spec(pltpu.VMEM),
        scratch_shapes=[pltpu.VMEM((rows, members), F32), pltpu.SemaphoreType.DMA((3,))],
        cost_estimate=cost(4 * rows * members * members, 4 * rows * members),
        compiler_params=params(),
    )(ensemble)


def gather(ensemble, mean_state, observed, error_var, owner, obs_rows, gram):
    members = ensemble.shape[1]
    half = jax.ShapeDtypeStruct((PACKED // 2, LANES), F32)
    return pl.pallas_call(
        gather_kernel,
        out_shape=(half, half),
        in_specs=[spec(pltpu.SMEM), spec(pltpu.SMEM)] + [spec(pltpu.VMEM)] * 5 + [spec(pltpu.HBM)],
        out_specs=[spec(pltpu.VMEM)] * 2,
        scratch_shapes=[
            pltpu.VMEM((PACKED, LANES), F32),
            pltpu.VMEM((2, OBS, members), F32),
            pltpu.SemaphoreType.DMA((2,)),
        ],
        compiler_params=params(),
    )(owner, obs_rows, obs_rows, observed, error_var, mean_state.reshape(-1, LANES), gram, ensemble)


def update(packed, ensemble, mean_state):
    rows, members = ensemble.shape
    chunks = 4
    out, mean = pl.pallas_call(
        functools.partial(update_kernel, chunks),
        out_shape=(jax.ShapeDtypeStruct((rows, members), F32), jax.ShapeDtypeStruct((1, rows), F32)),
        in_specs=[spec(pltpu.VMEM)] * 3 + [spec(pltpu.HBM)],
        out_specs=(spec(pltpu.HBM), spec(pltpu.VMEM)),
        scratch_shapes=[
            pltpu.VMEM((PACKED, LANES), F32),
            pltpu.VMEM((rows, members), F32),
            pltpu.VMEM((rows, members), F32),
            pltpu.SemaphoreType.DMA((chunks + 1,)),
            pltpu.SemaphoreType.DMA((chunks + 1,)),
        ],
        compiler_params=params(),
    )(*packed, mean_state.reshape(1, rows), ensemble)
    return out, mean.reshape(rows)


def swap(value, count, mask):
    return lax.ppermute(value, AXIS, [(i, i ^ mask) for i in range(count)])


def total(keep, send, count):
    odd = ((lax.axis_index(AXIS) >> 1) & 1) == 1
    value = keep + swap(send, count, 1)
    low, high = jnp.split(value, 2, axis=0)
    value = jnp.where(odd, high, low) + swap(jnp.where(odd, low, high), count, 2)
    mask = 4
    while mask < count:
        value = value + swap(value, count, mask)
        mask *= 2
    got = swap(value, count, 2)
    value = jnp.concatenate([jnp.where(odd, got, value), jnp.where(odd, value, got)], axis=0)
    return value, swap(value, count, 1)


def on_device(count, ensemble, mean_state, observed, error_var, owner, obs_rows):
    gram = gram_of(ensemble)
    keep, send = gather(ensemble, mean_state, observed, error_var, owner, obs_rows, gram)
    return update(total(keep, send, count), ensemble, mean_state)


def solution(mesh):
    count = mesh.shape[AXIS]
    in_specs = (
        P(("groups", "rows"), None),
        P(("groups", "rows")),
        P("groups", None),
        P("groups", None),
        P("groups"),
        P("groups", None),
    )
    out_specs = (P(("groups", "rows"), None), P(("groups", "rows")))

    def body(*args):
        return on_device(count, *args)

    return jax.shard_map(body, mesh=mesh, in_specs=in_specs, out_specs=out_specs, check_vma=False)
```

```python
import functools

import jax
import jax.numpy as jnp
from jax import lax
from jax.experimental import pallas as pl
from jax.experimental.pallas import tpu as pltpu
from jax.sharding import PartitionSpec as P

RELAX = 0.6
HI = lax.Precision.HIGHEST
AXIS = "rows"
F32 = jnp.float32
BF16 = jnp.bfloat16
LANES = 128
SUB = 8
OBS = 128
VMEM_LIMIT = 51 * 1024 * 1024
STEP = 16
SCALE = 2.0**-16

A0, A1, B0, B1, G00, G01, G11 = range(0, 7 * 128, 128)
PACKED = G11 + 64
INNOV = G00 + 96
INNOV_LANES = 32


def dot(a, b, dims=((1,), (0,)), precision=HI):
    return lax.dot_general(a, b, (dims, ((), ())), precision=precision, preferred_element_type=F32)


def column(row):
    return jnp.broadcast_to(row, (LANES, LANES)).T


def split(x):
    high = x.astype(BF16)
    return high, (x - high.astype(F32)).astype(BF16)


def piece_copy(source, target, sem, pieces):
    def copy(i, at, size):
        part = pl.ds(at, size)
        return pltpu.make_async_copy(source.at[part], target.at[part], sem.at[i])

    def every(act):
        for i, (at, size) in enumerate(pieces):
            act(copy(i, at, size))

    return copy, every


def gram_kernel(x_hbm, out, x_buf, sem):
    rows, members = x_buf.shape
    half = members // 2
    quarter = rows // 4
    pieces = [(0, quarter), (quarter, quarter), (2 * quarter, rows - 2 * quarter)]
    load, every_load = piece_copy(x_hbm, x_buf, sem, pieces)
    every_load(lambda copy: copy.start())
    total = None
    for i, (at, size) in enumerate(pieces):
        load(i, at, size).wait()
        high, low = split(x_buf[at : at + size, :])
        part = dot(high, jnp.concatenate([high, low], axis=1), ((0,), (0,)), None)
        total = part if total is None else total + part
    cross = total[:, members:]
    total = total[:, :members] + cross + cross.T
    quarter = half // 2
    out[:quarter, :] = total[:quarter, :half]
    out[quarter:half, :] = jnp.concatenate(
        [total[half + quarter :, half + quarter :], total[quarter:half, quarter:half]], axis=1
    )
    out[half : 2 * half, :] = total[:half, half:]
    out[2 * half :, :] = total[half : half + quarter, half:]


def gather_kernel(
    owner_s, rows_s, rows_v, observed, error_var, mean_v, gram, x_hbm, keep, send, full, picked, sem
):
    me = lax.axis_index(AXIS)
    members = picked.shape[2]
    half = members // 2

    full[:G00, :] = jnp.zeros((G00, LANES), F32)
    full[G00:, :] = gram[...]
    full[INNOV : INNOV + 2 * OBS // INNOV_LANES, :INNOV_LANES] = jnp.zeros((2 * OBS // INNOV_LANES, INNOV_LANES), F32)
    lane = lax.broadcasted_iota(jnp.int32, (OBS, LANES), 1)

    for k, left, right in ((0, A0, A1), (1, B0, B1)):

        @pl.when(owner_s[k] == me)
        def _(k=k, left=left, right=right):
            for o in range(OBS):
                pltpu.make_async_copy(
                    x_hbm.at[pl.ds(rows_s[k, o], 1)], picked.at[k, pl.ds(o, 1)], sem.at[k]
                ).start(priority=o % 2)
            index = column(rows_v[k : k + 1, :].astype(F32)).astype(jnp.int32) - lane
            prior = jnp.zeros((OBS, LANES), F32)
            for r in range(mean_v.shape[0]):
                prior = prior + jnp.where(index == r * LANES, mean_v[r : r + 1, :], 0.0)
            prior = jnp.sum(prior.T, axis=0, keepdims=True)
            scale = lax.rsqrt(error_var[k : k + 1, :] * (members - 1.0))
            innov = scale * (observed[k : k + 1, :] - prior)
            count = OBS // INNOV_LANES
            for j in range(count):
                at = INNOV + count * k + j
                full[at : at + 1, :INNOV_LANES] = innov[:, j * INNOV_LANES : (j + 1) * INNOV_LANES]
            scales = column(scale)
            pltpu.make_async_copy(x_hbm.at[pl.ds(0, OBS)], picked.at[k], sem.at[k]).wait()
            full[left : left + OBS, :] = picked[k, :, :half] * scales
            full[right : right + OBS, :] = picked[k, :, half:] * scales

    mine = me & 1
    span = PACKED // 2
    keep[...] = full[pl.ds(pl.multiple_of(mine * span, SUB), span), :]
    send[...] = full[pl.ds(pl.multiple_of((1 - mine) * span, SUB), span), :]


def tree(terms):
    while len(terms) > 1:
        terms = [terms[i] + terms[i + 1] if i + 1 < len(terms) else terms[i] for i in range(0, len(terms), 2)]
    return terms[0]


def factor(a):
    a = a * SCALE
    count = LANES // SUB
    lane = lax.broadcasted_iota(jnp.int32, (SUB, LANES), 1)
    sub = lax.broadcasted_iota(jnp.int32, (SUB, LANES), 0)
    rows = [a[SUB * i : SUB * (i + 1), :] for i in range(count)]
    out = []

    def spread(x, c):
        return jnp.broadcast_to(x[:, c : c + 1], (SUB, LANES))

    def row(x, j):
        return jnp.broadcast_to(x[j : j + 1, :], (SUB, LANES))

    groups = STEP // SUB
    for s in range(0, count, groups):
        base = SUB * s
        here = (lane >= base) & (lane < base + STEP)
        cols = [[spread(rows[s + g], base + q) for g in range(groups)] for q in range(STEP)]
        work = [
            jnp.where(here, (lane - base == sub + SUB * g).astype(F32), rows[s + g]) for g in range(groups)
        ]
        done = [jnp.zeros((SUB, LANES), F32) for _ in range(groups)]
        for p in range(0, STEP, 2):
            at, j = divmod(p, SUB)
            first, second = sub == j, sub == j + 1
            pair = first | second
            pa, pb, pc = row(cols[p][at], j), row(cols[p][at], j + 1), row(cols[p + 1][at], j + 1)
            det = pa * pc - pb * pb
            if p % 4 == 0:
                inv = pl.reciprocal(det, approx=True)
                third, fourth = cols[p + 2][at], cols[p + 3][at]
                b00, b10, b01, b11 = row(third, j), row(third, j + 1), row(fourth, j), row(fourth, j + 1)
                w00, w10 = pc * b00 - pb * b10, pa * b10 - pb * b00
                w01, w11 = pc * b01 - pb * b11, pa * b11 - pb * b01
                s0 = det * row(third, j + 2) - (b00 * w00 + b10 * w10)
                s1 = det * row(third, j + 3) - (b00 * w01 + b10 * w11)
                s2 = det * row(fourth, j + 3) - (b01 * w01 + b11 * w11)
                next_inv = (det * det) * pl.reciprocal(s0 * s2 - s1 * s1, approx=True)
            else:
                inv = next_inv
            top, low = row(work[at], j), row(work[at], j + 1)
            done[at] = jnp.where(first, top * lax.rsqrt(pa), done[at])
            done[at] = jnp.where(second, (pa * low - pb * top) * lax.rsqrt(pa * det), done[at])
            raw, scaled = [], []
            for g in range(groups):
                m0, m1 = cols[p][g], cols[p + 1][g]
                if g == at:
                    m0 = jnp.where(first, -1.0, jnp.where(second, 0.0, m0))
                    m1 = jnp.where(second, -1.0, jnp.where(first, 0.0, m1))
                u0, u1 = m0 * pc - m1 * pb, m1 * pa - m0 * pb
                raw.append((u0, u1))
                scaled.append((u0 * inv, u1 * inv))
            for q in range(p + 2, STEP + 1):
                kept = cols[q] if q < STEP else work
                t, l = row(kept[at], j), row(kept[at], j + 1)
                moved = []
                for g in range(groups):
                    old = jnp.where(pair, 0.0, kept[g]) if g == at else kept[g]
                    if q < p + 4:
                        moved.append(old - (raw[g][0] * t + raw[g][1] * l) * inv)
                    else:
                        moved.append(old - (scaled[g][0] * t + scaled[g][1] * l))
                if q < STEP:
                    cols[q] = moved
                else:
                    work = moved
        for g in range(groups):
            out.append(jnp.where(lane <= base + SUB * g + sub, done[g], 0.0))
        lines = [row(work[p // SUB], p % SUB) for p in range(STEP)]
        later = s + 2 * groups
        for i in range(s + groups, min(later, count)):
            change = tree([spread(rows[i], base + p) * lines[p] for p in range(STEP)])
            rows[i] = jnp.where(here, 0.0, rows[i]) - change
        if later < count:
            rest = jnp.concatenate(rows[later:], axis=0)
            inside = jnp.concatenate([here] * (count - later), axis=0)
            pieces = [jnp.zeros((base, LANES), F32)] if base else []
            pieces += work + [jnp.zeros((LANES - base - STEP, LANES), F32)]
            change = dot(jnp.where(inside, rest, 0.0), jnp.concatenate(pieces, axis=0))
            rest = jnp.where(inside, 0.0, rest) - change
            rows[later:] = [rest[SUB * i : SUB * (i + 1), :] for i in range(count - later)]
    return jnp.concatenate(out, axis=0) * SCALE**0.5


def blend(before, after):
    return 1.0 + RELAX * (jnp.sqrt(before / after) - 1.0)


def add_up(x):
    return jnp.sum(jnp.sum(x, axis=0, keepdims=True), axis=1, keepdims=True)


def dot3(a, b):
    a_high, a_low = split(a)
    b_high, b_low = split(b)
    left = jnp.concatenate([a_high, a_low, a_high], axis=1)
    return dot(left, jnp.concatenate([b_high, b_high, b_low], axis=0), precision=None)


def identity(size):
    return (
        lax.broadcasted_iota(jnp.int32, (size, size), 0) == lax.broadcasted_iota(jnp.int32, (size, size), 1)
    ).astype(F32)


def update_kernel(
    chunks, mine_v, other_v, mean_v, x_hbm, out_hbm, mean_out, full, x_buf, o_buf, in_sem, out_sem
):
    members = x_buf.shape[1]
    rows = x_buf.shape[0]
    size = rows // chunks
    pieces = [(0, size // 2)] + [(size // 2 + i * size, size) for i in range(chunks - 1)] + [(rows - size // 2, size // 2)]
    load, every_load = piece_copy(x_hbm, x_buf, in_sem, pieces)
    store, every_store = piece_copy(o_buf, out_hbm, out_sem, pieces)
    every_load(lambda copy: copy.start())

    mine = lax.axis_index(AXIS) & 1
    span = PACKED // 2
    full[pl.ds(pl.multiple_of(mine * span, SUB), span), :] = mine_v[...]
    full[pl.ds(pl.multiple_of((1 - mine) * span, SUB), span), :] = other_v[...]

    half = members // 2
    quarter = half // 2

    def block(at):
        return full[at : at + half, :]

    def innovation(k):
        count = OBS // INNOV_LANES
        at = INNOV + count * k
        return column(jnp.concatenate([full[at + j : at + j + 1, :INNOV_LANES] for j in range(count)], axis=1))

    first = jnp.concatenate([block(A0), block(A1)], axis=1)
    second = jnp.concatenate([block(B0), block(B1)], axis=1)
    g00, g01, top = block(G00), block(G01), full[G11:, :]
    line = lax.broadcasted_iota(jnp.int32, (half, half), 0)
    lane = lax.broadcasted_iota(jnp.int32, (half, half), 1)
    last = jnp.concatenate([jnp.zeros((quarter, quarter), F32), g00[quarter:, :quarter]], axis=1)
    corner = (line >= quarter) & (lane < quarter)
    g00 = jnp.where(corner, g00.T, g00)
    g11 = jnp.concatenate([top, last], axis=0)
    inner = (line >= INNOV - G00) & (lane >= quarter) & (lane < quarter + INNOV_LANES)
    g11 = jnp.where(corner | inner, g11.T, g11)
    gram = jnp.concatenate(
        [jnp.concatenate([g00, g01], axis=1), jnp.concatenate([g01.T, g11], axis=1)], axis=0
    )
    eye = identity(half)

    inv_m = factor(eye + dot(first, first, ((1,), (1,))))
    v_and_f = dot3(inv_m, jnp.concatenate([first, innovation(0)], axis=1))
    v, f = v_and_f[:, :members], v_and_f[:, members:]
    before = add_up(eye * (g00 + g11))
    after1 = before - add_up(dot3(v, gram) * v)
    factor1 = blend(before, after1)
    increment = jnp.sum(v * jnp.concatenate([f, f], axis=1), axis=0, keepdims=True)
    innov2 = innovation(1) - jnp.sum(second * increment, axis=1, keepdims=True)

    a1 = dot(first, first, ((0,), (0,)))
    a2 = dot(second, second, ((0,), (0,)))
    square = factor1 * factor1
    k00 = eye + a1[:half, :half] + a2[:half, :half] * square
    k10 = a1[half:, :half] + a2[half:, :half] * square
    k11 = eye + a1[half:, half:] + a2[half:, half:] * square
    inv00 = factor(k00)
    l10 = dot(k10, inv00, ((1,), (1,)))
    inv11 = factor(k11 - dot(l10, l10, ((1,), (1,))))
    inv10 = -dot(inv11, dot(l10, inv00))
    target = dot(second, innov2, ((0,), (0,))) * square
    y0 = dot3(inv00, target[:half, :])
    y1 = dot3(inv11, target[half:, :] - dot3(l10, y0))
    bottom = jnp.concatenate([inv10, inv11], axis=1)
    top_trace = add_up(dot3(inv00, g00) * inv00)
    after2 = top_trace + add_up(dot3(bottom, gram) * bottom)
    factor2 = factor1 * blend(after1, after2)
    increment0 = jnp.sum(y0 * inv00 + y1 * inv10, axis=0, keepdims=True)
    increment1 = jnp.sum(y1 * inv11, axis=0, keepdims=True)
    increment = increment + jnp.concatenate([increment0, increment1], axis=1)

    turned = jnp.concatenate(
        [jnp.concatenate([inv00.T, inv10.T], axis=1), jnp.concatenate([jnp.zeros_like(inv00), inv11.T], axis=1)], axis=0
    )

    def stacked(x):
        high, low = split(x)
        return jnp.concatenate([high, high, low], axis=0)

    step_line = lax.broadcasted_iota(jnp.int32, (LANES, LANES), 0)
    diagonal = step_line == lax.broadcasted_iota(jnp.int32, (LANES, LANES), 1)

    def apply(i, at, size, transform, scale):
        load(i, at, size).wait()
        x = x_buf[pl.ds(at, size), :]
        high, low = split(x)
        moved = dot(jnp.concatenate([high, low, high], axis=1), transform, precision=None)
        o_buf[pl.ds(at, size), :] = moved if scale is None else moved * scale
        store(i, at, size).start()
        steps = jnp.sum(x * increment, axis=1, keepdims=True)
        for j in range(0, size, LANES):
            step = jnp.sum(jnp.where(diagonal, steps[j : j + LANES, :], 0.0), axis=0, keepdims=True)
            part = pl.ds(at + j, LANES)
            mean_out[:, part] = mean_v[:, part] + step

    apply(0, *pieces[0], stacked(turned), factor2)
    scaled = stacked(turned * factor2)

    def body(i, _):
        apply(i, pl.multiple_of(i * size - size // 2, size // 2), size, scaled, None)
        return 0

    lax.fori_loop(1, chunks, body, 0)
    apply(chunks, *pieces[-1], scaled, None)
    every_store(lambda copy: copy.wait())


def spec(space):
    return pl.BlockSpec(memory_space=space)


def params():
    return pltpu.CompilerParams(vmem_limit_bytes=VMEM_LIMIT)


def cost(flops, bytes_accessed):
    return pl.CostEstimate(flops=flops, bytes_accessed=bytes_accessed, transcendentals=0)


def cost(flops, bytes_accessed):
    return pl.CostEstimate(flops=flops, bytes_accessed=bytes_accessed, transcendentals=0)


def gram_of(ensemble):
    rows, members = ensemble.shape
    return pl.pallas_call(
        gram_kernel,
        out_shape=jax.ShapeDtypeStruct((PACKED - G00, LANES), F32),
        in_specs=[spec(pltpu.HBM)],
        out_specs=spec(pltpu.VMEM),
        scratch_shapes=[pltpu.VMEM((rows, members), F32), pltpu.SemaphoreType.DMA((3,))],
        cost_estimate=cost(4 * rows * members * members, 4 * rows * members),
        compiler_params=params(),
    )(ensemble)


def gather(ensemble, mean_state, observed, error_var, owner, obs_rows, gram):
    members = ensemble.shape[1]
    half = jax.ShapeDtypeStruct((PACKED // 2, LANES), F32)
    return pl.pallas_call(
        gather_kernel,
        out_shape=(half, half),
        in_specs=[spec(pltpu.SMEM), spec(pltpu.SMEM)] + [spec(pltpu.VMEM)] * 5 + [spec(pltpu.HBM)],
        out_specs=[spec(pltpu.VMEM)] * 2,
        scratch_shapes=[
            pltpu.VMEM((PACKED, LANES), F32),
            pltpu.VMEM((2, OBS, members), F32),
            pltpu.SemaphoreType.DMA((2,)),
        ],
        compiler_params=params(),
    )(owner, obs_rows, obs_rows, observed, error_var, mean_state.reshape(-1, LANES), gram, ensemble)


def update(packed, ensemble, mean_state):
    rows, members = ensemble.shape
    chunks = 4
    out, mean = pl.pallas_call(
        functools.partial(update_kernel, chunks),
        out_shape=(jax.ShapeDtypeStruct((rows, members), F32), jax.ShapeDtypeStruct((1, rows), F32)),
        in_specs=[spec(pltpu.VMEM)] * 3 + [spec(pltpu.HBM)],
        out_specs=(spec(pltpu.HBM), spec(pltpu.VMEM)),
        scratch_shapes=[
            pltpu.VMEM((PACKED, LANES), F32),
            pltpu.VMEM((rows, members), F32),
            pltpu.VMEM((rows, members), F32),
            pltpu.SemaphoreType.DMA((chunks + 1,)),
            pltpu.SemaphoreType.DMA((chunks + 1,)),
        ],
        compiler_params=params(),
    )(*packed, mean_state.reshape(1, rows), ensemble)
    return out, mean.reshape(rows)


def swap(value, count, mask):
    return lax.ppermute(value, AXIS, [(i, i ^ mask) for i in range(count)])


def total(keep, send, count):
    odd = ((lax.axis_index(AXIS) >> 1) & 1) == 1
    value = keep + swap(send, count, 1)
    low, high = jnp.split(value, 2, axis=0)
    value = jnp.where(odd, high, low) + swap(jnp.where(odd, low, high), count, 2)
    mask = 4
    while mask < count:
        value = value + swap(value, count, mask)
        mask *= 2
    got = swap(value, count, 2)
    value = jnp.concatenate([jnp.where(odd, got, value), jnp.where(odd, value, got)], axis=0)
    return value, swap(value, count, 1)


def on_device(count, ensemble, mean_state, observed, error_var, owner, obs_rows):
    gram = gram_of(ensemble)
    keep, send = gather(ensemble, mean_state, observed, error_var, owner, obs_rows, gram)
    return update(total(keep, send, count), ensemble, mean_state)


def solution(mesh):
    count = mesh.shape[AXIS]
    in_specs = (
        P(("groups", "rows"), None),
        P(("groups", "rows")),
        P("groups", None),
        P("groups", None),
        P("groups"),
        P("groups", None),
    )
    out_specs = (P(("groups", "rows"), None), P(("groups", "rows")))

    def body(*args):
        return on_device(count, *args)

    return jax.shard_map(body, mesh=mesh, in_specs=in_specs, out_specs=out_specs, check_vma=False)
```

```python
import functools

import jax
import jax.numpy as jnp
from jax import lax
from jax.experimental import pallas as pl
from jax.experimental.pallas import tpu as pltpu
from jax.sharding import PartitionSpec as P

RELAX = 0.6
HI = lax.Precision.HIGHEST
AXIS = "rows"
F32 = jnp.float32
BF16 = jnp.bfloat16
LANES = 128
SUB = 8
OBS = 128
VMEM_LIMIT = 51 * 1024 * 1024
STEP = 16
SCALE = 2.0**-16

A0, A1, B0, B1, G00, G01, G11 = range(0, 7 * 128, 128)
PACKED = G11 + 64
INNOV = G00 + 96
INNOV_LANES = 32


def dot(a, b, dims=((1,), (0,)), precision=HI):
    return lax.dot_general(a, b, (dims, ((), ())), precision=precision, preferred_element_type=F32)


def column(row):
    return jnp.broadcast_to(row, (LANES, LANES)).T


def split(x):
    high = x.astype(BF16)
    return high, (x - high.astype(F32)).astype(BF16)


def piece_copy(source, target, sem, pieces):
    def copy(i, at, size):
        part = pl.ds(at, size)
        return pltpu.make_async_copy(source.at[part], target.at[part], sem.at[i])

    def every(act):
        for i, (at, size) in enumerate(pieces):
            act(copy(i, at, size))

    return copy, every


def gram_kernel(x_hbm, out, x_buf, sem):
    rows, members = x_buf.shape
    half = members // 2
    cut = 3 * rows // 8
    pieces = [(0, cut), (cut, rows - cut)]
    load, every_load = piece_copy(x_hbm, x_buf, sem, pieces)
    every_load(lambda copy: copy.start())
    total = None
    for i, (at, size) in enumerate(pieces):
        load(i, at, size).wait()
        high, low = split(x_buf[at : at + size, :])
        part = dot(high, jnp.concatenate([high, low], axis=1), ((0,), (0,)), None)
        total = part if total is None else total + part
    cross = total[:, members:]
    total = total[:, :members] + cross + cross.T
    quarter = half // 2
    out[:quarter, :] = total[:quarter, :half]
    out[quarter:half, :] = jnp.concatenate(
        [total[half + quarter :, half + quarter :], total[quarter:half, quarter:half]], axis=1
    )
    out[half : 2 * half, :] = total[:half, half:]
    out[2 * half :, :] = total[half : half + quarter, half:]


def gather_kernel(
    owner_s, rows_s, rows_v, observed, error_var, mean_v, gram, x_hbm, keep, send, full, picked, sem
):
    me = lax.axis_index(AXIS)
    members = picked.shape[2]
    half = members // 2

    full[:G00, :] = jnp.zeros((G00, LANES), F32)
    full[G00:, :] = gram[...]
    full[INNOV : INNOV + 2 * OBS // INNOV_LANES, :INNOV_LANES] = jnp.zeros((2 * OBS // INNOV_LANES, INNOV_LANES), F32)
    lane = lax.broadcasted_iota(jnp.int32, (OBS, LANES), 1)

    for k, left, right in ((0, A0, A1), (1, B0, B1)):

        @pl.when(owner_s[k] == me)
        def _(k=k, left=left, right=right):
            for o in range(OBS):
                pltpu.make_async_copy(
                    x_hbm.at[pl.ds(rows_s[k, o], 1)], picked.at[k, pl.ds(o, 1)], sem.at[k]
                ).start(priority=o % 2)
            index = column(rows_v[k : k + 1, :].astype(F32)).astype(jnp.int32) - lane
            prior = jnp.zeros((OBS, LANES), F32)
            for r in range(mean_v.shape[0]):
                prior = prior + jnp.where(index == r * LANES, mean_v[r : r + 1, :], 0.0)
            prior = jnp.sum(prior.T, axis=0, keepdims=True)
            scale = lax.rsqrt(error_var[k : k + 1, :] * (members - 1.0))
            innov = scale * (observed[k : k + 1, :] - prior)
            count = OBS // INNOV_LANES
            for j in range(count):
                at = INNOV + count * k + j
                full[at : at + 1, :INNOV_LANES] = innov[:, j * INNOV_LANES : (j + 1) * INNOV_LANES]
            scales = column(scale)
            pltpu.make_async_copy(x_hbm.at[pl.ds(0, OBS)], picked.at[k], sem.at[k]).wait()
            full[left : left + OBS, :] = picked[k, :, :half] * scales
            full[right : right + OBS, :] = picked[k, :, half:] * scales

    mine = me & 1
    span = PACKED // 2
    keep[...] = full[pl.ds(pl.multiple_of(mine * span, SUB), span), :]
    send[...] = full[pl.ds(pl.multiple_of((1 - mine) * span, SUB), span), :]


def tree(terms):
    while len(terms) > 1:
        terms = [terms[i] + terms[i + 1] if i + 1 < len(terms) else terms[i] for i in range(0, len(terms), 2)]
    return terms[0]


def factor(a):
    a = a * SCALE
    count = LANES // SUB
    lane = lax.broadcasted_iota(jnp.int32, (SUB, LANES), 1)
    sub = lax.broadcasted_iota(jnp.int32, (SUB, LANES), 0)
    rows = [a[SUB * i : SUB * (i + 1), :] for i in range(count)]
    out = []

    def spread(x, c):
        return jnp.broadcast_to(x[:, c : c + 1], (SUB, LANES))

    def row(x, j):
        return jnp.broadcast_to(x[j : j + 1, :], (SUB, LANES))

    groups = STEP // SUB
    for s in range(0, count, groups):
        base = SUB * s
        here = (lane >= base) & (lane < base + STEP)
        cols = [[spread(rows[s + g], base + q) for g in range(groups)] for q in range(STEP)]
        work = [
            jnp.where(here, (lane - base == sub + SUB * g).astype(F32), rows[s + g]) for g in range(groups)
        ]
        done = [jnp.zeros((SUB, LANES), F32) for _ in range(groups)]
        for p in range(0, STEP, 2):
            at, j = divmod(p, SUB)
            first, second = sub == j, sub == j + 1
            pair = first | second
            pa, pb, pc = row(cols[p][at], j), row(cols[p][at], j + 1), row(cols[p + 1][at], j + 1)
            det = pa * pc - pb * pb
            if p % 4 == 0:
                inv = pl.reciprocal(det, approx=True)
                third, fourth = cols[p + 2][at], cols[p + 3][at]
                b00, b10, b01, b11 = row(third, j), row(third, j + 1), row(fourth, j), row(fourth, j + 1)
                w00, w10 = pc * b00 - pb * b10, pa * b10 - pb * b00
                w01, w11 = pc * b01 - pb * b11, pa * b11 - pb * b01
                s0 = det * row(third, j + 2) - (b00 * w00 + b10 * w10)
                s1 = det * row(third, j + 3) - (b00 * w01 + b10 * w11)
                s2 = det * row(fourth, j + 3) - (b01 * w01 + b11 * w11)
                next_inv = (det * det) * pl.reciprocal(s0 * s2 - s1 * s1, approx=True)
            else:
                inv = next_inv
            top, low = row(work[at], j), row(work[at], j + 1)
            done[at] = jnp.where(first, top * lax.rsqrt(pa), done[at])
            done[at] = jnp.where(second, (pa * low - pb * top) * lax.rsqrt(pa * det), done[at])
            raw, scaled = [], []
            for g in range(groups):
                m0, m1 = cols[p][g], cols[p + 1][g]
                if g == at:
                    m0 = jnp.where(first, -1.0, jnp.where(second, 0.0, m0))
                    m1 = jnp.where(second, -1.0, jnp.where(first, 0.0, m1))
                u0, u1 = m0 * pc - m1 * pb, m1 * pa - m0 * pb
                raw.append((u0, u1))
                scaled.append((u0 * inv, u1 * inv))
            for q in range(p + 2, STEP + 1):
                kept = cols[q] if q < STEP else work
                t, l = row(kept[at], j), row(kept[at], j + 1)
                moved = []
                for g in range(groups):
                    old = jnp.where(pair, 0.0, kept[g]) if g == at else kept[g]
                    if q < p + 4:
                        moved.append(old - (raw[g][0] * t + raw[g][1] * l) * inv)
                    else:
                        moved.append(old - (scaled[g][0] * t + scaled[g][1] * l))
                if q < STEP:
                    cols[q] = moved
                else:
                    work = moved
        for g in range(groups):
            out.append(jnp.where(lane <= base + SUB * g + sub, done[g], 0.0))
        lines = [row(work[p // SUB], p % SUB) for p in range(STEP)]
        later = s + 2 * groups
        for i in range(s + groups, min(later, count)):
            change = tree([spread(rows[i], base + p) * lines[p] for p in range(STEP)])
            rows[i] = jnp.where(here, 0.0, rows[i]) - change
        if later < count:
            rest = jnp.concatenate(rows[later:], axis=0)
            inside = jnp.concatenate([here] * (count - later), axis=0)
            pieces = [jnp.zeros((base, LANES), F32)] if base else []
            pieces += work + [jnp.zeros((LANES - base - STEP, LANES), F32)]
            change = dot(jnp.where(inside, rest, 0.0), jnp.concatenate(pieces, axis=0))
            rest = jnp.where(inside, 0.0, rest) - change
            rows[later:] = [rest[SUB * i : SUB * (i + 1), :] for i in range(count - later)]
    return jnp.concatenate(out, axis=0) * SCALE**0.5


def blend(before, after):
    return 1.0 + RELAX * (jnp.sqrt(before / after) - 1.0)


def add_up(x):
    return jnp.sum(jnp.sum(x, axis=0, keepdims=True), axis=1, keepdims=True)


def dot3(a, b):
    a_high, a_low = split(a)
    b_high, b_low = split(b)
    left = jnp.concatenate([a_high, a_low, a_high], axis=1)
    return dot(left, jnp.concatenate([b_high, b_high, b_low], axis=0), precision=None)


def identity(size):
    return (
        lax.broadcasted_iota(jnp.int32, (size, size), 0) == lax.broadcasted_iota(jnp.int32, (size, size), 1)
    ).astype(F32)


def update_kernel(
    chunks, mine_v, other_v, mean_v, x_hbm, out_hbm, mean_out, full, x_buf, o_buf, in_sem, out_sem
):
    members = x_buf.shape[1]
    rows = x_buf.shape[0]
    size = rows // chunks
    pieces = [(0, size // 2)] + [(size // 2 + i * size, size) for i in range(chunks - 1)] + [(rows - size // 2, size // 2)]
    load, every_load = piece_copy(x_hbm, x_buf, in_sem, pieces)
    store, every_store = piece_copy(o_buf, out_hbm, out_sem, pieces)
    every_load(lambda copy: copy.start())

    mine = lax.axis_index(AXIS) & 1
    span = PACKED // 2
    full[pl.ds(pl.multiple_of(mine * span, SUB), span), :] = mine_v[...]
    full[pl.ds(pl.multiple_of((1 - mine) * span, SUB), span), :] = other_v[...]

    half = members // 2
    quarter = half // 2

    def block(at):
        return full[at : at + half, :]

    def innovation(k):
        count = OBS // INNOV_LANES
        at = INNOV + count * k
        return column(jnp.concatenate([full[at + j : at + j + 1, :INNOV_LANES] for j in range(count)], axis=1))

    first = jnp.concatenate([block(A0), block(A1)], axis=1)
    second = jnp.concatenate([block(B0), block(B1)], axis=1)
    g00, g01, top = block(G00), block(G01), full[G11:, :]
    line = lax.broadcasted_iota(jnp.int32, (half, half), 0)
    lane = lax.broadcasted_iota(jnp.int32, (half, half), 1)
    last = jnp.concatenate([jnp.zeros((quarter, quarter), F32), g00[quarter:, :quarter]], axis=1)
    corner = (line >= quarter) & (lane < quarter)
    g00 = jnp.where(corner, g00.T, g00)
    g11 = jnp.concatenate([top, last], axis=0)
    inner = (line >= INNOV - G00) & (lane >= quarter) & (lane < quarter + INNOV_LANES)
    g11 = jnp.where(corner | inner, g11.T, g11)
    gram = jnp.concatenate(
        [jnp.concatenate([g00, g01], axis=1), jnp.concatenate([g01.T, g11], axis=1)], axis=0
    )
    eye = identity(half)

    inv_m = factor(eye + dot(first, first, ((1,), (1,))))
    v_and_f = dot3(inv_m, jnp.concatenate([first, innovation(0)], axis=1))
    v, f = v_and_f[:, :members], v_and_f[:, members:]
    before = add_up(eye * (g00 + g11))
    after1 = before - add_up(dot3(v, gram) * v)
    factor1 = blend(before, after1)
    increment = jnp.sum(v * jnp.concatenate([f, f], axis=1), axis=0, keepdims=True)
    innov2 = innovation(1) - jnp.sum(second * increment, axis=1, keepdims=True)

    a1 = dot(first, first, ((0,), (0,)))
    a2 = dot(second, second, ((0,), (0,)))
    square = factor1 * factor1
    k00 = eye + a1[:half, :half] + a2[:half, :half] * square
    k10 = a1[half:, :half] + a2[half:, :half] * square
    k11 = eye + a1[half:, half:] + a2[half:, half:] * square
    inv00 = factor(k00)
    l10 = dot(k10, inv00, ((1,), (1,)))
    inv11 = factor(k11 - dot(l10, l10, ((1,), (1,))))
    inv10 = -dot(inv11, dot(l10, inv00))
    target = dot(second, innov2, ((0,), (0,))) * square
    y0 = dot3(inv00, target[:half, :])
    y1 = dot3(inv11, target[half:, :] - dot3(l10, y0))
    bottom = jnp.concatenate([inv10, inv11], axis=1)
    top_trace = add_up(dot3(inv00, g00) * inv00)
    after2 = top_trace + add_up(dot3(bottom, gram) * bottom)
    factor2 = factor1 * blend(after1, after2)
    increment0 = jnp.sum(y0 * inv00 + y1 * inv10, axis=0, keepdims=True)
    increment1 = jnp.sum(y1 * inv11, axis=0, keepdims=True)
    increment = increment + jnp.concatenate([increment0, increment1], axis=1)

    turned = jnp.concatenate(
        [jnp.concatenate([inv00.T, inv10.T], axis=1), jnp.concatenate([jnp.zeros_like(inv00), inv11.T], axis=1)], axis=0
    )

    def stacked(x):
        high, low = split(x)
        return jnp.concatenate([high, high, low], axis=0)

    step_line = lax.broadcasted_iota(jnp.int32, (LANES, LANES), 0)
    diagonal = step_line == lax.broadcasted_iota(jnp.int32, (LANES, LANES), 1)

    def apply(i, at, size, transform, scale):
        load(i, at, size).wait()
        x = x_buf[pl.ds(at, size), :]
        high, low = split(x)
        moved = dot(jnp.concatenate([high, low, high], axis=1), transform, precision=None)
        o_buf[pl.ds(at, size), :] = moved if scale is None else moved * scale
        store(i, at, size).start()
        steps = jnp.sum(x * increment, axis=1, keepdims=True)
        for j in range(0, size, LANES):
            step = jnp.sum(jnp.where(diagonal, steps[j : j + LANES, :], 0.0), axis=0, keepdims=True)
            part = pl.ds(at + j, LANES)
            mean_out[:, part] = mean_v[:, part] + step

    apply(0, *pieces[0], stacked(turned), factor2)
    scaled = stacked(turned * factor2)

    def body(i, _):
        apply(i, pl.multiple_of(i * size - size // 2, size // 2), size, scaled, None)
        return 0

    lax.fori_loop(1, chunks, body, 0)
    apply(chunks, *pieces[-1], scaled, None)
    every_store(lambda copy: copy.wait())


def spec(space):
    return pl.BlockSpec(memory_space=space)


def params():
    return pltpu.CompilerParams(vmem_limit_bytes=VMEM_LIMIT)


def cost(flops, bytes_accessed):
    return pl.CostEstimate(flops=flops, bytes_accessed=bytes_accessed, transcendentals=0)


def cost(flops, bytes_accessed):
    return pl.CostEstimate(flops=flops, bytes_accessed=bytes_accessed, transcendentals=0)


def gram_of(ensemble):
    rows, members = ensemble.shape
    return pl.pallas_call(
        gram_kernel,
        out_shape=jax.ShapeDtypeStruct((PACKED - G00, LANES), F32),
        in_specs=[spec(pltpu.HBM)],
        out_specs=spec(pltpu.VMEM),
        scratch_shapes=[pltpu.VMEM((rows, members), F32), pltpu.SemaphoreType.DMA((2,))],
        cost_estimate=cost(4 * rows * members * members, 4 * rows * members),
        compiler_params=params(),
    )(ensemble)


def gather(ensemble, mean_state, observed, error_var, owner, obs_rows, gram):
    members = ensemble.shape[1]
    half = jax.ShapeDtypeStruct((PACKED // 2, LANES), F32)
    return pl.pallas_call(
        gather_kernel,
        out_shape=(half, half),
        in_specs=[spec(pltpu.SMEM), spec(pltpu.SMEM)] + [spec(pltpu.VMEM)] * 5 + [spec(pltpu.HBM)],
        out_specs=[spec(pltpu.VMEM)] * 2,
        scratch_shapes=[
            pltpu.VMEM((PACKED, LANES), F32),
            pltpu.VMEM((2, OBS, members), F32),
            pltpu.SemaphoreType.DMA((2,)),
        ],
        compiler_params=params(),
    )(owner, obs_rows, obs_rows, observed, error_var, mean_state.reshape(-1, LANES), gram, ensemble)


def update(packed, ensemble, mean_state):
    rows, members = ensemble.shape
    chunks = 4
    out, mean = pl.pallas_call(
        functools.partial(update_kernel, chunks),
        out_shape=(jax.ShapeDtypeStruct((rows, members), F32), jax.ShapeDtypeStruct((1, rows), F32)),
        in_specs=[spec(pltpu.VMEM)] * 3 + [spec(pltpu.HBM)],
        out_specs=(spec(pltpu.HBM), spec(pltpu.VMEM)),
        scratch_shapes=[
            pltpu.VMEM((PACKED, LANES), F32),
            pltpu.VMEM((rows, members), F32),
            pltpu.VMEM((rows, members), F32),
            pltpu.SemaphoreType.DMA((chunks + 1,)),
            pltpu.SemaphoreType.DMA((chunks + 1,)),
        ],
        compiler_params=params(),
    )(*packed, mean_state.reshape(1, rows), ensemble)
    return out, mean.reshape(rows)


def swap(value, count, mask):
    return lax.ppermute(value, AXIS, [(i, i ^ mask) for i in range(count)])


def total(keep, send, count):
    odd = ((lax.axis_index(AXIS) >> 1) & 1) == 1
    value = keep + swap(send, count, 1)
    low, high = jnp.split(value, 2, axis=0)
    value = jnp.where(odd, high, low) + swap(jnp.where(odd, low, high), count, 2)
    mask = 4
    while mask < count:
        value = value + swap(value, count, mask)
        mask *= 2
    got = swap(value, count, 2)
    value = jnp.concatenate([jnp.where(odd, got, value), jnp.where(odd, value, got)], axis=0)
    return value, swap(value, count, 1)


def on_device(count, ensemble, mean_state, observed, error_var, owner, obs_rows):
    gram = gram_of(ensemble)
    keep, send = gather(ensemble, mean_state, observed, error_var, owner, obs_rows, gram)
    return update(total(keep, send, count), ensemble, mean_state)


def solution(mesh):
    count = mesh.shape[AXIS]
    in_specs = (
        P(("groups", "rows"), None),
        P(("groups", "rows")),
        P("groups", None),
        P("groups", None),
        P("groups"),
        P("groups", None),
    )
    out_specs = (P(("groups", "rows"), None), P(("groups", "rows")))

    def body(*args):
        return on_device(count, *args)

    return jax.shard_map(body, mesh=mesh, in_specs=in_specs, out_specs=out_specs, check_vma=False)
```

```python
import functools

import jax
import jax.numpy as jnp
from jax import lax
from jax.experimental import pallas as pl
from jax.experimental.pallas import tpu as pltpu
from jax.sharding import PartitionSpec as P

RELAX = 0.6
HI = lax.Precision.HIGHEST
AXIS = "rows"
F32 = jnp.float32
BF16 = jnp.bfloat16
LANES = 128
SUB = 8
OBS = 128
VMEM_LIMIT = 51 * 1024 * 1024
STEP = 16
SCALE = 2.0**-16

A0, A1, B0, B1, G00, G01, G11 = range(0, 7 * 128, 128)
PACKED = G11 + 64
INNOV = G00 + 96
INNOV_LANES = 32


def dot(a, b, dims=((1,), (0,)), precision=HI):
    return lax.dot_general(a, b, (dims, ((), ())), precision=precision, preferred_element_type=F32)


def column(row):
    return jnp.broadcast_to(row, (LANES, LANES)).T


def split(x):
    high = x.astype(BF16)
    return high, (x - high.astype(F32)).astype(BF16)


def piece_copy(source, target, sem, pieces):
    def copy(i, at, size):
        part = pl.ds(at, size)
        return pltpu.make_async_copy(source.at[part], target.at[part], sem.at[i])

    def every(act):
        for i, (at, size) in enumerate(pieces):
            act(copy(i, at, size))

    return copy, every


def gram_kernel(x_hbm, out, x_buf, sem):
    rows, members = x_buf.shape
    half = members // 2
    quarter = rows // 4
    pieces = [(0, quarter), (quarter, quarter), (2 * quarter, rows - 2 * quarter)]
    load, every_load = piece_copy(x_hbm, x_buf, sem, pieces)
    every_load(lambda copy: copy.start())
    total = None
    for i, (at, size) in enumerate(pieces):
        load(i, at, size).wait()
        high, low = split(x_buf[at : at + size, :])
        part = dot(high, jnp.concatenate([high, low], axis=1), ((0,), (0,)), None)
        total = part if total is None else total + part
    cross = total[:, members:]
    total = total[:, :members] + cross + cross.T
    quarter = half // 2
    out[:quarter, :] = total[:quarter, :half]
    out[quarter:half, :] = jnp.concatenate(
        [total[half + quarter :, half + quarter :], total[quarter:half, quarter:half]], axis=1
    )
    out[half : 2 * half, :] = total[:half, half:]
    out[2 * half :, :] = total[half : half + quarter, half:]


def gather_kernel(
    owner_s, rows_s, rows_v, observed, error_var, mean_v, gram, x_hbm, keep, send, full, picked, sem
):
    me = lax.axis_index(AXIS)
    members = picked.shape[2]
    half = members // 2

    full[:G00, :] = jnp.zeros((G00, LANES), F32)
    full[G00:, :] = gram[...]
    full[INNOV : INNOV + 2 * OBS // INNOV_LANES, :INNOV_LANES] = jnp.zeros((2 * OBS // INNOV_LANES, INNOV_LANES), F32)
    lane = lax.broadcasted_iota(jnp.int32, (OBS, LANES), 1)

    for k, left, right in ((0, A0, A1), (1, B0, B1)):

        @pl.when(owner_s[k] == me)
        def _(k=k, left=left, right=right):
            for o in range(OBS):
                pltpu.make_async_copy(
                    x_hbm.at[pl.ds(rows_s[k, o], 1)], picked.at[k, pl.ds(o, 1)], sem.at[k]
                ).start(priority=o % 2)
            index = column(rows_v[k : k + 1, :].astype(F32)).astype(jnp.int32) - lane
            prior = jnp.zeros((OBS, LANES), F32)
            for r in range(mean_v.shape[0]):
                prior = prior + jnp.where(index == r * LANES, mean_v[r : r + 1, :], 0.0)
            prior = jnp.sum(prior.T, axis=0, keepdims=True)
            scale = lax.rsqrt(error_var[k : k + 1, :] * (members - 1.0))
            innov = scale * (observed[k : k + 1, :] - prior)
            count = OBS // INNOV_LANES
            for j in range(count):
                at = INNOV + count * k + j
                full[at : at + 1, :INNOV_LANES] = innov[:, j * INNOV_LANES : (j + 1) * INNOV_LANES]
            scales = column(scale)
            pltpu.make_async_copy(x_hbm.at[pl.ds(0, OBS)], picked.at[k], sem.at[k]).wait()
            full[left : left + OBS, :] = picked[k, :, :half] * scales
            full[right : right + OBS, :] = picked[k, :, half:] * scales

    mine = me & 1
    span = PACKED // 2
    keep[...] = full[pl.ds(pl.multiple_of(mine * span, SUB), span), :]
    send[...] = full[pl.ds(pl.multiple_of((1 - mine) * span, SUB), span), :]


def tree(terms):
    while len(terms) > 1:
        terms = [terms[i] + terms[i + 1] if i + 1 < len(terms) else terms[i] for i in range(0, len(terms), 2)]
    return terms[0]


def factor(a):
    a = a * SCALE
    count = LANES // SUB
    lane = lax.broadcasted_iota(jnp.int32, (SUB, LANES), 1)
    sub = lax.broadcasted_iota(jnp.int32, (SUB, LANES), 0)
    rows = [a[SUB * i : SUB * (i + 1), :] for i in range(count)]
    out = []

    def spread(x, c):
        return jnp.broadcast_to(x[:, c : c + 1], (SUB, LANES))

    def row(x, j):
        return jnp.broadcast_to(x[j : j + 1, :], (SUB, LANES))

    groups = STEP // SUB
    for s in range(0, count, groups):
        base = SUB * s
        here = (lane >= base) & (lane < base + STEP)
        cols = [[spread(rows[s + g], base + q) for g in range(groups)] for q in range(STEP)]
        work = [
            jnp.where(here, (lane - base == sub + SUB * g).astype(F32), rows[s + g]) for g in range(groups)
        ]
        done = [jnp.zeros((SUB, LANES), F32) for _ in range(groups)]
        for p in range(0, STEP, 2):
            at, j = divmod(p, SUB)
            first, second = sub == j, sub == j + 1
            pair = first | second
            pa, pb, pc = row(cols[p][at], j), row(cols[p][at], j + 1), row(cols[p + 1][at], j + 1)
            det = pa * pc - pb * pb
            if p % 4 == 0:
                inv = pl.reciprocal(det, approx=True)
                third, fourth = cols[p + 2][at], cols[p + 3][at]
                b00, b10, b01, b11 = row(third, j), row(third, j + 1), row(fourth, j), row(fourth, j + 1)
                w00, w10 = pc * b00 - pb * b10, pa * b10 - pb * b00
                w01, w11 = pc * b01 - pb * b11, pa * b11 - pb * b01
                s0 = det * row(third, j + 2) - (b00 * w00 + b10 * w10)
                s1 = det * row(third, j + 3) - (b00 * w01 + b10 * w11)
                s2 = det * row(fourth, j + 3) - (b01 * w01 + b11 * w11)
                next_inv = (det * det) * pl.reciprocal(s0 * s2 - s1 * s1, approx=True)
            else:
                inv = next_inv
            top, low = row(work[at], j), row(work[at], j + 1)
            done[at] = jnp.where(first, top * lax.rsqrt(pa), done[at])
            done[at] = jnp.where(second, (pa * low - pb * top) * lax.rsqrt(pa * det), done[at])
            raw, scaled = [], []
            for g in range(groups):
                m0, m1 = cols[p][g], cols[p + 1][g]
                if g == at:
                    m0 = jnp.where(first, -1.0, jnp.where(second, 0.0, m0))
                    m1 = jnp.where(second, -1.0, jnp.where(first, 0.0, m1))
                u0, u1 = m0 * pc - m1 * pb, m1 * pa - m0 * pb
                raw.append((u0, u1))
                scaled.append((u0 * inv, u1 * inv))
            for q in range(p + 2, STEP + 1):
                kept = cols[q] if q < STEP else work
                t, l = row(kept[at], j), row(kept[at], j + 1)
                moved = []
                for g in range(groups):
                    old = jnp.where(pair, 0.0, kept[g]) if g == at else kept[g]
                    if q < p + 4:
                        moved.append(old - (raw[g][0] * t + raw[g][1] * l) * inv)
                    else:
                        moved.append(old - (scaled[g][0] * t + scaled[g][1] * l))
                if q < STEP:
                    cols[q] = moved
                else:
                    work = moved
        for g in range(groups):
            out.append(jnp.where(lane <= base + SUB * g + sub, done[g], 0.0))
        lines = [row(work[p // SUB], p % SUB) for p in range(STEP)]
        later = s + 2 * groups
        for i in range(s + groups, min(later, count)):
            change = tree([spread(rows[i], base + p) * lines[p] for p in range(STEP)])
            rows[i] = jnp.where(here, 0.0, rows[i]) - change
        if later < count:
            rest = jnp.concatenate(rows[later:], axis=0)
            inside = jnp.concatenate([here] * (count - later), axis=0)
            pieces = [jnp.zeros((base, LANES), F32)] if base else []
            pieces += work + [jnp.zeros((LANES - base - STEP, LANES), F32)]
            change = dot(jnp.where(inside, rest, 0.0), jnp.concatenate(pieces, axis=0))
            rest = jnp.where(inside, 0.0, rest) - change
            rows[later:] = [rest[SUB * i : SUB * (i + 1), :] for i in range(count - later)]
    return jnp.concatenate(out, axis=0) * SCALE**0.5


def blend(before, after):
    return 1.0 + RELAX * (jnp.sqrt(before / after) - 1.0)


def add_up(x):
    return jnp.sum(jnp.sum(x, axis=0, keepdims=True), axis=1, keepdims=True)


def dot3(a, b):
    a_high, a_low = split(a)
    b_high, b_low = split(b)
    left = jnp.concatenate([a_high, a_low, a_high], axis=1)
    return dot(left, jnp.concatenate([b_high, b_high, b_low], axis=0), precision=None)


def identity(size):
    return (
        lax.broadcasted_iota(jnp.int32, (size, size), 0) == lax.broadcasted_iota(jnp.int32, (size, size), 1)
    ).astype(F32)


def update_kernel(
    chunks, mine_v, other_v, mean_v, x_hbm, out_hbm, mean_out, full, x_buf, o_buf, in_sem, out_sem
):
    members = x_buf.shape[1]
    rows = x_buf.shape[0]
    size = rows // chunks
    pieces = [(0, size // 2)] + [(size // 2 + i * size, size) for i in range(chunks - 1)] + [(rows - size // 2, size // 2)]
    load, every_load = piece_copy(x_hbm, x_buf, in_sem, pieces)
    store, every_store = piece_copy(o_buf, out_hbm, out_sem, pieces)
    every_load(lambda copy: copy.start())

    mine = lax.axis_index(AXIS) & 1
    span = PACKED // 2
    full[pl.ds(pl.multiple_of(mine * span, SUB), span), :] = mine_v[...]
    full[pl.ds(pl.multiple_of((1 - mine) * span, SUB), span), :] = other_v[...]

    half = members // 2
    quarter = half // 2

    def block(at):
        return full[at : at + half, :]

    def innovation(k):
        count = OBS // INNOV_LANES
        at = INNOV + count * k
        return column(jnp.concatenate([full[at + j : at + j + 1, :INNOV_LANES] for j in range(count)], axis=1))

    first = jnp.concatenate([block(A0), block(A1)], axis=1)
    second = jnp.concatenate([block(B0), block(B1)], axis=1)
    g00, g01, top = block(G00), block(G01), full[G11:, :]
    line = lax.broadcasted_iota(jnp.int32, (half, half), 0)
    lane = lax.broadcasted_iota(jnp.int32, (half, half), 1)
    last = jnp.concatenate([jnp.zeros((quarter, quarter), F32), g00[quarter:, :quarter]], axis=1)
    corner = (line >= quarter) & (lane < quarter)
    g00 = jnp.where(corner, g00.T, g00)
    g11 = jnp.concatenate([top, last], axis=0)
    inner = (line >= INNOV - G00) & (lane >= quarter) & (lane < quarter + INNOV_LANES)
    g11 = jnp.where(corner | inner, g11.T, g11)
    gram = jnp.concatenate(
        [jnp.concatenate([g00, g01], axis=1), jnp.concatenate([g01.T, g11], axis=1)], axis=0
    )
    eye = identity(half)

    inv_m = factor(eye + dot(first, first, ((1,), (1,))))
    v_and_f = dot3(inv_m, jnp.concatenate([first, innovation(0)], axis=1))
    v, f = v_and_f[:, :members], v_and_f[:, members:]
    before = add_up(eye * (g00 + g11))
    after1 = before - add_up(dot3(v, gram) * v)
    factor1 = blend(before, after1)
    increment = jnp.sum(v * jnp.concatenate([f, f], axis=1), axis=0, keepdims=True)
    innov2 = innovation(1) - jnp.sum(second * increment, axis=1, keepdims=True)

    a1 = dot(first, first, ((0,), (0,)))
    a2 = dot(second, second, ((0,), (0,)))
    square = factor1 * factor1
    k00 = eye + a1[:half, :half] + a2[:half, :half] * square
    k10 = a1[half:, :half] + a2[half:, :half] * square
    k11 = eye + a1[half:, half:] + a2[half:, half:] * square
    inv00 = factor(k00)
    l10 = dot(k10, inv00, ((1,), (1,)))
    inv11 = factor(k11 - dot(l10, l10, ((1,), (1,))))
    inv10 = -dot(inv11, dot(l10, inv00))
    target = dot(second, innov2, ((0,), (0,))) * square
    y0 = dot3(inv00, target[:half, :])
    y1 = dot3(inv11, target[half:, :] - dot3(l10, y0))
    bottom = jnp.concatenate([inv10, inv11], axis=1)
    top_trace = add_up(dot3(inv00, g00) * inv00)
    after2 = top_trace + add_up(dot3(bottom, gram) * bottom)
    factor2 = factor1 * blend(after1, after2)
    increment0 = jnp.sum(y0 * inv00 + y1 * inv10, axis=0, keepdims=True)
    increment1 = jnp.sum(y1 * inv11, axis=0, keepdims=True)
    increment = increment + jnp.concatenate([increment0, increment1], axis=1)

    turned = jnp.concatenate(
        [jnp.concatenate([inv00.T, inv10.T], axis=1), jnp.concatenate([jnp.zeros_like(inv00), inv11.T], axis=1)], axis=0
    )

    def stacked(x):
        high, low = split(x)
        return jnp.concatenate([high, high, low], axis=0)

    step_line = lax.broadcasted_iota(jnp.int32, (LANES, LANES), 0)
    diagonal = step_line == lax.broadcasted_iota(jnp.int32, (LANES, LANES), 1)

    def apply(i, at, size, transform, scale):
        load(i, at, size).wait()
        x = x_buf[pl.ds(at, size), :]
        high, low = split(x)
        moved = dot(jnp.concatenate([high, low, high], axis=1), transform, precision=None)
        o_buf[pl.ds(at, size), :] = moved if scale is None else moved * scale
        store(i, at, size).start()
        steps = jnp.sum(x * increment, axis=1, keepdims=True)
        for j in range(0, size, LANES):
            step = jnp.sum(jnp.where(diagonal, steps[j : j + LANES, :], 0.0), axis=0, keepdims=True)
            part = pl.ds(at + j, LANES)
            mean_out[:, part] = mean_v[:, part] + step

    apply(0, *pieces[0], stacked(turned), factor2)
    scaled = stacked(turned * factor2)

    def body(i, _):
        apply(i, pl.multiple_of(i * size - size // 2, size // 2), size, scaled, None)
        return 0

    lax.fori_loop(1, chunks, body, 0)
    apply(chunks, *pieces[-1], scaled, None)
    every_store(lambda copy: copy.wait())


def spec(space):
    return pl.BlockSpec(memory_space=space)


def params():
    return pltpu.CompilerParams(vmem_limit_bytes=VMEM_LIMIT)


def cost(flops, bytes_accessed):
    return pl.CostEstimate(flops=flops, bytes_accessed=bytes_accessed, transcendentals=0)


def cost(flops, bytes_accessed):
    return pl.CostEstimate(flops=flops, bytes_accessed=bytes_accessed, transcendentals=0)


def gram_of(ensemble):
    rows, members = ensemble.shape
    return pl.pallas_call(
        gram_kernel,
        out_shape=jax.ShapeDtypeStruct((PACKED - G00, LANES), F32),
        in_specs=[spec(pltpu.HBM)],
        out_specs=spec(pltpu.VMEM),
        scratch_shapes=[pltpu.VMEM((rows, members), F32), pltpu.SemaphoreType.DMA((3,))],
        cost_estimate=cost(4 * rows * members * members, 4 * rows * members),
        compiler_params=params(),
    )(ensemble)


def gather(ensemble, mean_state, observed, error_var, owner, obs_rows, gram):
    members = ensemble.shape[1]
    half = jax.ShapeDtypeStruct((PACKED // 2, LANES), F32)
    return pl.pallas_call(
        gather_kernel,
        out_shape=(half, half),
        in_specs=[spec(pltpu.SMEM), spec(pltpu.SMEM)] + [spec(pltpu.VMEM)] * 5 + [spec(pltpu.HBM)],
        out_specs=[spec(pltpu.VMEM)] * 2,
        scratch_shapes=[
            pltpu.VMEM((PACKED, LANES), F32),
            pltpu.VMEM((2, OBS, members), F32),
            pltpu.SemaphoreType.DMA((2,)),
        ],
        compiler_params=params(),
    )(owner, obs_rows, obs_rows, observed, error_var, mean_state.reshape(-1, LANES), gram, ensemble)


def update(packed, ensemble, mean_state):
    rows, members = ensemble.shape
    chunks = 2
    out, mean = pl.pallas_call(
        functools.partial(update_kernel, chunks),
        out_shape=(jax.ShapeDtypeStruct((rows, members), F32), jax.ShapeDtypeStruct((1, rows), F32)),
        in_specs=[spec(pltpu.VMEM)] * 3 + [spec(pltpu.HBM)],
        out_specs=(spec(pltpu.HBM), spec(pltpu.VMEM)),
        scratch_shapes=[
            pltpu.VMEM((PACKED, LANES), F32),
            pltpu.VMEM((rows, members), F32),
            pltpu.VMEM((rows, members), F32),
            pltpu.SemaphoreType.DMA((chunks + 1,)),
            pltpu.SemaphoreType.DMA((chunks + 1,)),
        ],
        compiler_params=params(),
    )(*packed, mean_state.reshape(1, rows), ensemble)
    return out, mean.reshape(rows)


def swap(value, count, mask):
    return lax.ppermute(value, AXIS, [(i, i ^ mask) for i in range(count)])


def total(keep, send, count):
    odd = ((lax.axis_index(AXIS) >> 1) & 1) == 1
    value = keep + swap(send, count, 1)
    low, high = jnp.split(value, 2, axis=0)
    value = jnp.where(odd, high, low) + swap(jnp.where(odd, low, high), count, 2)
    mask = 4
    while mask < count:
        value = value + swap(value, count, mask)
        mask *= 2
    got = swap(value, count, 2)
    value = jnp.concatenate([jnp.where(odd, got, value), jnp.where(odd, value, got)], axis=0)
    return value, swap(value, count, 1)


def on_device(count, ensemble, mean_state, observed, error_var, owner, obs_rows):
    gram = gram_of(ensemble)
    keep, send = gather(ensemble, mean_state, observed, error_var, owner, obs_rows, gram)
    return update(total(keep, send, count), ensemble, mean_state)


def solution(mesh):
    count = mesh.shape[AXIS]
    in_specs = (
        P(("groups", "rows"), None),
        P(("groups", "rows")),
        P("groups", None),
        P("groups", None),
        P("groups"),
        P("groups", None),
    )
    out_specs = (P(("groups", "rows"), None), P(("groups", "rows")))

    def body(*args):
        return on_device(count, *args)

    return jax.shard_map(body, mesh=mesh, in_specs=in_specs, out_specs=out_specs, check_vma=False)
```
